32 devices in a mesh: batch: 8 (over z, x), head: 4 (over y, core).
Axes of the slice: x: 2, y: 2, z: 4, core: 2. Of those that a mesh axis runs over, the one named last changes fastest.
Arguments:
- block_input: bfloat16 [64, 1024, 768], P(('batch', 'head')), may hold values from -6 to 6
- cotangent: bfloat16 [64, 1024, 768], P(('batch', 'head')), may hold values from -6 to 6
- segment_lengths: int32 [64, 8], P('batch'), may hold values from 1 to 256, 1024 in all within a row
- thought_counts: int32 [64, 8], P('batch'), may hold values from 0 to 3
- packing_mask: int32 [64, 1024], P(('batch', 'head')), may hold values 0 or 1
- attend_weight: float32 [768, 3, 768], P('batch', None, 'head')
- output_weight: float32 [768, 768], P(('batch', 'head'))
- expand_weight: float32 [768, 3072], P(('batch', 'head'))
- reduce_weight: float32 [3072, 768], P(('batch', 'head'))
- vectors: float32 [768, 12], P(('batch', 'head'))
- first_attend: float32 [768, 3, 768], P('batch', None, 'head')
- first_output: float32 [768, 768], P(('batch', 'head'))
- first_expand: float32 [768, 3072], P(('batch', 'head'))
- first_reduce: float32 [3072, 768], P(('batch', 'head'))
- first_vectors: float32 [768, 12], P(('batch', 'head'))
- second_attend: float32 [768, 3, 768], P('batch', None, 'head'), as said below
- second_output: float32 [768, 768], P(('batch', 'head')), as said below
- second_expand: float32 [768, 3072], P(('batch', 'head')), as said below
- second_reduce: float32 [3072, 768], P(('batch', 'head')), as said below
- second_vectors: float32 [768, 12], P(('batch', 'head')), as said below
Outputs:
- hidden_states: bfloat16 [64, 1024, 768], P(('batch', 'head'))
- input_gradient: bfloat16 [64, 1024, 768], P(('batch', 'head'))
- moment_attend: float32 [768, 3, 768], P('batch', None, 'head')
- moment_output: float32 [768, 768], P(('batch', 'head'))
- moment_expand: float32 [768, 3072], P(('batch', 'head'))
- moment_reduce: float32 [3072, 768], P(('batch', 'head'))
- moment_vectors: float32 [768, 12], P(('batch', 'head'))
- square_attend: float32 [768, 3, 768], P('batch', None, 'head')
- square_output: float32 [768, 768], P(('batch', 'head'))
- square_expand: float32 [768, 3072], P(('batch', 'head'))
- square_reduce: float32 [3072, 768], P(('batch', 'head'))
- square_vectors: float32 [768, 12], P(('batch', 'head'))
- master_attend: float32 [768, 3, 768], P('batch', None, 'head')
- master_output: float32 [768, 768], P(('batch', 'head'))
- master_expand: float32 [768, 3072], P(('batch', 'head'))
- master_reduce: float32 [3072, 768], P(('batch', 'head'))
- master_vectors: float32 [768, 12], P(('batch', 'head'))
- trust_norms: float32 [3, 16], replicated
The draws below stay inside these ranges and needn't reach their ends.
Inputs may be any that keep to these rules, and one draw needn't show every extreme that they name: `segment_lengths`: each row's lengths sum to 1024. `second_attend`: positive. `second_output`: positive. `second_expand`: positive. `second_reduce`: positive. `second_vectors`: positive.
All inputs are finite; a program needn't handle non-finite values. No bound on the sum of `packing_mask` on one device may be relied on, other than what follows from the above.
Results may differ from the reference program's by a relative error of at most 0.013.
The reference program's roundings to bfloat16 on the way count: a program that leaves them out, or rounds other values in their place, can miss the bound.
Values may be sent and summed in bfloat16 or wider, within the bound.
No kernel may reach another device: no remote copies, remote signals or barrier semaphores. Data moves between devices by JAX's collectives and lax.ppermute only.
A program may use at most 256 MiB of HBM per device.

```python
import math
import jax
import jax.numpy as jnp
import numpy as np
from jax import lax

D = 768
FEEDFORWARD_UNITS = 3072
HEADS = 12
HEAD_DIM = 64
LEN = 1024
SEQ_DEV = 1
MICRO = 2
SEGS = 8
THOUGHT_TOKENS = 8
STEP = 6
VCOLS = 12
SEQS = 64
TOKENS = 65536


def rough(key, shape):
    first = jax.random.fold_in(key, 0)
    normal = jnp.clip(jax.random.normal(first, shape, jnp.float32), -4.0, 4.0)
    return normal


def ramp(count, top):
    return top ** (jnp.arange(count, dtype=jnp.float32) / max(count - 1, 1) - 0.5)


def rising(count):
    return 1.0 + 3.0 * jnp.arange(count, dtype=jnp.float32) / max(count - 1, 1)


def shaped_weight(key, shape, fan, boost, top):
    base = rough(key, shape) * (boost / math.sqrt(fan))
    return base * ramp(shape[0], top).reshape((shape[0],) + (1,) * (len(shape) - 1))


def first_state(key, shape, size):
    return size * rough(key, shape)


def second_state(key, shape, size, spread_dims):
    factor = jnp.exp(jax.random.uniform(key, shape, jnp.float32, math.log(0.5), math.log(2.0)))
    result = size * size * factor
    power = 1.0 / len(spread_dims)
    for dim in spread_dims:
        extent = [1] * len(shape)
        extent[dim] = shape[dim]
        result = result * (rising(shape[dim]) ** power).reshape(extent)
    return result


def draw_attend_weight(key, part):
    key = jax.random.fold_in(key, 1)
    top = math.sqrt(3.0)
    base = shaped_weight(key, (D, 3, D), D, 1.0, top)
    return base * ramp(D, top)[None, None, :]


def draw_output_weight(key, part):
    key = jax.random.fold_in(key, 2)
    top = math.sqrt(3.0)
    return shaped_weight(key, (D, D), D, 4.0, top)


def draw_expand_weight(key, part):
    key = jax.random.fold_in(key, 3)
    top = math.sqrt(3.0)
    return shaped_weight(key, (D, FEEDFORWARD_UNITS), D, 1.0, top)


def draw_reduce_weight(key, part):
    key = jax.random.fold_in(key, 4)
    top = math.sqrt(3.0)
    return shaped_weight(key, (FEEDFORWARD_UNITS, D), FEEDFORWARD_UNITS, 1.0, top)


def draw_vectors(key, part):
    key = jax.random.fold_in(key, 5)
    top = math.sqrt(3.0)
    first, second = jax.random.split(key)
    rows = ramp(D, top)[:, None]
    gains = rows * jnp.exp(jax.random.uniform(first, (D, VCOLS), jnp.float32, -0.35, 0.35))
    biases = 0.5 * rows * rough(second, (D, VCOLS))
    columns = jnp.arange(VCOLS)
    is_gain = (columns == 0) | (columns == 5)
    return jnp.where(is_gain[None, :], gains, biases)


def draw_first_attend(key, part):
    key = jax.random.fold_in(key, 11)
    return first_state(key, (D, 3, D), 0.1 * math.sqrt(TOKENS))


def draw_first_output(key, part):
    key = jax.random.fold_in(key, 12)
    return first_state(key, (D, D), 0.2 * math.sqrt(TOKENS))


def draw_first_expand(key, part):
    key = jax.random.fold_in(key, 13)
    return first_state(key, (D, FEEDFORWARD_UNITS), 0.25 * math.sqrt(TOKENS))


def draw_first_reduce(key, part):
    key = jax.random.fold_in(key, 14)
    return first_state(key, (FEEDFORWARD_UNITS, D), 0.5 * math.sqrt(TOKENS))


def draw_first_vectors(key, part):
    key = jax.random.fold_in(key, 15)
    return first_state(key, (D, VCOLS), math.sqrt(TOKENS))


def draw_second_attend(key, part):
    key = jax.random.fold_in(key, 21)
    return second_state(key, (D, 3, D), 0.1 * math.sqrt(TOKENS), (0, 2))


def draw_second_output(key, part):
    key = jax.random.fold_in(key, 22)
    return second_state(key, (D, D), 0.2 * math.sqrt(TOKENS), (0,))


def draw_second_expand(key, part):
    key = jax.random.fold_in(key, 23)
    return second_state(key, (D, FEEDFORWARD_UNITS), 0.25 * math.sqrt(TOKENS), (0,))


def draw_second_reduce(key, part):
    key = jax.random.fold_in(key, 24)
    return second_state(key, (FEEDFORWARD_UNITS, D), 0.5 * math.sqrt(TOKENS), (0,))


def draw_second_vectors(key, part):
    key = jax.random.fold_in(key, 25)
    return second_state(key, (D, VCOLS), math.sqrt(TOKENS), (0,))


def with_ends(drawn, key, least, top_value):
    spot = [jax.random.randint(jax.random.fold_in(key, axis), (), 0, length) for axis, length in enumerate(drawn.shape)]
    main_axis = drawn.shape.index(max(drawn.shape))
    neighbour = spot[:main_axis] + [(spot[main_axis] + 1) % drawn.shape[main_axis]] + spot[main_axis + 1:]
    return drawn.at[tuple(spot)].set(least).at[tuple(neighbour)].set(top_value)


def steps_of(rng, dims, cuts, low, top_value):
    def one(axis_at, blocks):
        steps = jax.random.uniform(jax.random.fold_in(jax.random.fold_in(rng, 6), axis_at), (blocks,), jnp.float32, low / len(cuts), top_value / len(cuts))
        return jnp.repeat(jnp.exp(steps), dims[axis_at] // blocks).reshape((-1,) + (1,) * (len(dims) - axis_at - 1))

    factor_of = one(*cuts[0])
    for cut in cuts[1:]:
        factor_of = factor_of * one(*cut)
    return factor_of


def split_up(number_of, total, reach, slope):
    loads = [(1 << 20) // math.isqrt(grade ** slope) + 1 for grade in range(2, number_of + 1)]
    spare, given = total - reach - (number_of - 1), [1] * (number_of - 1)
    while spare > 0:
        movable = [i for i in range(number_of - 1) if given[i] < reach]
        whole, remaining = sum([loads[i] for i in movable]), spare
        for i in movable:
            more = min(reach - given[i], max(1, remaining * loads[i] // whole), spare)
            given[i] = given[i] + more
            spare = spare - more
    return np.array([reach] + given)


def uneven(stream_key, amount, total, bound, skew):
    if amount == 2:
        one = jax.random.randint(stream_key, (), max(1, total - bound), min(bound, total - 1) + 1)
        return jnp.stack([one, total - one])
    sizes = jnp.asarray(split_up(amount, total, bound, skew), jnp.int32)
    couples = (amount - 1) // 2
    source_of, receiver = sizes[1:1 + 2 * couples:2], sizes[2:2 + 2 * couples:2]
    slack = jnp.minimum(source_of - 1, bound - receiver)
    passed = jax.random.randint(jax.random.fold_in(stream_key, 1), (couples,), 0, 1 << 20) % (slack + 1)
    sizes = sizes.at[1:1 + 2 * couples:2].set(source_of - passed).at[2:2 + 2 * couples:2].set(receiver + passed)
    return sizes[jax.random.permutation(jax.random.fold_in(stream_key, 2), amount)]


def scatter_about(stream_key, dims, width, bound, shards=(), kind=jnp.bfloat16):
    factor_of = steps_of(stream_key, dims, shards, -0.22, 0.18) if shards else 1.0
    entries = jax.random.normal(stream_key, dims, jnp.float32) * width * factor_of
    return jnp.minimum(jnp.maximum(entries, -bound), bound).astype(kind)


def setup_inputs(seed: int = 0) -> dict:
    streams_of = jax.random.split(jax.random.key(seed), 21)
    return {
        "block_input": scatter_about(streams_of[0], (SEQS, LEN, D), 1.0, 6.0, ((0, 32),)),
        "cotangent": scatter_about(streams_of[1], (SEQS, LEN, D), 1.0, 6.0, ((0, 32),)),
        "segment_lengths": jax.vmap(lambda own: uneven(own, SEGS, LEN, LEN // 4, 2))(jax.random.split(streams_of[2], SEQS)).reshape((SEQS, SEGS)).astype(jnp.int32),
        "thought_counts": with_ends(jax.random.randint(streams_of[3], (SEQS, SEGS), 0, 4), jax.random.fold_in(streams_of[3], 1), 0, 3).astype(jnp.int32),
        "packing_mask": with_ends((jax.random.randint(streams_of[4], (SEQS, LEN), 0, 8) < 7).astype(jnp.int32), jax.random.fold_in(streams_of[4], 1), 0, 1),
        "attend_weight": draw_attend_weight(jax.random.fold_in(streams_of[20], 71), 0),
        "output_weight": draw_output_weight(jax.random.fold_in(streams_of[20], 71), 0),
        "expand_weight": draw_expand_weight(jax.random.fold_in(streams_of[20], 71), 0),
        "reduce_weight": draw_reduce_weight(jax.random.fold_in(streams_of[20], 71), 0),
        "vectors": draw_vectors(jax.random.fold_in(streams_of[20], 71), 0),
        "first_attend": draw_first_attend(jax.random.fold_in(streams_of[20], 71), 0),
        "first_output": draw_first_output(jax.random.fold_in(streams_of[20], 71), 0),
        "first_expand": draw_first_expand(jax.random.fold_in(streams_of[20], 71), 0),
        "first_reduce": draw_first_reduce(jax.random.fold_in(streams_of[20], 71), 0),
        "first_vectors": draw_first_vectors(jax.random.fold_in(streams_of[20], 71), 0),
        "second_attend": draw_second_attend(jax.random.fold_in(streams_of[20], 71), 0),
        "second_output": draw_second_output(jax.random.fold_in(streams_of[20], 71), 0),
        "second_expand": draw_second_expand(jax.random.fold_in(streams_of[20], 71), 0),
        "second_reduce": draw_second_reduce(jax.random.fold_in(streams_of[20], 71), 0),
        "second_vectors": draw_second_vectors(jax.random.fold_in(streams_of[20], 71), 0),
    }


@jax.custom_vjp
def low(v):
    return lax.optimization_barrier(v.astype(jnp.bfloat16)).astype(jnp.float32)

@jax.custom_vjp
def low_back(v):
    return v

def low_keep(v):
    return (low(v), None)

def low_pass(kept, grad):
    return (grad,)

def back_keep(v):
    return (v, None)

def back_low(kept, grad):
    return (low(grad),)
low.defvjp(low_keep, low_pass)
low_back.defvjp(back_keep, back_low)
NORM_EPS = 1e-05
NEGATIVE = -1e+30
BETA = 0.5
RATE = 0.5
DECAY = 0.01
ADAM_EPS = 1e-06
PRECISION_HIGH = lax.Precision.HIGHEST

def layer_norm(values, gain, shift):
    centre = values - lax.optimization_barrier(jnp.mean(values, axis=-1, keepdims=True))
    factor = lax.rsqrt(lax.optimization_barrier(jnp.mean(centre * centre, axis=-1, keepdims=True)) + NORM_EPS)
    return centre * factor * gain + shift

def segment_ids(lengths, positions):
    ends = jnp.cumsum(lengths, axis=-1)
    return lax.optimization_barrier(jnp.sum((positions[None, :, None] >= ends[:, None, :]).astype(jnp.int32), axis=-1))

def loss_weight(lengths, counts, mask, first, span):
    positions = first + jnp.arange(span, dtype=jnp.int32)
    ends = jnp.cumsum(lengths, axis=-1)
    starts = ends - lengths
    segment = segment_ids(lengths, positions)
    onehot = segment[:, :, None] == jnp.arange(lengths.shape[-1], dtype=jnp.int32)[None, None, :]
    start_of = lax.optimization_barrier(jnp.sum(jnp.where(onehot, starts[:, None, :], 0), axis=-1))
    passes = lax.optimization_barrier(jnp.sum(jnp.where(onehot, counts[:, None, :], 0), axis=-1))
    keep = (positions[None, :] - start_of >= THOUGHT_TOKENS * passes) & (mask > 0)
    return keep.astype(jnp.float32)

def attend_sequence(parts):
    query, keys, values, segment = parts
    length = query.shape[0]
    scores = jnp.einsum('qhd,khd->hqk', query, keys, precision=PRECISION_HIGH) * HEAD_DIM ** (-0.5)
    scores = low_back(scores)
    positions = jnp.arange(length, dtype=jnp.int32)
    allowed = (positions[None, :] <= positions[:, None]) & (segment[None, :] == segment[:, None])
    scores = jnp.where(allowed[None], scores, NEGATIVE)
    probs = low(jax.nn.softmax(scores, axis=-1))
    return jnp.einsum('hqk,khd->qhd', probs, values, precision=PRECISION_HIGH)

def forward(block, attend_w, output_w, expand_w, reduce_w, vector_w, segment):
    model_parameters = low(vector_w)
    attend_layer = low(attend_w)
    block_result = low(output_w)
    expand_layer = low(expand_w)
    reduce_lowered = low(reduce_w)
    seqs, length = (block.shape[0], block.shape[1])
    input_normed = low(layer_norm(block, model_parameters[:, 0], model_parameters[:, 1]))
    project_layer = jnp.einsum('jie,eym->jiym', input_normed, attend_layer, precision=PRECISION_HIGH)
    query = low_back(low(project_layer[:, :, 0] + model_parameters[:, 2]))
    keys = low_back(low(project_layer[:, :, 1]))
    values = low_back(low(project_layer[:, :, 2] + model_parameters[:, 3]))
    shaped = (seqs, length, HEADS, HEAD_DIM)
    outs = lax.map(jax.checkpoint(attend_sequence), (query.reshape(shaped), keys.reshape(shaped), values.reshape(shaped), segment))
    context_rows = low_back(low(outs.reshape(seqs, length, D)))
    attention_branch = low_back(jnp.einsum('gxp,ph->gxh', context_rows, block_result, precision=PRECISION_HIGH) + model_parameters[:, 4])
    middle = block + attention_branch
    middle_normed = low(layer_norm(middle, model_parameters[:, 5], model_parameters[:, 6]))
    preactivation = low_back(jnp.einsum('nwj,jp->nwp', middle_normed, expand_layer, precision=PRECISION_HIGH) + model_parameters[:, 8:].T.reshape(FEEDFORWARD_UNITS))
    hidden_activated = low(jax.nn.gelu(preactivation, approximate=True))
    residual_branch = low_back(jnp.einsum('tkx,xw->tkw', hidden_activated, reduce_lowered, precision=PRECISION_HIGH) + model_parameters[:, 7])
    return middle + residual_branch

def adapt(grad, first, second, weight):
    moment = BETA * first + (1.0 - BETA) * grad
    square = BETA * second + (1.0 - BETA) * grad * grad
    correct = 1.0 - BETA ** STEP
    update = moment / correct / (jnp.sqrt(square / correct) + ADAM_EPS) + DECAY * weight
    return (moment, square, update)

def reference(block_input, cotangent, segment_lengths, thought_counts, packing_mask, attend_weight, output_weight, expand_weight, reduce_weight, vectors, first_attend, first_output, first_expand, first_reduce, first_vectors, second_attend, second_output, second_expand, second_reduce, second_vectors):
    group = SEQ_DEV * MICRO
    groups = SEQS // group
    weights = (attend_weight, output_weight, expand_weight, reduce_weight, vectors)

    def one_group(carry, data):
        block, cotan, lengths, counts, mask = data
        segment = segment_ids(lengths, jnp.arange(LEN, dtype=jnp.int32))
        weight_rows = loss_weight(lengths, counts, mask, 0, LEN)

        def run(block_f, attend_w, output_w, expand_w, reduce_w, vector_w):
            return forward(block_f, attend_w, output_w, expand_w, reduce_w, vector_w, segment)
        result, pull = jax.vjp(run, block.astype(jnp.float32), *weights)
        grads = pull(cotan.astype(jnp.float32) * weight_rows[..., None])
        new_carry = tuple((total + piece for total, piece in zip(carry, grads[1:])))
        return (new_carry, (result.astype(jnp.bfloat16), grads[0].astype(jnp.bfloat16)))
    start = tuple((jnp.zeros_like(weight) for weight in weights))
    data = (block_input.reshape(groups, group, LEN, D), cotangent.reshape(groups, group, LEN, D), segment_lengths.reshape(groups, group, SEGS), thought_counts.reshape(groups, group, SEGS), packing_mask.reshape(groups, group, LEN))
    totals, (hidden, backed) = lax.scan(one_group, start, data)
    hidden_states = hidden.reshape(SEQS, LEN, D)
    input_gradient = backed.reshape(SEQS, LEN, D)
    firsts = (first_attend, first_output, first_expand, first_reduce, first_vectors)
    seconds = (second_attend, second_output, second_expand, second_reduce, second_vectors)
    adapted = [adapt(totals[number], firsts[number], seconds[number], weights[number]) for number in range(5)]
    weight_squares = jnp.concatenate([jnp.stack([jnp.sum(weights[number] * weights[number]) for number in range(4)]), lax.optimization_barrier(jnp.sum(vectors * vectors, axis=0))])
    update_squares = jnp.concatenate([jnp.stack([jnp.sum(adapted[number][2] * adapted[number][2]) for number in range(4)]), lax.optimization_barrier(jnp.sum(adapted[4][2] * adapted[4][2], axis=0))])
    weight_norm = jnp.sqrt(weight_squares)
    update_norm = jnp.sqrt(update_squares)
    ratio = weight_norm / (update_norm + ADAM_EPS)
    masters = [weights[number] - RATE * ratio[number] * adapted[number][2] for number in range(4)]
    masters.append(vectors - RATE * ratio[4:][None, :] * adapted[4][2])
    trust_norms = jnp.log(jnp.stack([weight_norm, update_norm, ratio]))
    return (hidden_states, input_gradient, adapted[0][0], adapted[1][0], adapted[2][0], adapted[3][0], adapted[4][0], adapted[0][1], adapted[1][1], adapted[2][1], adapted[3][1], adapted[4][1], masters[0], masters[1], masters[2], masters[3], masters[4], trust_norms)
```

```python
import jax
import jax.numpy as jnp
from jax import lax
from jax.experimental import pallas as pl
from jax.experimental.pallas import tpu as pltpu
from jax.sharding import PartitionSpec as P

HEAD_DIM = 64
THOUGHT_TOKENS = 8
STEP = 6
PARTS = 32
SPAN = 256
BLOCK = 128

NORM_EPS = 1e-05
NEGATIVE = -1e30
BETA = 0.5
RATE = 0.5
DECAY = 0.01
ADAM_EPS = 1e-06
AXES = ("batch", "head")
ROOT = 0.7978845608028654
CUBE = 0.044715
F32 = jnp.float32
BF16 = jnp.bfloat16
NT = (((1,), (1,)), ((), ()))
TN = (((0,), (0,)), ((), ()))


def dot(a, b, dims=(((1,), (0,)), ((), ()))):
    return lax.dot_general(a, b, dims, preferred_element_type=F32)


def params(grid=1, vmem=60):
    return pltpu.CompilerParams(
        dimension_semantics=("arbitrary",) * grid, vmem_limit_bytes=vmem * 1024 * 1024
    )


def cost(micros):
    return pl.CostEstimate(flops=int(micros * 0.29e9), bytes_accessed=1 << 18, transcendentals=0)


def whole(shape):
    return pl.BlockSpec(shape, lambda *_: (0,) * len(shape), pipeline_mode=pl.Buffered(1))


SCALARS = pl.BlockSpec(memory_space=pltpu.SMEM)


def row_facts(lengths, counts, mask, span):
    positions = jnp.arange(span, dtype=jnp.int32)
    ends = jnp.cumsum(lengths, axis=-1)
    starts = ends - lengths
    inside = (positions[None, :, None] >= starts[:, None, :]) & (
        positions[None, :, None] < ends[:, None, :]
    )
    start_of = jnp.sum(jnp.where(inside, starts[:, None, :], 0), axis=-1)
    passes = jnp.sum(jnp.where(inside, counts[:, None, :], 0), axis=-1)
    keep = (positions[None, :] - start_of >= THOUGHT_TOKENS * passes) & (mask > 0)
    return start_of, keep.astype(F32)


def windows(length):
    return [
        (low, max(0, low - SPAN), low + BLOCK - max(0, low - SPAN)) for low in range(0, length, BLOCK)
    ]


def fill_caps(start_ref, cap_ref, length):
    for number, (low, first, count) in enumerate(windows(length)):
        key = lax.broadcasted_iota(jnp.int32, (count, BLOCK), 0) + first
        query = lax.broadcasted_iota(jnp.int32, (count, BLOCK), 1) + low
        start = start_ref[0, :, low : low + BLOCK]
        allowed = (key <= query) & (key >= start)
        cap_ref[number, :count] = jnp.where(allowed, 3e38, NEGATIVE)


def cap_of(cap_ref, number, count):
    cap = cap_ref[number, :count]
    return jnp.concatenate([cap, cap], axis=1)


def for_heads(values):
    lane = lax.broadcasted_iota(jnp.int32, (1, 2 * HEAD_DIM), 1)
    return jnp.concatenate(
        [jnp.where(lane < HEAD_DIM, values, 0), jnp.where(lane >= HEAD_DIM, values, 0)], axis=0
    )


def of_heads(values):
    return jnp.concatenate([values[:HEAD_DIM, :BLOCK], values[HEAD_DIM:, BLOCK:]], axis=0)


def in_stages(units, ahead, behind, first, middle, last):
    started, worked = [first(unit) for unit in units[:ahead]], []
    for number, unit in enumerate(units):
        if number + ahead < len(units):
            started.append(first(units[number + ahead]))
        worked.append((unit, middle(unit, started.pop(0))))
        if len(worked) > behind:
            last(*worked.pop(0))
    for both in worked:
        last(*both)


def attend_forward_kernel(fresh, start_ref, q_ref, k_ref, v_ref, o_ref, log_ref, cap_ref):
    length = q_ref.shape[0]
    pl.when(fresh)(lambda: fill_caps(start_ref, cap_ref, length))
    value_t = v_ref[...].T

    def score(unit):
        _, (low, first, count) = unit
        query = for_heads(q_ref[low : low + BLOCK, :] * (HEAD_DIM**-0.5))
        return dot(k_ref[first : first + count, :], query, NT)

    def soften(unit, scores):
        number, (low, _, count) = unit
        scores = jnp.minimum(scores, cap_of(cap_ref, number, count))
        top = jnp.max(scores, axis=0, keepdims=True)
        grown = jnp.exp(scores - top)
        whole_sum = jnp.sum(grown, axis=0, keepdims=True)
        logs = top + jnp.log(whole_sum)
        log_ref[0, 0, :, low : low + BLOCK] = jnp.concatenate(
            [logs[:, :BLOCK], logs[:, BLOCK:]], axis=0
        )
        return grown.astype(BF16), 1.0 / whole_sum

    def mix(unit, found):
        _, (low, first, count) = unit
        grown, scale = found
        result = dot(value_t[:, first : first + count], grown) * scale
        o_ref[low : low + BLOCK, :] = of_heads(result).T.astype(BF16)

    in_stages(list(enumerate(windows(length))), 4, 1, score, soften, mix)


def attend_backward_kernel(
    fresh, start_ref, q_ref, k_ref, v_ref, o_ref, do_ref, log_ref, *rest
):
    d_ref, cap_ref = rest[-2:]
    length = q_ref.shape[0]
    pl.when(fresh)(lambda: fill_caps(start_ref, cap_ref, length))
    key_t = k_ref[...].T
    grad_key, grad_value = {}, {}

    def query_of(low):
        return for_heads(q_ref[low : low + BLOCK, :] * (HEAD_DIM**-0.5))

    def grad_of(low):
        return for_heads(do_ref[low : low + BLOCK, :])

    def side_by_side(values):
        return jnp.concatenate(values, axis=1)

    def score(unit):
        _, (low, first, count) = unit
        key, value = k_ref[first : first + count, :], v_ref[first : first + count, :]
        return dot(key, query_of(low), NT), dot(value, grad_of(low), NT)

    def soften(unit, found):
        number, (low, _, count) = unit
        scores, grad_probs = found
        product = do_ref[low : low + BLOCK, :].astype(F32) * o_ref[low : low + BLOCK, :].astype(F32)
        product = product.T
        inner = side_by_side([total(product[:HEAD_DIM]), total(product[HEAD_DIM:])])
        logs = side_by_side([log_ref[0, 0, h : h + 1, low : low + BLOCK] for h in range(2)])
        probs = jnp.exp(jnp.minimum(scores, cap_of(cap_ref, number, count)) - logs)
        return probs.astype(BF16), (probs * (grad_probs - inner)).astype(BF16)

    def mix(unit, found):
        _, (low, first, count) = unit
        probs, grad_scores = found
        terms = dot(probs, grad_of(low)), dot(grad_scores, query_of(low))
        grad_query = dot(key_t[:, first : first + count], grad_scores)
        d_ref[0, low : low + BLOCK, :] = (of_heads(grad_query).T * (HEAD_DIM**-0.5)).astype(BF16)
        for sums, term, place in ((grad_value, terms[0], 2), (grad_key, terms[1], 1)):
            for at in range(first, first + count, BLOCK):
                one = term[at - first : at - first + BLOCK]
                sums[at] = sums[at] + one if at in sums else one
            for at in list(sums):
                if at <= low - SPAN or low + BLOCK == length:
                    d_ref[place, at : at + BLOCK, :] = sums.pop(at).astype(BF16)

    in_stages(list(enumerate(windows(length))), 2, 0, score, soften, mix)


def attention_specs(length, pairs, low=0):
    pair = 2 * HEAD_DIM

    def at(i):
        return (i + low) // pairs, (i + low) % pairs

    def columns(n):
        return lambda i: (at(i)[0], n * pairs + at(i)[1])

    qkv = [pl.BlockSpec((length, pair), columns(n)) for n in range(3)]
    rows = pl.BlockSpec((length, pair), columns(0))
    logs = pl.BlockSpec((1, 1, 2, length), lambda i: (*at(i), 0, 0))
    start = pl.BlockSpec((1, 1, length), lambda i: (at(i)[0], 0, 0))
    return start, qkv, rows, logs, lambda i: (0, *at(i))


def attend_forward(start, qkv, length):
    tokens, model = qkv.shape[0], qkv.shape[1] // 3
    pairs = model // (2 * HEAD_DIM)
    rows = tokens // length
    start_spec, qkv_specs, row_spec, log_spec, _ = attention_specs(length, pairs)

    def kernel(*refs):
        attend_forward_kernel(pl.program_id(0) % pairs == 0, *refs)

    return pl.pallas_call(
        kernel,
        grid=(rows * pairs,),
        in_specs=[start_spec] + qkv_specs,
        out_specs=[row_spec, log_spec],
        out_shape=[
            jax.ShapeDtypeStruct((tokens, model), BF16),
            jax.ShapeDtypeStruct((rows, pairs, 2, length), F32),
        ],
        scratch_shapes=[pltpu.VMEM((length // BLOCK, SPAN + BLOCK, BLOCK), F32)],
        compiler_params=params(),
        cost_estimate=cost(18),
        name="attend_forward",
    )(start, qkv, qkv, qkv)


def attend_backward(start, qkv, out, grad, logs, length, low, high, before=None):
    tokens, model = out.shape
    pairs = model // (2 * HEAD_DIM)
    start_spec, qkv_specs, row_spec, log_spec, at = attention_specs(length, pairs, low)
    operands = [start, qkv, qkv, qkv, out, grad, logs]
    in_specs = [start_spec] + qkv_specs + [row_spec, row_spec, log_spec]
    aliases = {}
    if before is not None:
        aliases = {len(operands): 0}
        operands.append(before)
        in_specs.append(pl.BlockSpec(memory_space=pl.ANY))

    def kernel(*refs):
        fresh = (pl.program_id(0) == 0) | ((pl.program_id(0) + low) % pairs == 0)
        attend_backward_kernel(fresh, *refs)

    return pl.pallas_call(
        kernel,
        grid=(high - low,),
        in_specs=in_specs,
        out_specs=pl.BlockSpec((3, length, 2 * HEAD_DIM), at),
        out_shape=jax.ShapeDtypeStruct((3, tokens, model), BF16),
        scratch_shapes=[pltpu.VMEM((length // BLOCK, SPAN + BLOCK, BLOCK), F32)],
        input_output_aliases=aliases,
        compiler_params=params(),
        cost_estimate=cost(2.3 * (high - low)),
        name="attend_backward",
    )(*operands)


def normalize(values):
    centre = values - jnp.mean(values, axis=-1, keepdims=True)
    factor = lax.rsqrt(jnp.mean(centre * centre, axis=-1, keepdims=True) + NORM_EPS)
    return centre * factor, factor


def norm_back(inner, normed, factor):
    return factor * (
        inner
        - jnp.mean(inner, axis=-1, keepdims=True)
        - normed * jnp.mean(inner * normed, axis=-1, keepdims=True)
    )


def total(values):
    return jnp.sum(values, axis=0, keepdims=True)


def project_kernel(place_ref, x_ref, own_ref, other_ref, nl_ref, qkv_ref, w_ref, vec_ref, *, heads):
    slots, rows, flat = own_ref.shape
    rows -= -(-vec_ref.shape[0] // 16) * 16
    part, model = flat // 3, x_ref.shape[1]
    groups = bit_groups(2 * slots)
    place = place_ref[0]

    @pl.when(pl.program_id(0) == 0)
    def _():
        for here in range(heads):

            @pl.when(place % heads == here)
            def _(here=here):
                for bit, ref in enumerate((own_ref, other_ref)):
                    for slot in range(slots):
                        mask = mask_of(slot, groups) | bit
                        head = here ^ (mask % heads)
                        row = pl.multiple_of(((place ^ mask) // heads) * rows, rows)
                        for j in range(3):
                            low = j * model + head * part
                            w_ref[pl.ds(row, rows), low : low + part] = ref[
                                slot, :rows, j * part : (j + 1) * part
                            ]

        count, each = vec_ref.shape[0], model // (2 * slots)
        lane = lax.broadcasted_iota(jnp.int32, (1, model), 1)
        found = jnp.zeros((count, model), F32)
        for bit, ref in enumerate((own_ref, other_ref)):
            for slot in range(slots):
                device = place ^ (mask_of(slot, groups) | bit)
                piece = ref[slot, rows:, :128].astype(F32)[:count]
                piece = jnp.concatenate([piece] * (model // 128), axis=1)
                piece = pltpu.roll(piece, (device * each) % 128, 1)
                inside = (lane >= device * each) & (lane < (device + 1) * each)
                found = jnp.where(inside, piece, found)
        vec_ref[...] = found

    normed, _ = normalize(x_ref[...].astype(F32))
    low = (normed * vec_ref[0:1, :] + vec_ref[1:2, :]).astype(BF16)
    nl_ref[...] = low
    for j in range(3):
        side = slice(j * model, (j + 1) * model)
        result = dot(low, w_ref[:, side])
        if j != 1:
            result = result + vec_ref[2 + j // 2 : 3 + j // 2, :]
        qkv_ref[:, side] = result.astype(BF16)


def project(place, x, own, other, heads, cols, tile=512):
    tokens, model = x.shape
    row = pl.BlockSpec((tile, model), lambda i: (i, 0))
    return pl.pallas_call(
        lambda *refs: project_kernel(*refs, heads=heads),
        grid=(tokens // tile,),
        in_specs=[SCALARS, row, whole(own.shape), whole(other.shape)],
        out_specs=[
            row,
            pl.BlockSpec((tile, 3 * model), lambda i: (i, 0)),
            pl.BlockSpec((model, 3 * model), lambda i: (0, 0)),
            pl.BlockSpec((cols, model), lambda i: (0, 0)),
        ],
        out_shape=[
            jax.ShapeDtypeStruct((tokens, model), BF16),
            jax.ShapeDtypeStruct((tokens, 3 * model), BF16),
            jax.ShapeDtypeStruct((model, 3 * model), BF16),
            jax.ShapeDtypeStruct((cols, model), F32),
        ],
        compiler_params=params(),
        cost_estimate=cost(14),
        name="project",
    )(place, x, own, other)


class Late:
    def __init__(self, refs, scratch):
        (self.parts,) = refs
        self.expand, self.reduce, self.output, self.stage, self.sem = scratch
        self.model = self.output.shape[1]
        self.chunks = self.expand.shape[0]

    def copies(self):
        per = self.model // self.stage.shape[1]
        red = self.reduce.shape[0] // (2 * self.stage.shape[1])
        end = 2 * per + red
        for device in range(self.parts.shape[0]):
            row, bit = (device // 2) * per, device % 2
            for n in range(2):
                yield (
                    self.parts.at[device, n * per : (n + 1) * per],
                    self.expand.at[2 * bit + n, row : row + per],
                )
            yield (
                self.parts.at[device, 2 * per : end],
                self.reduce.at[device * red : (device + 1) * red],
            )
            yield (
                self.parts.at[device, end : end + self.stage.shape[2]],
                self.stage.at[bit, device // 2],
            )

    def load(self):
        copies = [pltpu.make_async_copy(a, b, self.sem) for a, b in self.copies()]
        for copy in copies:
            copy.start()
        for copy in copies:
            copy.wait()
        slots = self.stage.shape[1]
        per = self.model // slots
        for n in range(slots):
            both = [self.stage[bit, n, : per // 2, :].astype(F32) for bit in range(2)]
            self.output[n * per : (n + 1) * per, :] = jnp.concatenate(both, axis=0).astype(BF16)

    def reduce_rows(self, c):
        return self.reduce[c * self.model : (c + 1) * self.model, :]

    @staticmethod
    def specs():
        return [pl.BlockSpec(memory_space=pl.ANY)]

    @staticmethod
    def scratch(late, hidden):
        slots, _, model = late[0].shape
        slots //= 2
        return [
            pltpu.VMEM((hidden // model, model, model), BF16),
            pltpu.VMEM((hidden, model), BF16),
            pltpu.VMEM((model, model), BF16),
            pltpu.VMEM((2, slots, 32, model), BF16),
            pltpu.SemaphoreType.DMA,
        ]


def mlp_forward_kernel(*refs):
    late = Late(refs[:-16], refs[-5:])
    ctx_ref, x_ref, cot_ref, wt_ref, vec_ref = refs[-16:-11]
    hid_ref, mid_ref, nm_ref, act_ref, dg_ref, gb_ref = refs[-11:-5]
    model = late.model
    pl.when(pl.program_id(0) == 0)(late.load)
    middle = x_ref[...].astype(F32) + dot(ctx_ref[...], late.output[...]) + vec_ref[4:5, :]
    mid_ref[...] = middle
    gb_ref[...] = (cot_ref[...].astype(F32) * wt_ref[...]).astype(BF16)
    normed, _ = normalize(middle)
    low = (normed * vec_ref[5:6, :] + vec_ref[6:7, :]).astype(BF16)
    nm_ref[...] = low
    result = middle + vec_ref[7:8, :]
    for c in range(late.chunks):
        side = slice(c * model, (c + 1) * model)
        pre = dot(low, late.expand[c]) + vec_ref[8 + c : 9 + c, :]
        square = pre * pre
        half = 0.5 + 0.5 * jnp.tanh(pre * (ROOT + (ROOT * CUBE) * square))
        act = pre * half
        dg = half + act * (1.0 - half) * (2.0 * ROOT + (6.0 * ROOT * CUBE) * square)
        dg_ref[:, side] = dg.astype(BF16)
        act = act.astype(BF16)
        act_ref[:, side] = act
        result = result + dot(act, late.reduce_rows(c))
    hid_ref[...] = result.astype(BF16)


def mlp_forward(late, ctx, x, cot, wt, vec, hidden, tile=256):
    tokens, model = x.shape
    row = pl.BlockSpec((tile, model), lambda i: (i, 0))
    wide = pl.BlockSpec((tile, hidden), lambda i: (i, 0))
    one = pl.BlockSpec((tile, 1), lambda i: (i, 0))

    def shape(width, kind=BF16):
        return jax.ShapeDtypeStruct((tokens, width), kind)

    return pl.pallas_call(
        mlp_forward_kernel,
        grid=(tokens // tile,),
        in_specs=Late.specs() + [row, row, row, one, whole(vec.shape)],
        out_specs=[row, row, row, wide, wide, row],
        out_shape=[
            shape(model), shape(model, F32), shape(model), shape(hidden), shape(hidden), shape(model),
        ],
        scratch_shapes=Late.scratch(late, hidden),
        compiler_params=params(),
        cost_estimate=cost(40),
        name="mlp_forward",
    )(*late, ctx, x, cot, wt, vec)


def mlp_backward_kernel(*refs):
    late = Late(refs[:-15], refs[-5:])
    cot_ref, wt_ref, mid_ref, dg_ref, vec_ref = refs[-15:-10]
    gpre_ref, gm_ref, ga_ref, gc_ref, sum_ref = refs[-10:-5]
    model = late.model

    @pl.when(pl.program_id(0) == 0)
    def _():
        late.load()
        sum_ref[...] = jnp.zeros_like(sum_ref)

    grad_out = cot_ref[...].astype(F32) * wt_ref[...]
    branch = grad_out.astype(BF16)
    sum_ref[3:4, :] += total(branch.astype(F32))
    back = None
    for c in range(late.chunks):
        side = slice(c * model, (c + 1) * model)
        grad = (dot(branch, late.reduce_rows(c), NT) * dg_ref[:, side].astype(F32)).astype(BF16)
        gpre_ref[:, side] = grad
        sum_ref[4 + c : 5 + c, :] += total(grad.astype(F32))
        term = dot(grad, late.expand[c], NT)
        back = term if back is None else back + term
    normed, factor = normalize(mid_ref[...])
    sum_ref[1:2, :] += total(back * normed)
    sum_ref[2:3, :] += total(back)
    grad_middle = grad_out + norm_back(back * vec_ref[5:6, :], normed, factor)
    gm_ref[...] = grad_middle
    low = grad_middle.astype(BF16)
    ga_ref[...] = low
    sum_ref[0:1, :] += total(low.astype(F32))
    gc_ref[...] = dot(low, late.output[...], NT).astype(BF16)


def mlp_backward(late, cot, wt, mid, dg, vec, tile=256):
    tokens, model = cot.shape
    hidden = dg.shape[1]
    row = pl.BlockSpec((tile, model), lambda i: (i, 0))
    wide = pl.BlockSpec((tile, hidden), lambda i: (i, 0))
    one = pl.BlockSpec((tile, 1), lambda i: (i, 0))

    def shape(width, kind=BF16):
        return jax.ShapeDtypeStruct((tokens, width), kind)

    return pl.pallas_call(
        mlp_backward_kernel,
        grid=(tokens // tile,),
        in_specs=Late.specs() + [row, one, row, wide, whole(vec.shape)],
        out_specs=[wide, row, row, row, pl.BlockSpec((8, model), lambda i: (0, 0))],
        out_shape=[
            shape(hidden), shape(model, F32), shape(model), shape(model),
            jax.ShapeDtypeStruct((8, model), F32),
        ],
        scratch_shapes=Late.scratch(late, hidden),
        compiler_params=params(),
        cost_estimate=cost(36),
        name="mlp_backward",
    )(*late, cot, wt, mid, dg, vec)


def put_parts(place, outs, pieces, turn=False):
    groups = bit_groups(2 * outs[0].shape[0])
    for bit in range(2):

        @pl.when(place % 2 == bit)
        def _(bit=bit):
            for device, index, value in pieces:
                mask = place ^ device
                slot = slot_of(turned(mask, groups) if turn else mask, groups)
                outs[(device % 2) ^ bit][(slot,) + index] = value


def reduce_weight_grad_kernel(place_ref, a_ref, b_ref, *outs):
    slots, rows, _ = outs[0].shape
    result = dot(a_ref[...], b_ref[...], TN).astype(BF16)
    count = result.shape[0] // (2 * rows)
    for step in range(2 * slots // count):

        @pl.when(pl.program_id(0) == step)
        def _(step=step):
            for half in range(2):
                put_parts(
                    place_ref[0],
                    outs[half::2],
                    [
                        (
                            step * count + n,
                            (),
                            result[(2 * n + half) * rows : (2 * n + half + 1) * rows],
                        )
                        for n in range(count)
                    ],
                    half == 1,
                )


def outs_of(*shapes):
    return dict(
        out_specs=[pl.BlockSpec(shape, lambda *_: (0,) * len(shape)) for shape in shapes],
        out_shape=[jax.ShapeDtypeStruct(shape, BF16) for shape in shapes],
    )


def reduce_weight_grad(place, act, branch):
    tokens, model = branch.shape
    hidden = act.shape[1]
    shape = (PARTS // 2, hidden // PARTS // 2, model)
    found = pl.pallas_call(
        reduce_weight_grad_kernel,
        grid=(hidden // model,),
        in_specs=[SCALARS, pl.BlockSpec((tokens, model), lambda i: (0, i)), whole(branch.shape)],
        **outs_of(*[shape] * 4),
        compiler_params=params(),
        cost_estimate=cost(15),
        name="reduce_weight_grad",
    )(place, act, branch)
    return found[:2], found[2:]


def mid_weight_grad_kernel(place_ref, nm_ref, gpre_ref, ctx_ref, ga_ref, *outs):
    slots, rows, model = outs[0].shape
    per = model // slots
    step = pl.program_id(0)
    last = pl.num_programs(0) - 1
    place = place_ref[0]

    for c in range(4):

        @pl.when(step == c)
        def _(c=c):
            result = dot(nm_ref[...], gpre_ref[...], TN).astype(BF16)
            put_parts(
                place,
                outs[c % 2 :: 2],
                [
                    (2 * n + c // 2, (slice(0, per),), result[n * per : (n + 1) * per])
                    for n in range(slots)
                ],
                c % 2 == 1,
            )

    @pl.when(step == last)
    def _():
        result = dot(ctx_ref[...], ga_ref[...], TN)
        half = per // 2
        empty = jnp.zeros((rows - per - half, model), F32)
        put_parts(
            place,
            outs[::2],
            [
                (
                    n,
                    (slice(per, rows),),
                    jnp.concatenate([result[n * half : (n + 1) * half], empty], axis=0).astype(BF16),
                )
                for n in range(2 * slots)
            ],
        )


def mid_weight_grad(place, nm, gpre, ctx, ga):
    tokens, model = nm.shape
    hidden = gpre.shape[1]
    assert hidden == 4 * model
    slots, per = PARTS // 2, 2 * model // PARTS
    shapes = [(slots, per + 32, model), (slots, per, model)]
    found = pl.pallas_call(
        mid_weight_grad_kernel,
        grid=(5,),
        in_specs=[
            SCALARS,
            whole(nm.shape),
            pl.BlockSpec((tokens, model), lambda i: (0, jnp.minimum(i, 3))),
            whole(ctx.shape),
            whole(ga.shape),
        ],
        **outs_of(*shapes * 2),
        compiler_params=params(),
        cost_estimate=cost(19),
        name="mid_weight_grad",
    )(place, nm, gpre, ctx, ga)
    return found[:2], found[2:]


def attend_weight_grad_kernel(place_ref, a_ref, b_ref, keep_ref, send_ref, *, heads):
    slots, rows, flat = keep_ref.shape
    part = flat // 3
    result = dot(a_ref[...], b_ref[0], TN).astype(BF16)
    for j in range(3):

        @pl.when(pl.program_id(0) == j)
        def _(j=j):
            put_parts(
                place_ref[0],
                (keep_ref, send_ref),
                [
                    (
                        d,
                        (slice(None), slice(j * part, (j + 1) * part)),
                        result[
                            d // heads * rows : (d // heads + 1) * rows,
                            d % heads * part : (d % heads + 1) * part,
                        ],
                    )
                    for d in range(2 * slots)
                ],
            )


def attend_weight_grad(place, nl, d_qkv, heads):
    tokens, model = nl.shape
    return pl.pallas_call(
        lambda *refs: attend_weight_grad_kernel(*refs, heads=heads),
        grid=(3,),
        in_specs=[SCALARS, whole(nl.shape), pl.BlockSpec((1, tokens, model), lambda j: (j, 0, 0))],
        **outs_of(*[(PARTS // 2, model * heads // PARTS, 3 * model // heads)] * 2),
        compiler_params=params(),
        cost_estimate=cost(13),
        name="attend_weight_grad",
    )(place, nl, d_qkv)


def input_grad_kernel(d_ref, x_ref, gm_ref, w_ref, vec_ref, mid_ref, out_ref, sum_ref):
    model = x_ref.shape[1]

    @pl.when(pl.program_id(0) == 0)
    def _():
        sum_ref[:4, :] = jnp.zeros((4, model), F32)
        sum_ref[4:, :] = mid_ref[...]

    back = None
    for j in range(3):
        term = dot(d_ref[j], w_ref[:, j * model : (j + 1) * model], NT)
        back = term if back is None else back + term
    normed, factor = normalize(x_ref[...].astype(F32))
    sum_ref[0:1, :] += total(back * normed)
    sum_ref[1:2, :] += total(back)
    sum_ref[2:3, :] += total(d_ref[0].astype(F32))
    sum_ref[3:4, :] += total(d_ref[2].astype(F32))
    out_ref[...] = (gm_ref[...] + norm_back(back * vec_ref[0:1, :], normed, factor)).astype(BF16)


def input_grad(d_qkv, x, gm, w, vec, mid_sums, tile=512):
    tokens, model = x.shape
    row = pl.BlockSpec((tile, model), lambda i: (i, 0))
    return pl.pallas_call(
        input_grad_kernel,
        grid=(tokens // tile,),
        in_specs=[
            pl.BlockSpec((3, tile, model), lambda i: (0, i, 0)), row, row,
            whole(w.shape), whole(vec.shape), whole(mid_sums.shape),
        ],
        out_specs=[row, pl.BlockSpec(vec.shape, lambda i: (0, 0))],
        out_shape=[
            jax.ShapeDtypeStruct((tokens, model), BF16), jax.ShapeDtypeStruct(vec.shape, F32),
        ],
        compiler_params=params(),
        cost_estimate=cost(16),
        name="input_grad",
    )(d_qkv, x, gm, w, vec, mid_sums)


def bit_groups(count):
    bits = count.bit_length() - 1
    assert count == 1 << bits
    return [(0, 1)] + [(low, min(2, bits - low)) for low in range(1, bits, 2)]


def slot_of(mask, groups):
    slot = 0
    for low, width in groups[1:]:
        slot = slot * (1 << width) + ((mask >> low) & ((1 << width) - 1))
    return slot


def mask_of(slot, groups):
    mask = 0
    for low, width in groups[:0:-1]:
        mask |= (slot & ((1 << width) - 1)) << low
        slot >>= width
    return mask


def swap(value, mask):
    count = lax.axis_size("batch") * lax.axis_size("head")
    return lax.ppermute(value, AXES, [(i, i ^ mask) for i in range(count)])


def spread(piece, group):
    low, width = group
    return [piece] + [swap(piece, step << low) for step in range(1, 1 << width)]


def join(parts):
    return jnp.concatenate(parts, axis=0)


def gather_far(piece, groups):
    piece = piece[None]
    for group in groups[:1:-1]:
        piece = join(spread(piece, group))
    return piece


def ordered(*values):
    return lax.optimization_barrier(values)


class Halves:
    def __init__(self, keep, send, groups):
        self.groups = groups
        self.bits = [2 << groups[1][0], 1 << groups[1][0]]
        self.terms = [[kept, swap(sent, 1)] for kept, sent in zip(keep, send)]
        self.count = keep[0].shape[0]

    def flat(self):
        return [t for terms in self.terms for t in terms]

    def set(self, flat):
        count = len(self.terms[0])
        self.terms = [list(flat[:count]), list(flat[count:])]

    def sends(self):
        self.count //= 2
        here = slice(self.count, 2 * self.count)
        return [added([t[here] for t in terms]).astype(BF16) for terms in self.terms]

    def receive(self, sends):
        received = [swap(send, bit) for send, bit in zip(sends, self.bits)]
        self.bits = self.bits[::-1]
        return received

    def add(self, received):
        self.terms = [terms + [one] for terms, one in zip(self.terms, received)]

    def at(self, slot):
        return jnp.concatenate([added([t[slot] for t in terms]) for terms in self.terms], axis=0)

    def last_sends(self):
        return [self.at(slot).astype(BF16) for slot in range(1, self.count)]

    def last_receive(self, sends):
        return [swap(send, (n + 1) << self.groups[2][0]) for n, send in enumerate(sends)]

    def finish(self, received):
        return added([self.at(0), *received])


class Whole:
    def __init__(self, keep, send, groups):
        self.groups = groups
        self.terms = [keep, swap(send, 1)]
        self.count = keep.shape[0]

    def sends(self):
        self.count //= 4
        return [
            added([t[n * self.count : (n + 1) * self.count] for t in self.terms]).astype(BF16)
            for n in range(1, 4)
        ]

    def receive(self, sends):
        return [swap(send, (n + 1) << self.groups[1][0]) for n, send in enumerate(sends)]

    def last_sends(self):
        return [added([t[n] for t in self.terms]).astype(BF16) for n in range(1, self.count)]

    def last_receive(self, sends):
        return [swap(send, (n + 1) << self.groups[2][0]) for n, send in enumerate(sends)]

    def finish(self, received):
        return added([added([t[0] for t in self.terms]), *received])


def added(terms):
    return sum(term.astype(F32) for term in terms)


def scatter(keep, send, groups):
    terms = [keep, swap(send, 1)]
    for low, width in groups[1:]:
        count = 1 << width
        terms = [t.reshape((count, -1) + t.shape[1:]) for t in terms]
        sends = [added([t[step] for t in terms]).astype(BF16) for step in range(1, count)]
        terms = [added([t[0] for t in terms])]
        terms += [swap(send, (n + 1) << low) for n, send in enumerate(sends)]
    return added(terms)[0]


def all_sum(value, groups):
    for low, width in groups:
        value = sum([swap(value, s << low) for s in range(1, 1 << width)], value)
    return value


def turned(mask, groups):
    low = groups[1][0]
    both = (mask >> low) & 3
    return mask ^ ((both ^ (both >> 1) ^ ((both & 1) << 1)) << low)


def slot_masks(groups, turn=False):
    masks = [mask_of(slot, groups) for slot in range(1 << sum(width for _, width in groups[1:]))]
    return [turned(mask, groups) for mask in masks] if turn else masks


def in_order(parts, masks, place):
    found = [mask for part in masks for mask in part]
    slots = [0] * len(found)
    for slot, mask in enumerate(found):
        slots[mask] = slot
    devices = jnp.arange(len(found), dtype=jnp.int32)
    return jnp.take(join(parts), jnp.asarray(slots, jnp.int32)[place ^ devices], axis=0)


def by_slot(parts, place, groups):
    masks = jnp.asarray(slot_masks(groups), jnp.int32)
    return [jnp.take(parts, place ^ (masks | bit), axis=0) for bit in range(2)]


def adapt_kernel(rows, *refs):
    count = len(rows)
    inputs, outputs = refs[: 4 * count + 1], refs[4 * count + 1 :]
    sum_ref = outputs[-1]
    sum_ref[...] = inputs[-1][...]
    half = sum_ref.shape[0] // 2
    correct = 1.0 - BETA**STEP
    for number, row in enumerate(rows):
        grad_ref, first_ref, second_ref, weight_ref = inputs[4 * number : 4 * number + 4]
        moment_ref, square_ref, update_ref = outputs[3 * number : 3 * number + 3]
        planes = weight_ref.shape[0] if len(weight_ref.shape) == 3 else 1
        width = grad_ref.shape[1] // planes
        norms = []
        for n in range(planes):
            at = n if len(weight_ref.shape) == 3 else Ellipsis
            grad = grad_ref[:, n * width : (n + 1) * width]
            moment = BETA * first_ref[at] + (1.0 - BETA) * grad
            square = BETA * second_ref[at] + (1.0 - BETA) * grad * grad
            weight = weight_ref[at]
            update = moment / correct / (jnp.sqrt(square / correct) + ADAM_EPS) + DECAY * weight
            moment_ref[at] = moment
            square_ref[at] = square
            update_ref[at] = update
            norms.append([jnp.sum(v * v, axis=1, keepdims=True) for v in (weight, update)])
        for n in range(2):
            norm = sum(both[n] for both in norms)
            if row < 4:
                norm = total(norm)
            place = n * half + row
            sum_ref[place : place + norm.shape[0], :] = jnp.broadcast_to(norm, (norm.shape[0], 128))


def adapt(states, rows, sums=None):
    if sums is None:
        sums = jnp.zeros((32, 128), F32)
    operands = [array for state in states for array in state] + [sums]
    shapes = [state[3].shape for state in states for _ in range(3)] + [sums.shape]
    *found, sums = pl.pallas_call(
        lambda *refs: adapt_kernel(rows, *refs),
        grid=(1,),
        in_specs=[whole(a.shape) for a in operands],
        out_specs=[pl.BlockSpec(s, lambda *_, n=len(s): (0,) * n) for s in shapes],
        out_shape=[jax.ShapeDtypeStruct(s, F32) for s in shapes],
        compiler_params=params(),
        cost_estimate=cost(4),
        name="adapt",
    )(*operands)
    return [found[3 * n : 3 * n + 3] for n in range(len(states))], sums


def master_kernel(sum_ref, *refs):
    *refs, trust_ref = refs
    count = len(refs) // 3
    half = sum_ref.shape[0] // 2
    norms = [jnp.sqrt(sum_ref[n * half : (n + 1) * half, :]) for n in range(2)]
    ratio = norms[0] / (norms[1] + ADAM_EPS)
    row = lax.broadcasted_iota(jnp.int32, ratio.shape, 0)
    lane = lax.broadcasted_iota(jnp.int32, ratio.shape, 1)
    for n, value in enumerate([*norms, ratio]):
        line = jnp.log(total(jnp.where(row == lane, value, 0.0)))
        trust_ref[n : n + 1, :] = line[:, : trust_ref.shape[1]]
    for n in range(count):
        update_ref, weight_ref, out_ref = refs[n], refs[count + n], refs[2 * count + n]
        scale = RATE * (ratio[n : n + 1, :1] if n < 4 else ratio[4:, :1])
        for at in range(weight_ref.shape[0]) if len(weight_ref.shape) == 3 else [Ellipsis]:
            out_ref[at] = weight_ref[at] - scale * update_ref[at]


def master(sums, updates, weights):
    arrays = [sums, *updates, *weights]
    shapes = [a.shape for a in weights] + [(3, sums.shape[0] // 2)]
    return pl.pallas_call(
        master_kernel,
        grid=(1,),
        in_specs=[whole(a.shape) for a in arrays],
        out_specs=[pl.BlockSpec(s, lambda *_, n=len(s): (0,) * n) for s in shapes],
        out_shape=[jax.ShapeDtypeStruct(s, F32) for s in shapes],
        compiler_params=params(),
        cost_estimate=cost(3),
        name="master",
    )(*arrays)


def halves(parts, groups):
    return by_slot(parts, jnp.int32(0), groups)


def by_index(keep, send, groups, turn=False):
    masks = slot_masks(groups, turn)
    return in_order([keep, send], [masks, [mask | 1 for mask in masks]], jnp.int32(0))


def join_heads(pieces):
    nb, nh, rows, flat = pieces.shape
    wider = nb * nh // PARTS
    parts = pieces.reshape(nb // wider, wider, nh, rows, flat).transpose(0, 2, 1, 3, 4)
    return parts.reshape(PARTS, wider * rows, flat)


def join_parts(parts, nh):
    count = lax.axis_size("batch") * lax.axis_size("head")
    wider = count // PARTS
    _, rows, flat = parts.shape
    parts = parts.reshape(PARTS // nh, nh, wider, rows // wider, flat).transpose(0, 2, 1, 3, 4)
    return parts.reshape(count, rows // wider, flat)


def shards(
    block_input,
    cotangent,
    segment_lengths,
    thought_counts,
    packing_mask,
    attend_weight,
    output_weight,
    expand_weight,
    reduce_weight,
    vectors,
    first_attend,
    first_output,
    first_expand,
    first_reduce,
    first_vectors,
    second_attend,
    second_output,
    second_expand,
    second_reduce,
    second_vectors,
):
    nb, nh = lax.axis_size("batch"), lax.axis_size("head")
    count = nb * nh
    groups, kernel_groups = bit_groups(count), bit_groups(PARTS)
    same = count == PARTS
    place = (lax.axis_index("batch") * nh + lax.axis_index("head")).astype(jnp.int32)
    core = place % 2
    kernel_place = (place if same else jnp.zeros_like(place)).reshape(1)
    rows, length, model = block_input.shape
    tokens = rows * length
    hidden = expand_weight.shape[1]
    own_in, _, own_out = attend_weight.shape
    own = output_weight.shape[0]
    own_red = reduce_weight.shape[0]
    cols = vectors.shape[1]
    wide = hidden // model
    flat = 3 * own_out

    extra = jnp.pad(vectors.astype(BF16).T, ((0, -cols % 16), (0, flat - own)))
    piece = jnp.concatenate([attend_weight.astype(BF16).reshape(own_in, flat), extra], axis=0)
    attend_far = gather_far(piece, groups)

    blocks = expand_weight.astype(BF16).reshape(own, 2, wide // 2, model).transpose(1, 2, 0, 3)
    beside = swap(jnp.where(core == 0, blocks[1], blocks[0]), 1)
    mine = jnp.where(core == 0, blocks[0], blocks[1])
    piece = [
        jnp.concatenate(
            [jnp.where(core == 0, mine, beside), jnp.where(core == 0, beside, mine)], axis=1
        ).reshape(2 * own * (wide // 2), model),
        reduce_weight.astype(BF16),
        output_weight.astype(BF16),
    ]
    pad = -(own_red + own) % 16
    piece = jnp.concatenate(piece + [jnp.zeros((pad, model), BF16)], axis=0)
    late_all = lax.all_gather(piece, AXES, axis=0, tiled=False)
    attend_own = join(spread(attend_far, groups[1]))
    attend_other = swap(attend_own, 1)
    if not same:
        masks = slot_masks(groups)
        attend = in_order([attend_own, attend_other], [masks, [m | 1 for m in masks]], place)
        vec = attend[:, own_in:, :own].transpose(1, 0, 2).reshape(-1, PARTS, model // PARTS)
        vec = jnp.pad(vec.transpose(1, 0, 2), ((0, 0), (0, 0), (0, flat - model // PARTS)))
        attend = join_heads(attend[:, :own_in].reshape(nb, nh, own_in, flat))
        attend_own, attend_other = halves(
            jnp.concatenate([attend, vec], axis=1), kernel_groups
        )

    own_lengths = lax.dynamic_slice_in_dim(
        segment_lengths, lax.axis_index("head") * rows, rows, 0
    )
    own_counts = lax.dynamic_slice_in_dim(thought_counts, lax.axis_index("head") * rows, rows, 0)
    start_of, weight_rows = row_facts(own_lengths, own_counts, packing_mask, length)
    start_of = start_of.reshape(rows, 1, length)
    weight_rows = weight_rows.reshape(tokens, 1)

    x = block_input.reshape(tokens, model)
    cot = cotangent.reshape(tokens, model)
    normed_low, qkv, attend_low, vec = project(
        kernel_place, x, attend_own, attend_other, nh, cols
    )
    context, logs = attend_forward(start_of, qkv, length)
    if not same:
        late = late_all
        both, per = 2 * own, 2 * model // PARTS
        expand_low = (
            late[:, : both * wide // 2]
            .reshape(count // 2, 2, wide // 2, both, model)
            .transpose(1, 2, 0, 3, 4)
            .reshape(2, wide // 2, PARTS // 2, per, model)
            .transpose(2, 0, 1, 3, 4)
            .reshape(PARTS, per * (wide // 2), model)
        )
        low = both * wide // 2
        rest = [
            expand_low,
            late[:, low : low + own_red].reshape(PARTS, hidden // PARTS, model),
            late[:, low + own_red : low + own_red + own].reshape(PARTS, per // 2, model),
            jnp.zeros((PARTS, 8, model), BF16),
        ]
        late_all = jnp.concatenate(rest, axis=1)
    late = (late_all,)
    hidden_states, middle, middle_low, activated, slope, branch = mlp_forward(
        late, context, x, cot, weight_rows, vec, hidden
    )

    def for_devices(keep, send, split):
        parts = [by_index(*both, kernel_groups, n == 1) for n, both in enumerate(zip(keep, send))]
        return by_slot(split(jnp.concatenate(parts, axis=1)), place, groups)

    def split_mid(parts):
        per = 2 * model // PARTS
        expand = (
            jnp.stack([parts[:, :per], parts[:, per + 32 :]], axis=1)
            .reshape(PARTS // 2, 2, 2, per, model)
            .transpose(1, 2, 0, 3, 4)
            .reshape(2, 2, count // 2, 2 * own, model)
            .transpose(2, 0, 1, 3, 4)
            .reshape(count, 4 * own, model)
        )
        output = parts[:, per : per + per // 2].reshape(count, own, model)
        return jnp.concatenate([expand, output], axis=1)

    red_keep, red_send = reduce_weight_grad(kernel_place, activated, branch)
    if same:
        cot, *red_send = ordered(cot, *red_send)
        red = Halves(red_keep, red_send, groups)
    grad_pre, grad_middle, grad_attn, grad_context, mid_sums = mlp_backward(
        late, cot, weight_rows, middle, slope, vec
    )
    if same:
        grad_pre, *terms = ordered(grad_pre, *red.flat())
        red.set(terms)
        grad_pre, *sends = ordered(grad_pre, *red.sends())
        red_received = red.receive(sends)

    mid_keep, mid_send = mid_weight_grad(
        kernel_place, middle_low, grad_pre, context, grad_attn
    )
    if same:
        grad_context, *terms = ordered(grad_context, *mid_send, *red_received)
        mid = Halves(mid_keep, terms[:2], groups)
        red.add(terms[2:])
        grad_context, *sends = ordered(grad_context, *red.sends())
        red_received = red.receive(sends)

    pairs = model // (2 * HEAD_DIM)
    operands = (start_of, qkv, context, grad_context, logs, length)
    d_qkv = attend_backward(*operands, 0, pairs // 2)
    if same:
        d_qkv, *terms = ordered(d_qkv, *mid.flat(), *red_received)
        mid.set(terms[:4])
        red.add(terms[4:])
        d_qkv, *sends = ordered(d_qkv, *mid.sends(), *red.last_sends())
        mid_received = mid.receive(sends[:2])
        red_received = red.last_receive(sends[2:])
    d_qkv = attend_backward(*operands, pairs // 2, rows * pairs, d_qkv)
    if same:
        d_qkv, *terms = ordered(d_qkv, *mid_received, *red_received)
        mid.add(terms[:2])
        red_received = terms[2:]
        d_qkv, *sends = ordered(d_qkv, *mid.sends())
        mid_received = mid.receive(sends)
    att_keep, att_send = attend_weight_grad(kernel_place, normed_low, d_qkv, nh)
    if same:
        att_send, *mid_received = ordered(att_send, *mid_received)
        att = Whole(att_keep, att_send, groups)
        mid.add(mid_received)
        d_qkv, *terms = ordered(d_qkv, *mid.last_sends(), *att.terms)
        att.terms = terms[-2:]
        mid_received = mid.last_receive(terms[:-2])
        d_qkv, *sends = ordered(d_qkv, *att.sends())
        att_received = att.receive(sends)
    grad_input, sums = input_grad(d_qkv, x, grad_middle, attend_low, vec, mid_sums)
    if same:
        sums, *terms = ordered(sums, *att_received, *mid_received)
        att.terms = att.terms + terms[:3]
        att_received = att.last_receive(att.last_sends())
        red_grad, found = red.finish(red_received), mid.finish(terms[3:])
        per = 2 * own
        mid = jnp.concatenate(
            [found[:per], found[per + 32 :], found[per : per + own]], axis=0
        )
    else:
        red_parts = for_devices(
            red_keep, red_send, lambda parts: parts.reshape(count, own_red, model)
        )
        mid_parts = for_devices(mid_keep, mid_send, split_mid)
        att_parts = for_devices(
            [att_keep], [att_send], lambda parts: join_parts(parts, nh).reshape(count, own_in, flat)
        )
        red_grad, mid = scatter(*red_parts, groups), scatter(*mid_parts, groups)
        att_grad = scatter(*att_parts, groups)
    out_grad = mid[4 * own : 5 * own]
    exp_both = mid[: 4 * own].reshape(2, 2, own, model)
    kept = jnp.where(core == 0, exp_both[:, 0], exp_both[:, 1])
    beside = swap(jnp.where(core == 0, exp_both[:, 1], exp_both[:, 0]), 1)
    exp_grad = jnp.stack(
        [jnp.where(core == 0, kept, beside), jnp.where(core == 0, beside, kept)]
    ).reshape(wide, own, model)
    exp_grad = exp_grad.transpose(1, 0, 2).reshape(own, hidden)


    sums = all_sum(sums, groups[:2])
    if same:
        sums, *att_received = ordered(sums, *att_received)
    vector_grad = all_sum(sums, groups[2:])
    late_weights = (output_weight, expand_weight, reduce_weight)
    late_states = [
        (grad, first, second, weight)
        for grad, first, second, weight in zip(
            (out_grad, exp_grad, red_grad),
            (first_output, first_expand, first_reduce),
            (second_output, second_expand, second_reduce),
            late_weights,
        )
    ]
    late_found, late_sums = adapt(late_states, [1, 2, 3])
    if same:
        late_sums, *att_received = ordered(late_sums, *att_received)
        att_grad = att.finish(att_received)

    def planes(state):
        return state.transpose(1, 0, 2)

    vector_grad = lax.dynamic_slice_in_dim(vector_grad, place * own, own, 1)
    found, sums = adapt(
        [
            (att_grad, planes(first_attend), planes(second_attend), planes(attend_weight)),
            (vector_grad, first_vectors.T, second_vectors.T, vectors.T),
        ],
        [0, 4],
        late_sums,
    )
    sums = all_sum(sums, groups)
    adapted = [list(found[0]), *late_found, [a.T for a in found[1]]]
    *masters, trust_norms = master(
        sums,
        [found[0][2], *[a[2] for a in late_found], found[1][2]],
        [planes(attend_weight), *late_weights, vectors.T],
    )
    masters[4] = masters[4].T
    adapted[0] = [planes(a) for a in adapted[0]]
    masters[0] = planes(masters[0])
    return (
        hidden_states.reshape(rows, length, model),
        grad_input.reshape(rows, length, model),
        *[a[0] for a in adapted],
        *[a[1] for a in adapted],
        *masters,
        trust_norms,
    )


def solution(mesh):
    rows = P(AXES, None, None)
    state = [P("batch", None, "head")] + [P(AXES, None)] * 4
    return jax.shard_map(
        shards,
        mesh=mesh,
        in_specs=(rows, rows, P("batch", None), P("batch", None), P(AXES, None), *state * 3),
        out_specs=(rows, rows, *state * 3, P()),
        check_vma=False,
    )
```

```python
import jax
import jax.numpy as jnp
from jax import lax
from jax.experimental import pallas as pl
from jax.experimental.pallas import tpu as pltpu
from jax.sharding import PartitionSpec as P

HEAD_DIM = 64
THOUGHT_TOKENS = 8
STEP = 6
PARTS = 32
SPAN = 256
BLOCK = 128

NORM_EPS = 1e-05
NEGATIVE = -1e30
BETA = 0.5
RATE = 0.5
DECAY = 0.01
ADAM_EPS = 1e-06
AXES = ("batch", "head")
ROOT = 0.7978845608028654
CUBE = 0.044715
F32 = jnp.float32
BF16 = jnp.bfloat16
NT = (((1,), (1,)), ((), ()))
TN = (((0,), (0,)), ((), ()))


def dot(a, b, dims=(((1,), (0,)), ((), ()))):
    return lax.dot_general(a, b, dims, preferred_element_type=F32)


def params(grid=1, vmem=60):
    return pltpu.CompilerParams(
        dimension_semantics=("arbitrary",) * grid, vmem_limit_bytes=vmem * 1024 * 1024
    )


def cost(micros):
    return pl.CostEstimate(flops=int(micros * 0.29e9), bytes_accessed=1 << 18, transcendentals=0)


def whole(shape):
    return pl.BlockSpec(shape, lambda *_: (0,) * len(shape), pipeline_mode=pl.Buffered(1))


SCALARS = pl.BlockSpec(memory_space=pltpu.SMEM)


def row_facts(lengths, counts, mask, span):
    positions = jnp.arange(span, dtype=jnp.int32)
    ends = jnp.cumsum(lengths, axis=-1)
    starts = ends - lengths
    inside = (positions[None, :, None] >= starts[:, None, :]) & (
        positions[None, :, None] < ends[:, None, :]
    )
    start_of = jnp.sum(jnp.where(inside, starts[:, None, :], 0), axis=-1)
    passes = jnp.sum(jnp.where(inside, counts[:, None, :], 0), axis=-1)
    keep = (positions[None, :] - start_of >= THOUGHT_TOKENS * passes) & (mask > 0)
    return start_of, keep.astype(F32)


def windows(length):
    return [
        (low, max(0, low - SPAN), low + BLOCK - max(0, low - SPAN)) for low in range(0, length, BLOCK)
    ]


def fill_caps(start_ref, cap_ref, length):
    for number, (low, first, count) in enumerate(windows(length)):
        key = lax.broadcasted_iota(jnp.int32, (count, BLOCK), 0) + first
        query = lax.broadcasted_iota(jnp.int32, (count, BLOCK), 1) + low
        start = start_ref[0, :, low : low + BLOCK]
        allowed = (key <= query) & (key >= start)
        cap_ref[number, :count] = jnp.where(allowed, 3e38, NEGATIVE)


def cap_of(cap_ref, number, count):
    cap = cap_ref[number, :count]
    return jnp.concatenate([cap, cap], axis=1)


def for_heads(values):
    lane = lax.broadcasted_iota(jnp.int32, (1, 2 * HEAD_DIM), 1)
    return jnp.concatenate(
        [jnp.where(lane < HEAD_DIM, values, 0), jnp.where(lane >= HEAD_DIM, values, 0)], axis=0
    )


def of_heads(values):
    return jnp.concatenate([values[:HEAD_DIM, :BLOCK], values[HEAD_DIM:, BLOCK:]], axis=0)


def in_stages(units, ahead, behind, first, middle, last):
    started, worked = [first(unit) for unit in units[:ahead]], []
    for number, unit in enumerate(units):
        if number + ahead < len(units):
            started.append(first(units[number + ahead]))
        worked.append((unit, middle(unit, started.pop(0))))
        if len(worked) > behind:
            last(*worked.pop(0))
    for both in worked:
        last(*both)


def attend_forward_kernel(fresh, start_ref, q_ref, k_ref, v_ref, o_ref, p_ref, cap_ref):
    length = q_ref.shape[0]
    pl.when(fresh)(lambda: fill_caps(start_ref, cap_ref, length))
    value_t = v_ref[...].T

    def score(unit):
        _, (low, first, count) = unit
        query = for_heads(q_ref[low : low + BLOCK, :] * (HEAD_DIM**-0.5))
        return dot(k_ref[first : first + count, :], query, NT)

    def soften(unit, scores):
        number, (_, _, count) = unit
        scores = jnp.minimum(scores, cap_of(cap_ref, number, count))
        grown = jnp.exp(scores - jnp.max(scores, axis=0, keepdims=True))
        probs = (grown * (1.0 / total(grown))).astype(BF16)
        p_ref[0, 0, number, :count] = probs
        return probs

    def mix(unit, probs):
        _, (low, first, count) = unit
        result = dot(value_t[:, first : first + count], probs)
        o_ref[low : low + BLOCK, :] = of_heads(result).T.astype(BF16)

    in_stages(list(enumerate(windows(length))), 4, 1, score, soften, mix)


def attend_backward_kernel(q_ref, k_ref, v_ref, o_ref, do_ref, p_ref, *rest):
    d_ref = rest[-1]
    length = q_ref.shape[0]
    key_t = k_ref[...].T
    grad_key, grad_value = {}, {}

    def query_of(low):
        return for_heads(q_ref[low : low + BLOCK, :] * (HEAD_DIM**-0.5))

    def grad_of(low):
        return for_heads(do_ref[low : low + BLOCK, :])

    def score(unit):
        _, (low, first, count) = unit
        return dot(v_ref[first : first + count, :], grad_of(low), NT)

    def soften(unit, grad_probs):
        number, (low, _, count) = unit
        product = do_ref[low : low + BLOCK, :].astype(F32) * o_ref[low : low + BLOCK, :].astype(F32)
        product = product.T
        inner = jnp.concatenate([total(product[:HEAD_DIM]), total(product[HEAD_DIM:])], axis=1)
        probs = p_ref[0, 0, number, :count]
        return probs, (probs.astype(F32) * (grad_probs - inner)).astype(BF16)

    def mix(unit, found):
        _, (low, first, count) = unit
        probs, grad_scores = found
        terms = dot(probs, grad_of(low)), dot(grad_scores, query_of(low))
        grad_query = dot(key_t[:, first : first + count], grad_scores)
        d_ref[0, low : low + BLOCK, :] = (of_heads(grad_query).T * (HEAD_DIM**-0.5)).astype(BF16)
        for sums, term, place in ((grad_value, terms[0], 2), (grad_key, terms[1], 1)):
            for at in range(first, first + count, BLOCK):
                one = term[at - first : at - first + BLOCK]
                sums[at] = sums[at] + one if at in sums else one
            for at in list(sums):
                if at <= low - SPAN or low + BLOCK == length:
                    d_ref[place, at : at + BLOCK, :] = sums.pop(at).astype(BF16)

    in_stages(list(enumerate(windows(length))), 2, 0, score, soften, mix)


def attention_specs(length, pairs, low=0):
    pair = 2 * HEAD_DIM

    def at(i):
        return (i + low) // pairs, (i + low) % pairs

    def columns(n):
        return lambda i: (at(i)[0], n * pairs + at(i)[1])

    qkv = [pl.BlockSpec((length, pair), columns(n)) for n in range(3)]
    rows = pl.BlockSpec((length, pair), columns(0))
    probs = pl.BlockSpec((1, 1) + probs_shape(length), lambda i: (*at(i), 0, 0, 0))
    start = pl.BlockSpec((1, 1, length), lambda i: (at(i)[0], 0, 0))
    return start, qkv, rows, probs, lambda i: (0, *at(i))


def probs_shape(length):
    return (length // BLOCK, SPAN + BLOCK, 2 * BLOCK)


def attend_forward(start, qkv, length):
    tokens, model = qkv.shape[0], qkv.shape[1] // 3
    pairs = model // (2 * HEAD_DIM)
    rows = tokens // length
    start_spec, qkv_specs, row_spec, probs_spec, _ = attention_specs(length, pairs)

    def kernel(*refs):
        attend_forward_kernel(pl.program_id(0) % pairs == 0, *refs)

    return pl.pallas_call(
        kernel,
        grid=(rows * pairs,),
        in_specs=[start_spec] + qkv_specs,
        out_specs=[row_spec, probs_spec],
        out_shape=[
            jax.ShapeDtypeStruct((tokens, model), BF16),
            jax.ShapeDtypeStruct((rows, pairs) + probs_shape(length), BF16),
        ],
        scratch_shapes=[pltpu.VMEM((length // BLOCK, SPAN + BLOCK, BLOCK), F32)],
        compiler_params=params(),
        cost_estimate=cost(18),
        name="attend_forward",
    )(start, qkv, qkv, qkv)


def attend_backward(qkv, out, grad, probs, length, low, high, before=None):
    tokens, model = out.shape
    pairs = model // (2 * HEAD_DIM)
    _, qkv_specs, row_spec, probs_spec, at = attention_specs(length, pairs, low)
    operands = [qkv, qkv, qkv, out, grad, probs]
    in_specs = qkv_specs + [row_spec, row_spec, probs_spec]
    aliases = {}
    if before is not None:
        aliases = {len(operands): 0}
        operands.append(before)
        in_specs.append(pl.BlockSpec(memory_space=pl.ANY))
    return pl.pallas_call(
        attend_backward_kernel,
        grid=(high - low,),
        in_specs=in_specs,
        out_specs=pl.BlockSpec((3, length, 2 * HEAD_DIM), at),
        out_shape=jax.ShapeDtypeStruct((3, tokens, model), BF16),
        input_output_aliases=aliases,
        compiler_params=params(),
        cost_estimate=cost(2.0 * (high - low)),
        name="attend_backward",
    )(*operands)


def normalize(values):
    centre = values - jnp.mean(values, axis=-1, keepdims=True)
    factor = lax.rsqrt(jnp.mean(centre * centre, axis=-1, keepdims=True) + NORM_EPS)
    return centre * factor, factor


def norm_back(inner, normed, factor):
    return factor * (
        inner
        - jnp.mean(inner, axis=-1, keepdims=True)
        - normed * jnp.mean(inner * normed, axis=-1, keepdims=True)
    )


def total(values):
    return jnp.sum(values, axis=0, keepdims=True)


def project_kernel(place_ref, x_ref, own_ref, other_ref, nl_ref, qkv_ref, w_ref, vec_ref, *, heads):
    slots, rows, flat = own_ref.shape
    rows -= -(-vec_ref.shape[0] // 16) * 16
    part, model = flat // 3, x_ref.shape[1]
    groups = bit_groups(2 * slots)
    place = place_ref[0]

    @pl.when(pl.program_id(0) == 0)
    def _():
        for here in range(heads):

            @pl.when(place % heads == here)
            def _(here=here):
                for bit, ref in enumerate((own_ref, other_ref)):
                    for slot in range(slots):
                        mask = mask_of(slot, groups) | bit
                        head = here ^ (mask % heads)
                        row = pl.multiple_of(((place ^ mask) // heads) * rows, rows)
                        for j in range(3):
                            low = j * model + head * part
                            w_ref[pl.ds(row, rows), low : low + part] = ref[
                                slot, :rows, j * part : (j + 1) * part
                            ]

        count, each = vec_ref.shape[0], model // (2 * slots)
        lane = lax.broadcasted_iota(jnp.int32, (1, model), 1)
        found = jnp.zeros((count, model), F32)
        for bit, ref in enumerate((own_ref, other_ref)):
            for slot in range(slots):
                device = place ^ (mask_of(slot, groups) | bit)
                piece = ref[slot, rows:, :128].astype(F32)[:count]
                piece = jnp.concatenate([piece] * (model // 128), axis=1)
                piece = pltpu.roll(piece, (device * each) % 128, 1)
                inside = (lane >= device * each) & (lane < (device + 1) * each)
                found = jnp.where(inside, piece, found)
        vec_ref[...] = found

    normed, _ = normalize(x_ref[...].astype(F32))
    low = (normed * vec_ref[0:1, :] + vec_ref[1:2, :]).astype(BF16)
    nl_ref[...] = low
    for j in range(3):
        side = slice(j * model, (j + 1) * model)
        result = dot(low, w_ref[:, side])
        if j != 1:
            result = result + vec_ref[2 + j // 2 : 3 + j // 2, :]
        qkv_ref[:, side] = result.astype(BF16)


def project(place, x, own, other, heads, cols, tile=512):
    tokens, model = x.shape
    row = pl.BlockSpec((tile, model), lambda i: (i, 0))
    return pl.pallas_call(
        lambda *refs: project_kernel(*refs, heads=heads),
        grid=(tokens // tile,),
        in_specs=[SCALARS, row, whole(own.shape), whole(other.shape)],
        out_specs=[
            row,
            pl.BlockSpec((tile, 3 * model), lambda i: (i, 0)),
            pl.BlockSpec((model, 3 * model), lambda i: (0, 0)),
            pl.BlockSpec((cols, model), lambda i: (0, 0)),
        ],
        out_shape=[
            jax.ShapeDtypeStruct((tokens, model), BF16),
            jax.ShapeDtypeStruct((tokens, 3 * model), BF16),
            jax.ShapeDtypeStruct((model, 3 * model), BF16),
            jax.ShapeDtypeStruct((cols, model), F32),
        ],
        compiler_params=params(),
        cost_estimate=cost(14),
        name="project",
    )(place, x, own, other)


class Late:
    def __init__(self, refs, scratch):
        (self.parts,) = refs
        self.expand, self.reduce, self.output, self.stage, self.sem = scratch
        self.model = self.output.shape[1]
        self.chunks = self.expand.shape[0]

    def copies(self):
        per = self.model // self.stage.shape[1]
        red = self.reduce.shape[0] // (2 * self.stage.shape[1])
        end = 2 * per + red
        for device in range(self.parts.shape[0]):
            row, bit = (device // 2) * per, device % 2
            for n in range(2):
                yield (
                    self.parts.at[device, n * per : (n + 1) * per],
                    self.expand.at[2 * bit + n, row : row + per],
                )
            yield (
                self.parts.at[device, 2 * per : end],
                self.reduce.at[device * red : (device + 1) * red],
            )
            yield (
                self.parts.at[device, end : end + self.stage.shape[2]],
                self.stage.at[bit, device // 2],
            )

    def load(self):
        copies = [pltpu.make_async_copy(a, b, self.sem) for a, b in self.copies()]
        for copy in copies:
            copy.start()
        for copy in copies:
            copy.wait()
        slots = self.stage.shape[1]
        per = self.model // slots
        for n in range(slots):
            both = [self.stage[bit, n, : per // 2, :].astype(F32) for bit in range(2)]
            self.output[n * per : (n + 1) * per, :] = jnp.concatenate(both, axis=0).astype(BF16)

    def reduce_rows(self, c):
        return self.reduce[c * self.model : (c + 1) * self.model, :]

    @staticmethod
    def specs():
        return [pl.BlockSpec(memory_space=pl.ANY)]

    @staticmethod
    def scratch(late, hidden):
        slots, _, model = late[0].shape
        slots //= 2
        return [
            pltpu.VMEM((hidden // model, model, model), BF16),
            pltpu.VMEM((hidden, model), BF16),
            pltpu.VMEM((model, model), BF16),
            pltpu.VMEM((2, slots, 32, model), BF16),
            pltpu.SemaphoreType.DMA,
        ]


def mlp_forward_kernel(*refs):
    late = Late(refs[:-16], refs[-5:])
    ctx_ref, x_ref, cot_ref, wt_ref, vec_ref = refs[-16:-11]
    hid_ref, mid_ref, nm_ref, act_ref, dg_ref, gb_ref = refs[-11:-5]
    model = late.model
    pl.when(pl.program_id(0) == 0)(late.load)
    middle = x_ref[...].astype(F32) + dot(ctx_ref[...], late.output[...]) + vec_ref[4:5, :]
    mid_ref[...] = middle
    gb_ref[...] = (cot_ref[...].astype(F32) * wt_ref[...]).astype(BF16)
    normed, _ = normalize(middle)
    low = (normed * vec_ref[5:6, :] + vec_ref[6:7, :]).astype(BF16)
    nm_ref[...] = low
    result = middle + vec_ref[7:8, :]
    for c in range(late.chunks):
        side = slice(c * model, (c + 1) * model)
        pre = dot(low, late.expand[c]) + vec_ref[8 + c : 9 + c, :]
        square = pre * pre
        half = 0.5 + 0.5 * jnp.tanh(pre * (ROOT + (ROOT * CUBE) * square))
        act = pre * half
        dg = half + act * (1.0 - half) * (2.0 * ROOT + (6.0 * ROOT * CUBE) * square)
        dg_ref[:, side] = dg.astype(BF16)
        act = act.astype(BF16)
        act_ref[:, side] = act
        result = result + dot(act, late.reduce_rows(c))
    hid_ref[...] = result.astype(BF16)


def mlp_forward(late, ctx, x, cot, wt, vec, hidden, tile=256):
    tokens, model = x.shape
    row = pl.BlockSpec((tile, model), lambda i: (i, 0))
    wide = pl.BlockSpec((tile, hidden), lambda i: (i, 0))
    one = pl.BlockSpec((tile, 1), lambda i: (i, 0))

    def shape(width, kind=BF16):
        return jax.ShapeDtypeStruct((tokens, width), kind)

    return pl.pallas_call(
        mlp_forward_kernel,
        grid=(tokens // tile,),
        in_specs=Late.specs() + [row, row, row, one, whole(vec.shape)],
        out_specs=[row, row, row, wide, wide, row],
        out_shape=[
            shape(model), shape(model, F32), shape(model), shape(hidden), shape(hidden), shape(model),
        ],
        scratch_shapes=Late.scratch(late, hidden),
        compiler_params=params(),
        cost_estimate=cost(40),
        name="mlp_forward",
    )(*late, ctx, x, cot, wt, vec)


def mlp_backward_kernel(*refs):
    late = Late(refs[:-15], refs[-5:])
    cot_ref, wt_ref, mid_ref, dg_ref, vec_ref = refs[-15:-10]
    gpre_ref, gm_ref, ga_ref, gc_ref, sum_ref = refs[-10:-5]
    model = late.model

    @pl.when(pl.program_id(0) == 0)
    def _():
        late.load()
        sum_ref[...] = jnp.zeros_like(sum_ref)

    grad_out = cot_ref[...].astype(F32) * wt_ref[...]
    branch = grad_out.astype(BF16)
    sum_ref[3:4, :] += total(branch.astype(F32))
    back = None
    for c in range(late.chunks):
        side = slice(c * model, (c + 1) * model)
        grad = (dot(branch, late.reduce_rows(c), NT) * dg_ref[:, side].astype(F32)).astype(BF16)
        gpre_ref[:, side] = grad
        sum_ref[4 + c : 5 + c, :] += total(grad.astype(F32))
        term = dot(grad, late.expand[c], NT)
        back = term if back is None else back + term
    normed, factor = normalize(mid_ref[...])
    sum_ref[1:2, :] += total(back * normed)
    sum_ref[2:3, :] += total(back)
    grad_middle = grad_out + norm_back(back * vec_ref[5:6, :], normed, factor)
    gm_ref[...] = grad_middle
    low = grad_middle.astype(BF16)
    ga_ref[...] = low
    sum_ref[0:1, :] += total(low.astype(F32))
    gc_ref[...] = dot(low, late.output[...], NT).astype(BF16)


def mlp_backward(late, cot, wt, mid, dg, vec, tile=256):
    tokens, model = cot.shape
    hidden = dg.shape[1]
    row = pl.BlockSpec((tile, model), lambda i: (i, 0))
    wide = pl.BlockSpec((tile, hidden), lambda i: (i, 0))
    one = pl.BlockSpec((tile, 1), lambda i: (i, 0))

    def shape(width, kind=BF16):
        return jax.ShapeDtypeStruct((tokens, width), kind)

    return pl.pallas_call(
        mlp_backward_kernel,
        grid=(tokens // tile,),
        in_specs=Late.specs() + [row, one, row, wide, whole(vec.shape)],
        out_specs=[wide, row, row, row, pl.BlockSpec((8, model), lambda i: (0, 0))],
        out_shape=[
            shape(hidden), shape(model, F32), shape(model), shape(model),
            jax.ShapeDtypeStruct((8, model), F32),
        ],
        scratch_shapes=Late.scratch(late, hidden),
        compiler_params=params(),
        cost_estimate=cost(36),
        name="mlp_backward",
    )(*late, cot, wt, mid, dg, vec)


def put_parts(place, outs, pieces, turn=False):
    groups = bit_groups(2 * outs[0].shape[0])
    for bit in range(2):

        @pl.when(place % 2 == bit)
        def _(bit=bit):
            for device, index, value in pieces:
                mask = place ^ device
                slot = slot_of(turned(mask, groups) if turn else mask, groups)
                outs[(device % 2) ^ bit][(slot,) + index] = value


def reduce_weight_grad_kernel(place_ref, a_ref, b_ref, *outs):
    slots, rows, _ = outs[0].shape
    result = dot(a_ref[...], b_ref[...], TN).astype(BF16)
    count = result.shape[0] // (2 * rows)
    for step in range(2 * slots // count):

        @pl.when(pl.program_id(0) == step)
        def _(step=step):
            for half in range(2):
                put_parts(
                    place_ref[0],
                    outs[half::2],
                    [
                        (
                            step * count + n,
                            (),
                            result[(2 * n + half) * rows : (2 * n + half + 1) * rows],
                        )
                        for n in range(count)
                    ],
                    half == 1,
                )


def outs_of(*shapes):
    return dict(
        out_specs=[pl.BlockSpec(shape, lambda *_: (0,) * len(shape)) for shape in shapes],
        out_shape=[jax.ShapeDtypeStruct(shape, BF16) for shape in shapes],
    )


def reduce_weight_grad(place, act, branch):
    tokens, model = branch.shape
    hidden = act.shape[1]
    shape = (PARTS // 2, hidden // PARTS // 2, model)
    found = pl.pallas_call(
        reduce_weight_grad_kernel,
        grid=(hidden // model,),
        in_specs=[SCALARS, pl.BlockSpec((tokens, model), lambda i: (0, i)), whole(branch.shape)],
        **outs_of(*[shape] * 4),
        compiler_params=params(),
        cost_estimate=cost(15),
        name="reduce_weight_grad",
    )(place, act, branch)
    return found[:2], found[2:]


def mid_weight_grad_kernel(place_ref, nm_ref, gpre_ref, ctx_hbm, ga_hbm, *outs):
    *outs, ctx_ref, ga_ref, sems = outs
    copies = [
        pltpu.make_async_copy(ctx_hbm, ctx_ref, sems.at[0]),
        pltpu.make_async_copy(ga_hbm, ga_ref, sems.at[1]),
    ]
    slots, rows, model = outs[0].shape
    per = model // slots
    step = pl.program_id(0)
    last = pl.num_programs(0) - 1
    place = place_ref[0]

    @pl.when(step == 1)
    def _():
        for copy in copies:
            copy.start()

    for c in range(4):

        @pl.when(step == c)
        def _(c=c):
            result = dot(nm_ref[...], gpre_ref[...], TN).astype(BF16)
            put_parts(
                place,
                outs[c % 2 :: 2],
                [
                    (2 * n + c // 2, (slice(0, per),), result[n * per : (n + 1) * per])
                    for n in range(slots)
                ],
                c % 2 == 1,
            )

    @pl.when(step == last)
    def _():
        for copy in copies:
            copy.wait()
        result = dot(ctx_ref[...], ga_ref[...], TN)
        half = per // 2
        empty = jnp.zeros((rows - per - half, model), F32)
        put_parts(
            place,
            outs[::2],
            [
                (
                    n,
                    (slice(per, rows),),
                    jnp.concatenate([result[n * half : (n + 1) * half], empty], axis=0).astype(BF16),
                )
                for n in range(2 * slots)
            ],
        )


def mid_weight_grad(place, nm, gpre, ctx, ga):
    tokens, model = nm.shape
    hidden = gpre.shape[1]
    assert hidden == 4 * model
    slots, per = PARTS // 2, 2 * model // PARTS
    shapes = [(slots, per + 32, model), (slots, per, model)]
    found = pl.pallas_call(
        mid_weight_grad_kernel,
        grid=(5,),
        in_specs=[
            SCALARS,
            whole(nm.shape),
            pl.BlockSpec((tokens, model), lambda i: (0, jnp.minimum(i, 3))),
            pl.BlockSpec(memory_space=pl.ANY),
            pl.BlockSpec(memory_space=pl.ANY),
        ],
        **outs_of(*shapes * 2),
        scratch_shapes=[
            pltpu.VMEM(ctx.shape, BF16),
            pltpu.VMEM(ga.shape, BF16),
            pltpu.SemaphoreType.DMA((2,)),
        ],
        compiler_params=params(),
        cost_estimate=cost(19),
        name="mid_weight_grad",
    )(place, nm, gpre, ctx, ga)
    return found[:2], found[2:]


def attend_weight_grad_kernel(place_ref, a_ref, b_ref, keep_ref, send_ref, *, heads):
    slots, rows, flat = keep_ref.shape
    part = flat // 3
    result = dot(a_ref[...], b_ref[0], TN).astype(BF16)
    for j in range(3):

        @pl.when(pl.program_id(0) == j)
        def _(j=j):
            put_parts(
                place_ref[0],
                (keep_ref, send_ref),
                [
                    (
                        d,
                        (slice(None), slice(j * part, (j + 1) * part)),
                        result[
                            d // heads * rows : (d // heads + 1) * rows,
                            d % heads * part : (d % heads + 1) * part,
                        ],
                    )
                    for d in range(2 * slots)
                ],
            )


def attend_weight_grad(place, nl, d_qkv, heads):
    tokens, model = nl.shape
    return pl.pallas_call(
        lambda *refs: attend_weight_grad_kernel(*refs, heads=heads),
        grid=(3,),
        in_specs=[SCALARS, whole(nl.shape), pl.BlockSpec((1, tokens, model), lambda j: (j, 0, 0))],
        **outs_of(*[(PARTS // 2, model * heads // PARTS, 3 * model // heads)] * 2),
        compiler_params=params(),
        cost_estimate=cost(13),
        name="attend_weight_grad",
    )(place, nl, d_qkv)


def input_grad_kernel(d_ref, x_ref, gm_ref, w_ref, vec_ref, mid_ref, out_ref, sum_ref, part_ref):
    model = x_ref.shape[1]

    @pl.when(pl.program_id(0) == 0)
    def _():
        sum_ref[:4, :] = jnp.zeros((4, model), F32)
        sum_ref[4:, :] = mid_ref[...]

    back = None
    for j in range(3):
        term = dot(d_ref[j], w_ref[:, j * model : (j + 1) * model], NT)
        back = term if back is None else back + term
    normed, factor = normalize(x_ref[...].astype(F32))
    sum_ref[0:1, :] += total(back * normed)
    sum_ref[1:2, :] += total(back)
    sum_ref[2:3, :] += total(d_ref[0].astype(F32))
    sum_ref[3:4, :] += total(d_ref[2].astype(F32))
    out_ref[...] = (gm_ref[...] + norm_back(back * vec_ref[0:1, :], normed, factor)).astype(BF16)

    @pl.when(pl.program_id(0) == pl.num_programs(0) - 1)
    def _():
        count = part_ref.shape[0]
        each = model // count
        part_ref[...] = jnp.zeros_like(part_ref)
        for n in range(count):
            part_ref[n, : sum_ref.shape[0], :each] = sum_ref[:, n * each : (n + 1) * each]


def input_grad(d_qkv, x, gm, w, vec, mid_sums, tile=512):
    tokens, model = x.shape
    row = pl.BlockSpec((tile, model), lambda i: (i, 0))
    return pl.pallas_call(
        input_grad_kernel,
        grid=(tokens // tile,),
        in_specs=[
            pl.BlockSpec((3, tile, model), lambda i: (0, i, 0)), row, row,
            whole(w.shape), whole(vec.shape), whole(mid_sums.shape),
        ],
        out_specs=[
            row,
            pl.BlockSpec(vec.shape, lambda i: (0, 0)),
            pl.BlockSpec((PARTS, 16, 128), lambda i: (0, 0, 0)),
        ],
        out_shape=[
            jax.ShapeDtypeStruct((tokens, model), BF16),
            jax.ShapeDtypeStruct(vec.shape, F32),
            jax.ShapeDtypeStruct((PARTS, 16, 128), F32),
        ],
        compiler_params=params(),
        cost_estimate=cost(16),
        name="input_grad",
    )(d_qkv, x, gm, w, vec, mid_sums)


def bit_groups(count):
    bits = count.bit_length() - 1
    assert count == 1 << bits
    return [(0, 1)] + [(low, min(2, bits - low)) for low in range(1, bits, 2)]


def slot_of(mask, groups):
    slot = 0
    for low, width in groups[1:]:
        slot = slot * (1 << width) + ((mask >> low) & ((1 << width) - 1))
    return slot


def mask_of(slot, groups):
    mask = 0
    for low, width in groups[:0:-1]:
        mask |= (slot & ((1 << width) - 1)) << low
        slot >>= width
    return mask


def swap(value, mask):
    count = lax.axis_size("batch") * lax.axis_size("head")
    return lax.ppermute(value, AXES, [(i, i ^ mask) for i in range(count)])


def spread(piece, group):
    low, width = group
    return [piece] + [swap(piece, step << low) for step in range(1, 1 << width)]


def join(parts):
    return jnp.concatenate(parts, axis=0)


def gather_far(piece, groups):
    piece = piece[None]
    for group in groups[:1:-1]:
        piece = join(spread(piece, group))
    return piece


def ordered(*values):
    return lax.optimization_barrier(values)


class Halves:
    def __init__(self, keep, send, groups):
        self.groups = groups
        self.bits = [2 << groups[1][0], 1 << groups[1][0]]
        self.terms = [[kept, swap(sent, 1)] for kept, sent in zip(keep, send)]
        self.count = keep[0].shape[0]

    def flat(self):
        return [t for terms in self.terms for t in terms]

    def set(self, flat):
        count = len(self.terms[0])
        self.terms = [list(flat[:count]), list(flat[count:])]

    def sends(self):
        self.count //= 2
        here = slice(self.count, 2 * self.count)
        return [added([t[here] for t in terms]).astype(BF16) for terms in self.terms]

    def receive(self, sends):
        received = [swap(send, bit) for send, bit in zip(sends, self.bits)]
        self.bits = self.bits[::-1]
        return received

    def add(self, received):
        self.terms = [terms + [one] for terms, one in zip(self.terms, received)]

    def at(self, slot):
        return jnp.concatenate([added([t[slot] for t in terms]) for terms in self.terms], axis=0)

    def last_sends(self):
        return [self.at(slot).astype(BF16) for slot in range(1, self.count)]

    def last_receive(self, sends):
        return [swap(send, (n + 1) << self.groups[2][0]) for n, send in enumerate(sends)]

    def finish(self, received):
        return added([self.at(0), *received])


class Whole:
    def __init__(self, keep, send, groups):
        self.groups = groups
        self.terms = [keep, swap(send, 1)]
        self.count = keep.shape[0]

    def sends(self):
        self.count //= 4
        return [
            added([t[n * self.count : (n + 1) * self.count] for t in self.terms]).astype(BF16)
            for n in range(1, 4)
        ]

    def receive(self, sends):
        return [swap(send, (n + 1) << self.groups[1][0]) for n, send in enumerate(sends)]

    def last_sends(self):
        return [added([t[n] for t in self.terms]).astype(BF16) for n in range(1, self.count)]

    def last_receive(self, sends):
        return [swap(send, (n + 1) << self.groups[2][0]) for n, send in enumerate(sends)]

    def finish(self, received):
        return added([added([t[0] for t in self.terms]), *received])


def added(terms):
    return sum(term.astype(F32) for term in terms)


def scatter(keep, send, groups):
    terms = [keep, swap(send, 1)]
    for low, width in groups[1:]:
        count = 1 << width
        terms = [t.reshape((count, -1) + t.shape[1:]) for t in terms]
        sends = [added([t[step] for t in terms]).astype(BF16) for step in range(1, count)]
        terms = [added([t[0] for t in terms])]
        terms += [swap(send, (n + 1) << low) for n, send in enumerate(sends)]
    return added(terms)[0]


def all_sum(value, groups):
    for low, width in groups:
        value = sum([swap(value, s << low) for s in range(1, 1 << width)], value)
    return value


def turned(mask, groups):
    low = groups[1][0]
    both = (mask >> low) & 3
    return mask ^ ((both ^ (both >> 1) ^ ((both & 1) << 1)) << low)


def slot_masks(groups, turn=False):
    masks = [mask_of(slot, groups) for slot in range(1 << sum(width for _, width in groups[1:]))]
    return [turned(mask, groups) for mask in masks] if turn else masks


def in_order(parts, masks, place):
    found = [mask for part in masks for mask in part]
    slots = [0] * len(found)
    for slot, mask in enumerate(found):
        slots[mask] = slot
    devices = jnp.arange(len(found), dtype=jnp.int32)
    return jnp.take(join(parts), jnp.asarray(slots, jnp.int32)[place ^ devices], axis=0)


def by_slot(parts, place, groups):
    masks = jnp.asarray(slot_masks(groups), jnp.int32)
    return [jnp.take(parts, place ^ (masks | bit), axis=0) for bit in range(2)]


def adapt_kernel(rows, copies, *refs):
    count = len(rows)
    inputs, outputs = refs[: 4 * count + 1], refs[4 * count + 1 :]
    sum_ref = outputs[3 * count]
    sum_ref[...] = inputs[-1][...]
    half = sum_ref.shape[0] // 2
    correct = 1.0 - BETA**STEP
    for number, row in enumerate(rows):
        grad_ref, first_ref, second_ref, weight_ref = inputs[4 * number : 4 * number + 4]
        moment_ref, square_ref, update_ref = outputs[3 * number : 3 * number + 3]
        planes = weight_ref.shape[0] if len(weight_ref.shape) == 3 else 1
        width = weight_ref.shape[-1]
        norms = []
        for n in range(planes):
            at = n if len(weight_ref.shape) == 3 else Ellipsis
            if len(grad_ref.shape) == 3:
                grad = jnp.sum(grad_ref[...], axis=0)[: weight_ref.shape[0], :width]
            else:
                grad = grad_ref[:, n * width : (n + 1) * width]
            moment = BETA * first_ref[at] + (1.0 - BETA) * grad
            square = BETA * second_ref[at] + (1.0 - BETA) * grad * grad
            weight = weight_ref[at]
            update = moment / correct / (jnp.sqrt(square / correct) + ADAM_EPS) + DECAY * weight
            moment_ref[at] = moment
            square_ref[at] = square
            update_ref[at] = update
            norms.append([jnp.sum(v * v, axis=1, keepdims=True) for v in (weight, update)])
        for n in range(2):
            norm = sum(both[n] for both in norms)
            if row < 4:
                norm = total(norm)
            place = n * half + row
            sum_ref[place : place + norm.shape[0], :] = jnp.broadcast_to(norm, (norm.shape[0], 128))
    if copies:
        outputs[-1][...] = jnp.broadcast_to(diagonal(sum_ref[...]), outputs[-1].shape)


def diagonal(values):
    row = lax.broadcasted_iota(jnp.int32, values.shape, 0)
    lane = lax.broadcasted_iota(jnp.int32, values.shape, 1)
    return total(jnp.where(row == lane, values, 0.0))


def adapt(states, rows, sums=None, copies=0):
    if sums is None:
        sums = jnp.zeros((32, 128), F32)
    operands = [array for state in states for array in state] + [sums]
    shapes = [state[3].shape for state in states for _ in range(3)] + [sums.shape]
    if copies:
        shapes.append((copies, 8, 128))
    found = pl.pallas_call(
        lambda *refs: adapt_kernel(rows, copies, *refs),
        grid=(1,),
        in_specs=[whole(a.shape) for a in operands],
        out_specs=[pl.BlockSpec(s, lambda *_, n=len(s): (0,) * n) for s in shapes],
        out_shape=[jax.ShapeDtypeStruct(s, F32) for s in shapes],
        compiler_params=params(),
        cost_estimate=cost(4),
        name="adapt",
    )(*operands)
    return [found[3 * n : 3 * n + 3] for n in range(len(states))], found[-1]


def master_kernel(sum_ref, *refs):
    *refs, trust_ref = refs
    count = len(refs) // 3
    width = trust_ref.shape[1]
    if len(sum_ref.shape) == 3:
        line = jnp.sum(sum_ref[...], axis=0)[:1]
    else:
        line = diagonal(sum_ref[...])
    norms = [jnp.sqrt(line[:, n * width : (n + 1) * width]) for n in range(2)]
    ratio = norms[0] / (norms[1] + ADAM_EPS)
    for n, value in enumerate([*norms, ratio]):
        trust_ref[n : n + 1, :] = jnp.log(value)
    for n in range(count):
        update_ref, weight_ref, out_ref = refs[n], refs[count + n], refs[2 * count + n]
        if n < 4:
            scale = RATE * ratio[:, n : n + 1]
        else:
            shape = (weight_ref.shape[0], width)
            row = lax.broadcasted_iota(jnp.int32, shape, 0)
            lane = lax.broadcasted_iota(jnp.int32, shape, 1)
            picked = jnp.where(lane == row + 4, jnp.broadcast_to(ratio, shape), 0.0)
            scale = RATE * jnp.sum(picked, axis=1, keepdims=True)
        for at in range(weight_ref.shape[0]) if len(weight_ref.shape) == 3 else [Ellipsis]:
            out_ref[at] = weight_ref[at] - scale * update_ref[at]


def master(sums, updates, weights, width):
    arrays = [sums, *updates, *weights]
    shapes = [a.shape for a in weights] + [(3, width)]
    return pl.pallas_call(
        master_kernel,
        grid=(1,),
        in_specs=[whole(a.shape) for a in arrays],
        out_specs=[pl.BlockSpec(s, lambda *_, n=len(s): (0,) * n) for s in shapes],
        out_shape=[jax.ShapeDtypeStruct(s, F32) for s in shapes],
        compiler_params=params(),
        cost_estimate=cost(3),
        name="master",
    )(*arrays)


def halves(parts, groups):
    return by_slot(parts, jnp.int32(0), groups)


def by_index(keep, send, groups, turn=False):
    masks = slot_masks(groups, turn)
    return in_order([keep, send], [masks, [mask | 1 for mask in masks]], jnp.int32(0))


def join_heads(pieces):
    nb, nh, rows, flat = pieces.shape
    wider = nb * nh // PARTS
    parts = pieces.reshape(nb // wider, wider, nh, rows, flat).transpose(0, 2, 1, 3, 4)
    return parts.reshape(PARTS, wider * rows, flat)


def join_parts(parts, nh):
    count = lax.axis_size("batch") * lax.axis_size("head")
    wider = count // PARTS
    _, rows, flat = parts.shape
    parts = parts.reshape(PARTS // nh, nh, wider, rows // wider, flat).transpose(0, 2, 1, 3, 4)
    return parts.reshape(count, rows // wider, flat)


def shards(
    block_input,
    cotangent,
    segment_lengths,
    thought_counts,
    packing_mask,
    attend_weight,
    output_weight,
    expand_weight,
    reduce_weight,
    vectors,
    first_attend,
    first_output,
    first_expand,
    first_reduce,
    first_vectors,
    second_attend,
    second_output,
    second_expand,
    second_reduce,
    second_vectors,
):
    nb, nh = lax.axis_size("batch"), lax.axis_size("head")
    count = nb * nh
    groups, kernel_groups = bit_groups(count), bit_groups(PARTS)
    same = count == PARTS
    place = (lax.axis_index("batch") * nh + lax.axis_index("head")).astype(jnp.int32)
    core = place % 2
    kernel_place = (place if same else jnp.zeros_like(place)).reshape(1)
    rows, length, model = block_input.shape
    tokens = rows * length
    hidden = expand_weight.shape[1]
    own_in, _, own_out = attend_weight.shape
    own = output_weight.shape[0]
    own_red = reduce_weight.shape[0]
    cols = vectors.shape[1]
    wide = hidden // model
    flat = 3 * own_out

    extra = jnp.pad(vectors.astype(BF16).T, ((0, -cols % 16), (0, flat - own)))
    piece = jnp.concatenate([attend_weight.astype(BF16).reshape(own_in, flat), extra], axis=0)
    attend_far = gather_far(piece, groups)

    blocks = expand_weight.astype(BF16).reshape(own, 2, wide // 2, model).transpose(1, 2, 0, 3)
    beside = swap(jnp.where(core == 0, blocks[1], blocks[0]), 1)
    mine = jnp.where(core == 0, blocks[0], blocks[1])
    piece = [
        jnp.concatenate(
            [jnp.where(core == 0, mine, beside), jnp.where(core == 0, beside, mine)], axis=1
        ).reshape(2 * own * (wide // 2), model),
        reduce_weight.astype(BF16),
        output_weight.astype(BF16),
    ]
    pad = -(own_red + own) % 16
    piece = jnp.concatenate(piece + [jnp.zeros((pad, model), BF16)], axis=0)
    late_all = lax.all_gather(piece, AXES, axis=0, tiled=False)
    attend_own = join(spread(attend_far, groups[1]))
    attend_other = swap(attend_own, 1)
    if not same:
        masks = slot_masks(groups)
        attend = in_order([attend_own, attend_other], [masks, [m | 1 for m in masks]], place)
        vec = attend[:, own_in:, :own].transpose(1, 0, 2).reshape(-1, PARTS, model // PARTS)
        vec = jnp.pad(vec.transpose(1, 0, 2), ((0, 0), (0, 0), (0, flat - model // PARTS)))
        attend = join_heads(attend[:, :own_in].reshape(nb, nh, own_in, flat))
        attend_own, attend_other = halves(
            jnp.concatenate([attend, vec], axis=1), kernel_groups
        )

    own_lengths = lax.dynamic_slice_in_dim(
        segment_lengths, lax.axis_index("head") * rows, rows, 0
    )
    own_counts = lax.dynamic_slice_in_dim(thought_counts, lax.axis_index("head") * rows, rows, 0)
    start_of, weight_rows = row_facts(own_lengths, own_counts, packing_mask, length)
    start_of = start_of.reshape(rows, 1, length)
    weight_rows = weight_rows.reshape(tokens, 1)

    x = block_input.reshape(tokens, model)
    cot = cotangent.reshape(tokens, model)
    normed_low, qkv, attend_low, vec = project(
        kernel_place, x, attend_own, attend_other, nh, cols
    )
    context, probs = attend_forward(start_of, qkv, length)
    if not same:
        late = late_all
        both, per = 2 * own, 2 * model // PARTS
        expand_low = (
            late[:, : both * wide // 2]
            .reshape(count // 2, 2, wide // 2, both, model)
            .transpose(1, 2, 0, 3, 4)
            .reshape(2, wide // 2, PARTS // 2, per, model)
            .transpose(2, 0, 1, 3, 4)
            .reshape(PARTS, per * (wide // 2), model)
        )
        low = both * wide // 2
        rest = [
            expand_low,
            late[:, low : low + own_red].reshape(PARTS, hidden // PARTS, model),
            late[:, low + own_red : low + own_red + own].reshape(PARTS, per // 2, model),
            jnp.zeros((PARTS, 8, model), BF16),
        ]
        late_all = jnp.concatenate(rest, axis=1)
    late = (late_all,)
    hidden_states, middle, middle_low, activated, slope, branch = mlp_forward(
        late, context, x, cot, weight_rows, vec, hidden
    )

    def for_devices(keep, send, split):
        parts = [by_index(*both, kernel_groups, n == 1) for n, both in enumerate(zip(keep, send))]
        return by_slot(split(jnp.concatenate(parts, axis=1)), place, groups)

    def split_mid(parts):
        per = 2 * model // PARTS
        expand = (
            jnp.stack([parts[:, :per], parts[:, per + 32 :]], axis=1)
            .reshape(PARTS // 2, 2, 2, per, model)
            .transpose(1, 2, 0, 3, 4)
            .reshape(2, 2, count // 2, 2 * own, model)
            .transpose(2, 0, 1, 3, 4)
            .reshape(count, 4 * own, model)
        )
        output = parts[:, per : per + per // 2].reshape(count, own, model)
        return jnp.concatenate([expand, output], axis=1)

    red_keep, red_send = reduce_weight_grad(kernel_place, activated, branch)
    if same:
        cot, *red_send = ordered(cot, *red_send)
        red = Halves(red_keep, red_send, groups)
    grad_pre, grad_middle, grad_attn, grad_context, mid_sums = mlp_backward(
        late, cot, weight_rows, middle, slope, vec
    )
    if same:
        grad_pre, *terms = ordered(grad_pre, *red.flat())
        red.set(terms)
        grad_pre, *sends = ordered(grad_pre, *red.sends())
        red_received = red.receive(sends)

    mid_keep, mid_send = mid_weight_grad(
        kernel_place, middle_low, grad_pre, context, grad_attn
    )
    if same:
        grad_context, *terms = ordered(grad_context, *mid_send, *red_received)
        mid = Halves(mid_keep, terms[:2], groups)
        red.add(terms[2:])
        grad_context, *sends = ordered(grad_context, *red.sends())
        red_received = red.receive(sends)

    pairs = model // (2 * HEAD_DIM)
    operands = (qkv, context, grad_context, probs, length)
    d_qkv = attend_backward(*operands, 0, pairs // 2)
    if same:
        d_qkv, *terms = ordered(d_qkv, *mid.flat(), *red_received)
        mid.set(terms[:4])
        red.add(terms[4:])
        d_qkv, *sends = ordered(d_qkv, *mid.sends(), *red.last_sends())
        mid_received = mid.receive(sends[:2])
        red_received = red.last_receive(sends[2:])
    d_qkv = attend_backward(*operands, pairs // 2, rows * pairs, d_qkv)
    if same:
        d_qkv, *terms = ordered(d_qkv, *mid_received, *red_received)
        mid.add(terms[:2])
        red_received = terms[2:]
        d_qkv, *sends = ordered(d_qkv, *mid.sends())
        mid_received = mid.receive(sends)
    att_keep, att_send = attend_weight_grad(kernel_place, normed_low, d_qkv, nh)
    if same:
        att_send, *mid_received = ordered(att_send, *mid_received)
        att = Whole(att_keep, att_send, groups)
        mid.add(mid_received)
        d_qkv, *terms = ordered(d_qkv, *mid.last_sends(), *att.terms)
        att.terms = terms[-2:]
        mid_received = mid.last_receive(terms[:-2])
        d_qkv, *sends = ordered(d_qkv, *att.sends())
        att_received = att.receive(sends)
    grad_input, sums, sum_parts = input_grad(d_qkv, x, grad_middle, attend_low, vec, mid_sums)
    if same:
        sum_parts, *terms = ordered(sum_parts, *att_received, *mid_received)
        att.terms = att.terms + terms[:3]
        att_received = att.last_receive(att.last_sends())
        red_grad, found = red.finish(red_received), mid.finish(terms[3:])
        per = 2 * own
        mid = jnp.concatenate(
            [found[:per], found[per + 32 :], found[per : per + own]], axis=0
        )
    else:
        red_parts = for_devices(
            red_keep, red_send, lambda parts: parts.reshape(count, own_red, model)
        )
        mid_parts = for_devices(mid_keep, mid_send, split_mid)
        att_parts = for_devices(
            [att_keep], [att_send], lambda parts: join_parts(parts, nh).reshape(count, own_in, flat)
        )
        red_grad, mid = scatter(*red_parts, groups), scatter(*mid_parts, groups)
        att_grad = scatter(*att_parts, groups)
    out_grad = mid[4 * own : 5 * own]
    exp_both = mid[: 4 * own].reshape(2, 2, own, model)
    kept = jnp.where(core == 0, exp_both[:, 0], exp_both[:, 1])
    beside = swap(jnp.where(core == 0, exp_both[:, 1], exp_both[:, 0]), 1)
    exp_grad = jnp.stack(
        [jnp.where(core == 0, kept, beside), jnp.where(core == 0, beside, kept)]
    ).reshape(wide, own, model)
    exp_grad = exp_grad.transpose(1, 0, 2).reshape(own, hidden)


    if same:
        vector_grad = lax.all_to_all(sum_parts, AXES, 0, 0, tiled=True)
    else:
        vector_grad = lax.dynamic_slice_in_dim(all_sum(sums, groups), place * own, own, 1)
    late_weights = (output_weight, expand_weight, reduce_weight)
    late_states = [
        (grad, first, second, weight)
        for grad, first, second, weight in zip(
            (out_grad, exp_grad, red_grad),
            (first_output, first_expand, first_reduce),
            (second_output, second_expand, second_reduce),
            late_weights,
        )
    ]
    late_found, late_sums = adapt(late_states, [1, 2, 3])
    if same:
        late_sums, *att_received = ordered(late_sums, *att_received)
        att_grad = att.finish(att_received)

    def planes(state):
        return state.transpose(1, 0, 2)

    found, sums = adapt(
        [
            (att_grad, planes(first_attend), planes(second_attend), planes(attend_weight)),
            (vector_grad, first_vectors.T, second_vectors.T, vectors.T),
        ],
        [0, 4],
        late_sums,
        count if same else 0,
    )
    sums = lax.all_to_all(sums, AXES, 0, 0, tiled=True) if same else all_sum(sums, groups)
    adapted = [list(found[0]), *late_found, [a.T for a in found[1]]]
    *masters, trust_norms = master(
        sums,
        [found[0][2], *[a[2] for a in late_found], found[1][2]],
        [planes(attend_weight), *late_weights, vectors.T],
        4 + cols,
    )
    masters[4] = masters[4].T
    adapted[0] = [planes(a) for a in adapted[0]]
    masters[0] = planes(masters[0])
    return (
        hidden_states.reshape(rows, length, model),
        grad_input.reshape(rows, length, model),
        *[a[0] for a in adapted],
        *[a[1] for a in adapted],
        *masters,
        trust_norms,
    )


def solution(mesh):
    rows = P(AXES, None, None)
    state = [P("batch", None, "head")] + [P(AXES, None)] * 4
    return jax.shard_map(
        shards,
        mesh=mesh,
        in_specs=(rows, rows, P("batch", None), P("batch", None), P(AXES, None), *state * 3),
        out_specs=(rows, rows, *state * 3, P()),
        check_vma=False,
    )
```

```python
import jax
import jax.numpy as jnp
from jax import lax
from jax.experimental import pallas as pl
from jax.experimental.pallas import tpu as pltpu
from jax.sharding import PartitionSpec as P

HEAD_DIM = 64
THOUGHT_TOKENS = 8
STEP = 6
PARTS = 32
SPAN = 256
BLOCK = 128

NORM_EPS = 1e-05
NEGATIVE = -1e30
BETA = 0.5
RATE = 0.5
DECAY = 0.01
ADAM_EPS = 1e-06
AXES = ("batch", "head")
ROOT = 0.7978845608028654
CUBE = 0.044715
F32 = jnp.float32
BF16 = jnp.bfloat16
NT = (((1,), (1,)), ((), ()))
TN = (((0,), (0,)), ((), ()))


def dot(a, b, dims=(((1,), (0,)), ((), ()))):
    return lax.dot_general(a, b, dims, preferred_element_type=F32)


def params(grid=1, vmem=60):
    return pltpu.CompilerParams(
        dimension_semantics=("arbitrary",) * grid, vmem_limit_bytes=vmem * 1024 * 1024
    )


def cost(micros):
    return pl.CostEstimate(flops=int(micros * 0.29e9), bytes_accessed=1 << 18, transcendentals=0)


def whole(shape):
    return pl.BlockSpec(shape, lambda *_: (0,) * len(shape), pipeline_mode=pl.Buffered(1))


SCALARS = pl.BlockSpec(memory_space=pltpu.SMEM)


def row_facts(lengths, counts, mask, span):
    positions = jnp.arange(span, dtype=jnp.int32)
    ends = jnp.cumsum(lengths, axis=-1)
    starts = ends - lengths
    inside = (positions[None, :, None] >= starts[:, None, :]) & (
        positions[None, :, None] < ends[:, None, :]
    )
    start_of = jnp.sum(jnp.where(inside, starts[:, None, :], 0), axis=-1)
    passes = jnp.sum(jnp.where(inside, counts[:, None, :], 0), axis=-1)
    keep = (positions[None, :] - start_of >= THOUGHT_TOKENS * passes) & (mask > 0)
    return start_of, keep.astype(F32)


def windows(length):
    return [
        (low, max(0, low - SPAN), low + BLOCK - max(0, low - SPAN)) for low in range(0, length, BLOCK)
    ]


def fill_caps(start_ref, cap_ref, length):
    for number, (low, first, count) in enumerate(windows(length)):
        key = lax.broadcasted_iota(jnp.int32, (count, BLOCK), 0) + first
        query = lax.broadcasted_iota(jnp.int32, (count, BLOCK), 1) + low
        start = start_ref[0, :, low : low + BLOCK]
        allowed = (key <= query) & (key >= start)
        cap_ref[number, :count] = jnp.where(allowed, 3e38, NEGATIVE)


def cap_of(cap_ref, number, count):
    cap = cap_ref[number, :count]
    return jnp.concatenate([cap, cap], axis=1)


def for_heads(values):
    lane = lax.broadcasted_iota(jnp.int32, (1, 2 * HEAD_DIM), 1)
    return jnp.concatenate(
        [jnp.where(lane < HEAD_DIM, values, 0), jnp.where(lane >= HEAD_DIM, values, 0)], axis=0
    )


def of_heads(values):
    return jnp.concatenate([values[:HEAD_DIM, :BLOCK], values[HEAD_DIM:, BLOCK:]], axis=0)


def in_stages(units, ahead, behind, first, middle, last):
    started, worked = [first(unit) for unit in units[:ahead]], []
    for number, unit in enumerate(units):
        if number + ahead < len(units):
            started.append(first(units[number + ahead]))
        worked.append((unit, middle(unit, started.pop(0))))
        if len(worked) > behind:
            last(*worked.pop(0))
    for both in worked:
        last(*both)


def attend_forward_kernel(fresh, start_ref, q_ref, k_ref, v_ref, o_ref, p_ref, cap_ref):
    length = q_ref.shape[0]
    pl.when(fresh)(lambda: fill_caps(start_ref, cap_ref, length))
    value_t = v_ref[...].T

    def score(unit):
        _, (low, first, count) = unit
        query = for_heads(q_ref[low : low + BLOCK, :] * (HEAD_DIM**-0.5))
        return dot(k_ref[first : first + count, :], query, NT)

    def soften(unit, scores):
        number, (_, _, count) = unit
        scores = jnp.minimum(scores, cap_of(cap_ref, number, count))
        grown = jnp.exp(scores - jnp.max(scores, axis=0, keepdims=True))
        probs = (grown * (1.0 / total(grown))).astype(BF16)
        p_ref[0, 0, number, :count] = probs
        return probs

    def mix(unit, probs):
        _, (low, first, count) = unit
        result = dot(value_t[:, first : first + count], probs)
        o_ref[low : low + BLOCK, :] = of_heads(result).T.astype(BF16)

    in_stages(list(enumerate(windows(length))), 4, 1, score, soften, mix)


def attend_backward_kernel(q_ref, k_ref, v_ref, o_ref, do_ref, p_ref, *rest):
    d_ref = rest[-1]
    length = q_ref.shape[0]
    key_t = k_ref[...].T
    grad_key, grad_value = {}, {}

    def query_of(low):
        return for_heads(q_ref[low : low + BLOCK, :] * (HEAD_DIM**-0.5))

    def grad_of(low):
        return for_heads(do_ref[low : low + BLOCK, :])

    def score(unit):
        _, (low, first, count) = unit
        return dot(v_ref[first : first + count, :], grad_of(low), NT)

    def soften(unit, grad_probs):
        number, (low, _, count) = unit
        product = do_ref[low : low + BLOCK, :].astype(F32) * o_ref[low : low + BLOCK, :].astype(F32)
        product = product.T
        inner = jnp.concatenate([total(product[:HEAD_DIM]), total(product[HEAD_DIM:])], axis=1)
        probs = p_ref[0, 0, number, :count]
        return probs, (probs.astype(F32) * (grad_probs - inner)).astype(BF16)

    def mix(unit, found):
        _, (low, first, count) = unit
        probs, grad_scores = found
        terms = dot(probs, grad_of(low)), dot(grad_scores, query_of(low))
        grad_query = dot(key_t[:, first : first + count], grad_scores)
        d_ref[0, low : low + BLOCK, :] = (of_heads(grad_query).T * (HEAD_DIM**-0.5)).astype(BF16)
        for sums, term, place in ((grad_value, terms[0], 2), (grad_key, terms[1], 1)):
            for at in range(first, first + count, BLOCK):
                one = term[at - first : at - first + BLOCK]
                sums[at] = sums[at] + one if at in sums else one
            for at in list(sums):
                if at <= low - SPAN or low + BLOCK == length:
                    d_ref[place, at : at + BLOCK, :] = sums.pop(at).astype(BF16)

    in_stages(list(enumerate(windows(length))), 2, 0, score, soften, mix)


def attention_specs(length, pairs, low=0):
    pair = 2 * HEAD_DIM

    def at(i):
        return (i + low) // pairs, (i + low) % pairs

    def columns(n):
        return lambda i: (at(i)[0], n * pairs + at(i)[1])

    qkv = [pl.BlockSpec((length, pair), columns(n)) for n in range(3)]
    rows = pl.BlockSpec((length, pair), columns(0))
    probs = pl.BlockSpec((1, 1) + probs_shape(length), lambda i: (*at(i), 0, 0, 0))
    start = pl.BlockSpec((1, 1, length), lambda i: (at(i)[0], 0, 0))
    return start, qkv, rows, probs, lambda i: (0, *at(i))


def probs_shape(length):
    return (length // BLOCK, SPAN + BLOCK, 2 * BLOCK)


def attend_forward(start, qkv, length):
    tokens, model = qkv.shape[0], qkv.shape[1] // 3
    pairs = model // (2 * HEAD_DIM)
    rows = tokens // length
    start_spec, qkv_specs, row_spec, probs_spec, _ = attention_specs(length, pairs)

    def kernel(*refs):
        attend_forward_kernel(pl.program_id(0) % pairs == 0, *refs)

    return pl.pallas_call(
        kernel,
        grid=(rows * pairs,),
        in_specs=[start_spec] + qkv_specs,
        out_specs=[row_spec, probs_spec],
        out_shape=[
            jax.ShapeDtypeStruct((tokens, model), BF16),
            jax.ShapeDtypeStruct((rows, pairs) + probs_shape(length), BF16),
        ],
        scratch_shapes=[pltpu.VMEM((length // BLOCK, SPAN + BLOCK, BLOCK), F32)],
        compiler_params=params(),
        cost_estimate=cost(18),
        name="attend_forward",
    )(start, qkv, qkv, qkv)


def attend_backward(qkv, out, grad, probs, length, low, high, before=None):
    tokens, model = out.shape
    pairs = model // (2 * HEAD_DIM)
    _, qkv_specs, row_spec, probs_spec, at = attention_specs(length, pairs, low)
    operands = [qkv, qkv, qkv, out, grad, probs]
    in_specs = qkv_specs + [row_spec, row_spec, probs_spec]
    aliases = {}
    if before is not None:
        aliases = {len(operands): 0}
        operands.append(before)
        in_specs.append(pl.BlockSpec(memory_space=pl.ANY))
    return pl.pallas_call(
        attend_backward_kernel,
        grid=(high - low,),
        in_specs=in_specs,
        out_specs=pl.BlockSpec((3, length, 2 * HEAD_DIM), at),
        out_shape=jax.ShapeDtypeStruct((3, tokens, model), BF16),
        input_output_aliases=aliases,
        compiler_params=params(),
        cost_estimate=cost(2.0 * (high - low)),
        name="attend_backward",
    )(*operands)


def normalize(values):
    centre = values - jnp.mean(values, axis=-1, keepdims=True)
    factor = lax.rsqrt(jnp.mean(centre * centre, axis=-1, keepdims=True) + NORM_EPS)
    return centre * factor, factor


def norm_back(inner, normed, factor):
    return factor * (
        inner
        - jnp.mean(inner, axis=-1, keepdims=True)
        - normed * jnp.mean(inner * normed, axis=-1, keepdims=True)
    )


def total(values):
    return jnp.sum(values, axis=0, keepdims=True)


def project_kernel(place_ref, x_ref, own_ref, other_ref, nl_ref, qkv_ref, w_ref, vec_ref, *, heads):
    slots, rows, flat = own_ref.shape
    rows -= -(-vec_ref.shape[0] // 16) * 16
    part, model = flat // 3, x_ref.shape[1]
    groups = bit_groups(2 * slots)
    place = place_ref[0]

    @pl.when(pl.program_id(0) == 0)
    def _():
        for here in range(heads):

            @pl.when(place % heads == here)
            def _(here=here):
                for bit, ref in enumerate((own_ref, other_ref)):
                    for slot in range(slots):
                        mask = mask_of(slot, groups) | bit
                        head = here ^ (mask % heads)
                        row = pl.multiple_of(((place ^ mask) // heads) * rows, rows)
                        for j in range(3):
                            low = j * model + head * part
                            w_ref[pl.ds(row, rows), low : low + part] = ref[
                                slot, :rows, j * part : (j + 1) * part
                            ]

        count, each = vec_ref.shape[0], model // (2 * slots)
        lane = lax.broadcasted_iota(jnp.int32, (1, model), 1)
        found = jnp.zeros((count, model), F32)
        for bit, ref in enumerate((own_ref, other_ref)):
            for slot in range(slots):
                device = place ^ (mask_of(slot, groups) | bit)
                piece = ref[slot, rows:, :128].astype(F32)[:count]
                piece = jnp.concatenate([piece] * (model // 128), axis=1)
                piece = pltpu.roll(piece, (device * each) % 128, 1)
                inside = (lane >= device * each) & (lane < (device + 1) * each)
                found = jnp.where(inside, piece, found)
        vec_ref[...] = found

    normed, _ = normalize(x_ref[...].astype(F32))
    low = (normed * vec_ref[0:1, :] + vec_ref[1:2, :]).astype(BF16)
    nl_ref[...] = low
    for j in range(3):
        side = slice(j * model, (j + 1) * model)
        result = dot(low, w_ref[:, side])
        if j != 1:
            result = result + vec_ref[2 + j // 2 : 3 + j // 2, :]
        qkv_ref[:, side] = result.astype(BF16)


def project(place, x, own, other, heads, cols, tile=512):
    tokens, model = x.shape
    row = pl.BlockSpec((tile, model), lambda i: (i, 0))
    return pl.pallas_call(
        lambda *refs: project_kernel(*refs, heads=heads),
        grid=(tokens // tile,),
        in_specs=[SCALARS, row, whole(own.shape), whole(other.shape)],
        out_specs=[
            row,
            pl.BlockSpec((tile, 3 * model), lambda i: (i, 0)),
            pl.BlockSpec((model, 3 * model), lambda i: (0, 0)),
            pl.BlockSpec((cols, model), lambda i: (0, 0)),
        ],
        out_shape=[
            jax.ShapeDtypeStruct((tokens, model), BF16),
            jax.ShapeDtypeStruct((tokens, 3 * model), BF16),
            jax.ShapeDtypeStruct((model, 3 * model), BF16),
            jax.ShapeDtypeStruct((cols, model), F32),
        ],
        compiler_params=params(),
        cost_estimate=cost(14),
        name="project",
    )(place, x, own, other)


class Late:
    def __init__(self, refs, scratch):
        (self.parts,) = refs
        self.expand, self.reduce, self.output, self.stage, self.sem = scratch
        self.model = self.output.shape[1]
        self.chunks = self.expand.shape[0]

    def copies(self):
        per = self.model // self.stage.shape[1]
        red = self.reduce.shape[0] // (2 * self.stage.shape[1])
        end = 2 * per + red
        for device in range(self.parts.shape[0]):
            row, bit = (device // 2) * per, device % 2
            for n in range(2):
                yield (
                    self.parts.at[device, n * per : (n + 1) * per],
                    self.expand.at[2 * bit + n, row : row + per],
                )
            yield (
                self.parts.at[device, 2 * per : end],
                self.reduce.at[device * red : (device + 1) * red],
            )
            yield (
                self.parts.at[device, end : end + self.stage.shape[2]],
                self.stage.at[bit, device // 2],
            )

    def load(self):
        copies = [pltpu.make_async_copy(a, b, self.sem) for a, b in self.copies()]
        for copy in copies:
            copy.start()
        for copy in copies:
            copy.wait()
        slots = self.stage.shape[1]
        per = self.model // slots
        for n in range(slots):
            both = [self.stage[bit, n, : per // 2, :].astype(F32) for bit in range(2)]
            self.output[n * per : (n + 1) * per, :] = jnp.concatenate(both, axis=0).astype(BF16)

    def reduce_rows(self, c):
        return self.reduce[c * self.model : (c + 1) * self.model, :]

    @staticmethod
    def specs():
        return [pl.BlockSpec(memory_space=pl.ANY)]

    @staticmethod
    def scratch(late, hidden):
        slots, _, model = late[0].shape
        slots //= 2
        return [
            pltpu.VMEM((hidden // model, model, model), BF16),
            pltpu.VMEM((hidden, model), BF16),
            pltpu.VMEM((model, model), BF16),
            pltpu.VMEM((2, slots, 32, model), BF16),
            pltpu.SemaphoreType.DMA,
        ]


def mlp_forward_kernel(*refs):
    late = Late(refs[:-16], refs[-5:])
    ctx_ref, x_ref, cot_ref, wt_ref, vec_ref = refs[-16:-11]
    hid_ref, mid_ref, nm_ref, act_ref, dg_ref, gb_ref = refs[-11:-5]
    model = late.model
    pl.when(pl.program_id(0) == 0)(late.load)
    middle = x_ref[...].astype(F32) + dot(ctx_ref[...], late.output[...]) + vec_ref[4:5, :]
    mid_ref[...] = middle
    gb_ref[...] = (cot_ref[...].astype(F32) * wt_ref[...]).astype(BF16)
    normed, _ = normalize(middle)
    low = (normed * vec_ref[5:6, :] + vec_ref[6:7, :]).astype(BF16)
    nm_ref[...] = low
    result = middle + vec_ref[7:8, :]
    for c in range(late.chunks):
        side = slice(c * model, (c + 1) * model)
        pre = dot(low, late.expand[c]) + vec_ref[8 + c : 9 + c, :]
        square = pre * pre
        half = 0.5 + 0.5 * jnp.tanh(pre * (ROOT + (ROOT * CUBE) * square))
        act = pre * half
        dg = half + act * (1.0 - half) * (2.0 * ROOT + (6.0 * ROOT * CUBE) * square)
        dg_ref[:, side] = dg.astype(BF16)
        act = act.astype(BF16)
        act_ref[:, side] = act
        result = result + dot(act, late.reduce_rows(c))
    hid_ref[...] = result.astype(BF16)


def mlp_forward(late, ctx, x, cot, wt, vec, hidden, tile=256):
    tokens, model = x.shape
    row = pl.BlockSpec((tile, model), lambda i: (i, 0))
    wide = pl.BlockSpec((tile, hidden), lambda i: (i, 0))
    one = pl.BlockSpec((tile, 1), lambda i: (i, 0))

    def shape(width, kind=BF16):
        return jax.ShapeDtypeStruct((tokens, width), kind)

    return pl.pallas_call(
        mlp_forward_kernel,
        grid=(tokens // tile,),
        in_specs=Late.specs() + [row, row, row, one, whole(vec.shape)],
        out_specs=[row, row, row, wide, wide, row],
        out_shape=[
            shape(model), shape(model, F32), shape(model), shape(hidden), shape(hidden), shape(model),
        ],
        scratch_shapes=Late.scratch(late, hidden),
        compiler_params=params(),
        cost_estimate=cost(40),
        name="mlp_forward",
    )(*late, ctx, x, cot, wt, vec)


def mlp_backward_kernel(*refs):
    late = Late(refs[:-15], refs[-5:])
    cot_ref, wt_ref, mid_ref, dg_ref, vec_ref = refs[-15:-10]
    gpre_ref, gm_ref, ga_ref, gc_ref, sum_ref = refs[-10:-5]
    model = late.model

    @pl.when(pl.program_id(0) == 0)
    def _():
        late.load()
        sum_ref[...] = jnp.zeros_like(sum_ref)

    grad_out = cot_ref[...].astype(F32) * wt_ref[...]
    branch = grad_out.astype(BF16)
    sum_ref[3:4, :] += total(branch.astype(F32))
    back = None
    for c in range(late.chunks):
        side = slice(c * model, (c + 1) * model)
        grad = (dot(branch, late.reduce_rows(c), NT) * dg_ref[:, side].astype(F32)).astype(BF16)
        gpre_ref[:, side] = grad
        sum_ref[4 + c : 5 + c, :] += total(grad.astype(F32))
        term = dot(grad, late.expand[c], NT)
        back = term if back is None else back + term
    normed, factor = normalize(mid_ref[...])
    sum_ref[1:2, :] += total(back * normed)
    sum_ref[2:3, :] += total(back)
    grad_middle = grad_out + norm_back(back * vec_ref[5:6, :], normed, factor)
    gm_ref[...] = grad_middle
    low = grad_middle.astype(BF16)
    ga_ref[...] = low
    sum_ref[0:1, :] += total(low.astype(F32))
    gc_ref[...] = dot(low, late.output[...], NT).astype(BF16)


def mlp_backward(late, cot, wt, mid, dg, vec, tile=256):
    tokens, model = cot.shape
    hidden = dg.shape[1]
    row = pl.BlockSpec((tile, model), lambda i: (i, 0))
    wide = pl.BlockSpec((tile, hidden), lambda i: (i, 0))
    one = pl.BlockSpec((tile, 1), lambda i: (i, 0))

    def shape(width, kind=BF16):
        return jax.ShapeDtypeStruct((tokens, width), kind)

    return pl.pallas_call(
        mlp_backward_kernel,
        grid=(tokens // tile,),
        in_specs=Late.specs() + [row, one, row, wide, whole(vec.shape)],
        out_specs=[wide, row, row, row, pl.BlockSpec((8, model), lambda i: (0, 0))],
        out_shape=[
            shape(hidden), shape(model, F32), shape(model), shape(model),
            jax.ShapeDtypeStruct((8, model), F32),
        ],
        scratch_shapes=Late.scratch(late, hidden),
        compiler_params=params(),
        cost_estimate=cost(36),
        name="mlp_backward",
    )(*late, cot, wt, mid, dg, vec)


def put_parts(place, outs, pieces, turn=False):
    groups = bit_groups(2 * outs[0].shape[0])
    for bit in range(2):

        @pl.when(place % 2 == bit)
        def _(bit=bit):
            for device, index, value in pieces:
                mask = place ^ device
                slot = slot_of(turned(mask, groups) if turn else mask, groups)
                outs[(device % 2) ^ bit][(slot,) + index] = value


class Outbox:
    def __init__(self, place, outs, buffer, sems, turn):
        self.place, self.outs, self.buffer, self.sems, self.turn = place, outs, buffer, sems, turn

    def begin(self, step, rows, count):
        @pl.when(step >= 2)
        def _():
            self.wait(step, rows, count)

    def wait(self, step, rows, count):
        for n in range(count):
            part = self.buffer.at[step % 2, n * rows : (n + 1) * rows]
            pltpu.make_async_copy(part, part, self.sems.at[step % 2]).wait()

    def send(self, step, pieces):
        groups = bit_groups(2 * self.outs[0].shape[0])
        for bit in range(2):

            @pl.when(self.place % 2 == bit)
            def _(bit=bit):
                for low, rows, odd, device, kind, there in pieces:
                    mask = self.place ^ device
                    mask = turned(mask, groups) if self.turn[kind] else mask
                    out = self.outs[2 * (odd ^ bit) + kind].at[slot_of(mask, groups)]
                    pltpu.make_async_copy(
                        self.buffer.at[step % 2, low : low + rows],
                        out.at[there : there + rows],
                        self.sems.at[step % 2],
                    ).start()


def reduce_weight_grad_kernel(place_ref, a_ref, b_ref, *rest):
    *outs, buffer, sems = rest
    slots, rows, model = outs[0].shape
    step, last = pl.program_id(0), pl.num_programs(0) - 1
    count = model // rows
    box = Outbox(place_ref[0], outs, buffer, sems, (False, True))
    result = dot(a_ref[...], b_ref[...], TN).astype(BF16)
    box.begin(step, rows, count)
    buffer[step % 2] = result
    box.send(
        step,
        [(n * rows, rows, n // 2 % 2, step * (count // 2) + n // 2, n % 2, 0) for n in range(count)],
    )

    @pl.when(step == last)
    def _():
        box.wait(step + 1, rows, count)
        box.wait(step, rows, count)


def hbm_outs_of(*shapes):
    return dict(
        out_specs=[pl.BlockSpec(memory_space=pl.ANY)] * len(shapes),
        out_shape=[jax.ShapeDtypeStruct(shape, BF16) for shape in shapes],
    )


def outs_of(*shapes):
    return dict(
        out_specs=[pl.BlockSpec(shape, lambda *_: (0,) * len(shape)) for shape in shapes],
        out_shape=[jax.ShapeDtypeStruct(shape, BF16) for shape in shapes],
    )


def reduce_weight_grad(place, act, branch):
    tokens, model = branch.shape
    hidden = act.shape[1]
    shape = (PARTS // 2, hidden // PARTS // 2, model)
    found = pl.pallas_call(
        reduce_weight_grad_kernel,
        grid=(hidden // model,),
        in_specs=[SCALARS, pl.BlockSpec((tokens, model), lambda i: (0, i)), whole(branch.shape)],
        **hbm_outs_of(*[shape] * 4),
        scratch_shapes=[pltpu.VMEM((2, model, model), BF16), pltpu.SemaphoreType.DMA((2,))],
        compiler_params=params(),
        cost_estimate=cost(15),
        name="reduce_weight_grad",
    )(place, act, branch)
    return found[:2], found[2:]


def mid_weight_grad_kernel(place_ref, nm_ref, gpre_ref, ctx_hbm, ga_hbm, *rest):
    *outs, ctx_ref, ga_ref, buffer, sems, out_sems = rest
    copies = [
        pltpu.make_async_copy(ctx_hbm, ctx_ref, sems.at[0]),
        pltpu.make_async_copy(ga_hbm, ga_ref, sems.at[1]),
    ]
    slots, rows, model = outs[0].shape
    per = model // slots
    step = pl.program_id(0)
    last = pl.num_programs(0) - 1
    box = Outbox(place_ref[0], outs, buffer, out_sems, (False, True))

    @pl.when(step == 1)
    def _():
        for copy in copies:
            copy.start()

    for c in range(4):

        @pl.when(step == c)
        def _(c=c):
            result = dot(nm_ref[...], gpre_ref[...], TN).astype(BF16)
            if c >= 2:
                box.wait(c, per, slots)
            buffer[c % 2, :model] = result
            box.send(
                c, [(n * per, per, c // 2, 2 * n + c // 2, c % 2, 0) for n in range(slots)]
            )

    @pl.when(step == last)
    def _():
        for copy in copies:
            copy.wait()
        result = dot(ctx_ref[...], ga_ref[...], TN)
        half, tall = per // 2, rows - per
        empty = jnp.zeros((tall - half, model), F32)
        box.wait(4, per, slots)
        for n in range(2 * slots):
            both = jnp.concatenate([result[n * half : (n + 1) * half], empty], axis=0)
            buffer[0, n * tall : (n + 1) * tall] = both.astype(BF16)
        box.send(4, [(n * tall, tall, n % 2, n, 0, per) for n in range(2 * slots)])
        box.wait(3, per, slots)
        box.wait(4, tall, 2 * slots)


def mid_weight_grad(place, nm, gpre, ctx, ga):
    tokens, model = nm.shape
    hidden = gpre.shape[1]
    assert hidden == 4 * model
    slots, per = PARTS // 2, 2 * model // PARTS
    shapes = [(slots, per + 32, model), (slots, per, model)]
    found = pl.pallas_call(
        mid_weight_grad_kernel,
        grid=(5,),
        in_specs=[
            SCALARS,
            whole(nm.shape),
            pl.BlockSpec((tokens, model), lambda i: (0, jnp.minimum(i, 3))),
            pl.BlockSpec(memory_space=pl.ANY),
            pl.BlockSpec(memory_space=pl.ANY),
        ],
        **hbm_outs_of(*shapes * 2),
        scratch_shapes=[
            pltpu.VMEM(ctx.shape, BF16),
            pltpu.VMEM(ga.shape, BF16),
            pltpu.VMEM((2, 32 * PARTS, model), BF16),
            pltpu.SemaphoreType.DMA((2,)),
            pltpu.SemaphoreType.DMA((2,)),
        ],
        compiler_params=params(),
        cost_estimate=cost(19),
        name="mid_weight_grad",
    )(place, nm, gpre, ctx, ga)
    return found[:2], found[2:]


def attend_weight_grad_kernel(place_ref, a_ref, b_ref, keep_ref, send_ref, *, heads):
    slots, rows, flat = keep_ref.shape
    part = flat // 3
    result = dot(a_ref[...], b_ref[0], TN).astype(BF16)
    for j in range(3):

        @pl.when(pl.program_id(0) == j)
        def _(j=j):
            put_parts(
                place_ref[0],
                (keep_ref, send_ref),
                [
                    (
                        d,
                        (slice(None), slice(j * part, (j + 1) * part)),
                        result[
                            d // heads * rows : (d // heads + 1) * rows,
                            d % heads * part : (d % heads + 1) * part,
                        ],
                    )
                    for d in range(2 * slots)
                ],
            )


def attend_weight_grad(place, nl, d_qkv, heads):
    tokens, model = nl.shape
    return pl.pallas_call(
        lambda *refs: attend_weight_grad_kernel(*refs, heads=heads),
        grid=(3,),
        in_specs=[SCALARS, whole(nl.shape), pl.BlockSpec((1, tokens, model), lambda j: (j, 0, 0))],
        **outs_of(*[(PARTS // 2, model * heads // PARTS, 3 * model // heads)] * 2),
        compiler_params=params(),
        cost_estimate=cost(13),
        name="attend_weight_grad",
    )(place, nl, d_qkv)


def input_grad_kernel(d_ref, x_ref, gm_ref, w_ref, vec_ref, mid_ref, out_ref, sum_ref, part_ref):
    model = x_ref.shape[1]

    @pl.when(pl.program_id(0) == 0)
    def _():
        sum_ref[:4, :] = jnp.zeros((4, model), F32)
        sum_ref[4:, :] = mid_ref[...]

    back = None
    for j in range(3):
        term = dot(d_ref[j], w_ref[:, j * model : (j + 1) * model], NT)
        back = term if back is None else back + term
    normed, factor = normalize(x_ref[...].astype(F32))
    sum_ref[0:1, :] += total(back * normed)
    sum_ref[1:2, :] += total(back)
    sum_ref[2:3, :] += total(d_ref[0].astype(F32))
    sum_ref[3:4, :] += total(d_ref[2].astype(F32))
    out_ref[...] = (gm_ref[...] + norm_back(back * vec_ref[0:1, :], normed, factor)).astype(BF16)

    @pl.when(pl.program_id(0) == pl.num_programs(0) - 1)
    def _():
        count = part_ref.shape[0]
        each = model // count
        part_ref[...] = jnp.zeros_like(part_ref)
        for n in range(count):
            part_ref[n, : sum_ref.shape[0], :each] = sum_ref[:, n * each : (n + 1) * each]


def input_grad(d_qkv, x, gm, w, vec, mid_sums, tile=512):
    tokens, model = x.shape
    row = pl.BlockSpec((tile, model), lambda i: (i, 0))
    return pl.pallas_call(
        input_grad_kernel,
        grid=(tokens // tile,),
        in_specs=[
            pl.BlockSpec((3, tile, model), lambda i: (0, i, 0)), row, row,
            whole(w.shape), whole(vec.shape), whole(mid_sums.shape),
        ],
        out_specs=[
            row,
            pl.BlockSpec(vec.shape, lambda i: (0, 0)),
            pl.BlockSpec((PARTS, 16, 128), lambda i: (0, 0, 0)),
        ],
        out_shape=[
            jax.ShapeDtypeStruct((tokens, model), BF16),
            jax.ShapeDtypeStruct(vec.shape, F32),
            jax.ShapeDtypeStruct((PARTS, 16, 128), F32),
        ],
        compiler_params=params(),
        cost_estimate=cost(16),
        name="input_grad",
    )(d_qkv, x, gm, w, vec, mid_sums)


def bit_groups(count):
    bits = count.bit_length() - 1
    assert count == 1 << bits
    return [(0, 1)] + [(low, min(2, bits - low)) for low in range(1, bits, 2)]


def slot_of(mask, groups):
    slot = 0
    for low, width in groups[1:]:
        slot = slot * (1 << width) + ((mask >> low) & ((1 << width) - 1))
    return slot


def mask_of(slot, groups):
    mask = 0
    for low, width in groups[:0:-1]:
        mask |= (slot & ((1 << width) - 1)) << low
        slot >>= width
    return mask


def swap(value, mask):
    count = lax.axis_size("batch") * lax.axis_size("head")
    return lax.ppermute(value, AXES, [(i, i ^ mask) for i in range(count)])


def spread(piece, group):
    low, width = group
    return [piece] + [swap(piece, step << low) for step in range(1, 1 << width)]


def join(parts):
    return jnp.concatenate(parts, axis=0)


def gather_far(piece, groups):
    piece = piece[None]
    for group in groups[:1:-1]:
        piece = join(spread(piece, group))
    return piece


def cross(pieces, group):
    count, rows = pieces.shape[0], pieces.shape[1] // 2
    low, high = 1 << group[0], 2 << group[0]
    first, second = pieces[:, :rows], pieces[:, rows:]
    received = swap(first, high), swap(second, low)
    first, second = join([first, received[0]]), join([second, received[1]])
    others = swap(first, low), swap(second, high)
    first = join([first[:count], others[0][:count], first[count:], others[0][count:]])
    return jnp.concatenate([first, join([second, others[1]])], axis=1)


def ordered(*values):
    return lax.optimization_barrier(values)


class Halves:
    def __init__(self, keep, send, groups):
        self.groups = groups
        self.bits = [2 << groups[1][0], 1 << groups[1][0]]
        self.terms = [[kept, swap(sent, 1)] for kept, sent in zip(keep, send)]
        self.count = keep[0].shape[0]

    def flat(self):
        return [t for terms in self.terms for t in terms]

    def set(self, flat):
        count = len(self.terms[0])
        self.terms = [list(flat[:count]), list(flat[count:])]

    def sends(self):
        self.count //= 2
        here = slice(self.count, 2 * self.count)
        return [added([t[here] for t in terms]).astype(BF16) for terms in self.terms]

    def receive(self, sends):
        received = [swap(send, bit) for send, bit in zip(sends, self.bits)]
        self.bits = self.bits[::-1]
        return received

    def add(self, received):
        self.terms = [terms + [one] for terms, one in zip(self.terms, received)]

    def at(self, slot):
        return jnp.concatenate([added([t[slot] for t in terms]) for terms in self.terms], axis=0)

    def last_sends(self):
        return [self.at(slot).astype(BF16) for slot in range(1, self.count)]

    def last_receive(self, sends):
        return [swap(send, (n + 1) << self.groups[2][0]) for n, send in enumerate(sends)]

    def finish(self, received):
        return added([self.at(0), *received])


class Whole:
    def __init__(self, keep, send, groups):
        self.groups = groups
        self.terms = [keep, swap(send, 1)]
        self.count = keep.shape[0]

    def sends(self):
        self.count //= 4
        return [
            added([t[n * self.count : (n + 1) * self.count] for t in self.terms]).astype(BF16)
            for n in range(1, 4)
        ]

    def receive(self, sends):
        return [swap(send, (n + 1) << self.groups[1][0]) for n, send in enumerate(sends)]

    def last_sends(self):
        return [added([t[n] for t in self.terms]).astype(BF16) for n in range(1, self.count)]

    def last_receive(self, sends):
        return [swap(send, (n + 1) << self.groups[2][0]) for n, send in enumerate(sends)]

    def finish(self, received):
        return added([added([t[0] for t in self.terms]), *received])


def added(terms):
    return sum(term.astype(F32) for term in terms)


def scatter(keep, send, groups):
    terms = [keep, swap(send, 1)]
    for low, width in groups[1:]:
        count = 1 << width
        terms = [t.reshape((count, -1) + t.shape[1:]) for t in terms]
        sends = [added([t[step] for t in terms]).astype(BF16) for step in range(1, count)]
        terms = [added([t[0] for t in terms])]
        terms += [swap(send, (n + 1) << low) for n, send in enumerate(sends)]
    return added(terms)[0]


def all_sum(value, groups):
    for low, width in groups:
        value = sum([swap(value, s << low) for s in range(1, 1 << width)], value)
    return value


def turned(mask, groups):
    low = groups[1][0]
    both = (mask >> low) & 3
    return mask ^ ((both ^ (both >> 1) ^ ((both & 1) << 1)) << low)


def slot_masks(groups, turn=False):
    masks = [mask_of(slot, groups) for slot in range(1 << sum(width for _, width in groups[1:]))]
    return [turned(mask, groups) for mask in masks] if turn else masks


def in_order(parts, masks, place):
    found = [mask for part in masks for mask in part]
    slots = [0] * len(found)
    for slot, mask in enumerate(found):
        slots[mask] = slot
    devices = jnp.arange(len(found), dtype=jnp.int32)
    return jnp.take(join(parts), jnp.asarray(slots, jnp.int32)[place ^ devices], axis=0)


def by_slot(parts, place, groups):
    masks = jnp.asarray(slot_masks(groups), jnp.int32)
    return [jnp.take(parts, place ^ (masks | bit), axis=0) for bit in range(2)]


def adapt_kernel(rows, copies, *refs):
    count = len(rows)
    inputs, outputs = refs[: 4 * count + 1], refs[4 * count + 1 :]
    sum_ref = outputs[3 * count]
    sum_ref[...] = inputs[-1][...]
    half = sum_ref.shape[0] // 2
    correct = 1.0 - BETA**STEP
    for number, row in enumerate(rows):
        grad_ref, first_ref, second_ref, weight_ref = inputs[4 * number : 4 * number + 4]
        moment_ref, square_ref, update_ref = outputs[3 * number : 3 * number + 3]
        planes = weight_ref.shape[0] if len(weight_ref.shape) == 3 else 1
        width = weight_ref.shape[-1]
        norms = []
        for n in range(planes):
            at = n if len(weight_ref.shape) == 3 else Ellipsis
            if len(grad_ref.shape) == 3:
                grad = jnp.sum(grad_ref[...], axis=0)[: weight_ref.shape[0], :width]
            else:
                grad = grad_ref[:, n * width : (n + 1) * width]
            moment = BETA * first_ref[at] + (1.0 - BETA) * grad
            square = BETA * second_ref[at] + (1.0 - BETA) * grad * grad
            weight = weight_ref[at]
            update = moment / correct / (jnp.sqrt(square / correct) + ADAM_EPS) + DECAY * weight
            moment_ref[at] = moment
            square_ref[at] = square
            update_ref[at] = update
            norms.append([jnp.sum(v * v, axis=1, keepdims=True) for v in (weight, update)])
        for n in range(2):
            norm = sum(both[n] for both in norms)
            if row < 4:
                norm = total(norm)
            place = n * half + row
            sum_ref[place : place + norm.shape[0], :] = jnp.broadcast_to(norm, (norm.shape[0], 128))
    if copies:
        outputs[-1][...] = jnp.broadcast_to(diagonal(sum_ref[...]), outputs[-1].shape)


def diagonal(values):
    row = lax.broadcasted_iota(jnp.int32, values.shape, 0)
    lane = lax.broadcasted_iota(jnp.int32, values.shape, 1)
    return total(jnp.where(row == lane, values, 0.0))


def adapt(states, rows, sums=None, copies=0):
    if sums is None:
        sums = jnp.zeros((32, 128), F32)
    operands = [array for state in states for array in state] + [sums]
    shapes = [state[3].shape for state in states for _ in range(3)] + [sums.shape]
    if copies:
        shapes.append((copies, 8, 128))
    found = pl.pallas_call(
        lambda *refs: adapt_kernel(rows, copies, *refs),
        grid=(1,),
        in_specs=[whole(a.shape) for a in operands],
        out_specs=[pl.BlockSpec(s, lambda *_, n=len(s): (0,) * n) for s in shapes],
        out_shape=[jax.ShapeDtypeStruct(s, F32) for s in shapes],
        compiler_params=params(),
        cost_estimate=cost(4),
        name="adapt",
    )(*operands)
    return [found[3 * n : 3 * n + 3] for n in range(len(states))], found[-1]


def master_kernel(sum_ref, *refs):
    *refs, trust_ref = refs
    count = len(refs) // 3
    width = trust_ref.shape[1]
    if len(sum_ref.shape) == 3:
        line = jnp.sum(sum_ref[...], axis=0)[:1]
    else:
        line = diagonal(sum_ref[...])
    norms = [jnp.sqrt(line[:, n * width : (n + 1) * width]) for n in range(2)]
    ratio = norms[0] / (norms[1] + ADAM_EPS)
    for n, value in enumerate([*norms, ratio]):
        trust_ref[n : n + 1, :] = jnp.log(value)
    for n in range(count):
        update_ref, weight_ref, out_ref = refs[n], refs[count + n], refs[2 * count + n]
        if n < 4:
            scale = RATE * ratio[:, n : n + 1]
        else:
            shape = (weight_ref.shape[0], width)
            row = lax.broadcasted_iota(jnp.int32, shape, 0)
            lane = lax.broadcasted_iota(jnp.int32, shape, 1)
            picked = jnp.where(lane == row + 4, jnp.broadcast_to(ratio, shape), 0.0)
            scale = RATE * jnp.sum(picked, axis=1, keepdims=True)
        for at in range(weight_ref.shape[0]) if len(weight_ref.shape) == 3 else [Ellipsis]:
            out_ref[at] = weight_ref[at] - scale * update_ref[at]


def master(sums, updates, weights, width):
    arrays = [sums, *updates, *weights]
    shapes = [a.shape for a in weights] + [(3, width)]
    return pl.pallas_call(
        master_kernel,
        grid=(1,),
        in_specs=[whole(a.shape) for a in arrays],
        out_specs=[pl.BlockSpec(s, lambda *_, n=len(s): (0,) * n) for s in shapes],
        out_shape=[jax.ShapeDtypeStruct(s, F32) for s in shapes],
        compiler_params=params(),
        cost_estimate=cost(3),
        name="master",
    )(*arrays)


def halves(parts, groups):
    return by_slot(parts, jnp.int32(0), groups)


def by_index(keep, send, groups, turn=False):
    masks = slot_masks(groups, turn)
    return in_order([keep, send], [masks, [mask | 1 for mask in masks]], jnp.int32(0))


def join_heads(pieces):
    nb, nh, rows, flat = pieces.shape
    wider = nb * nh // PARTS
    parts = pieces.reshape(nb // wider, wider, nh, rows, flat).transpose(0, 2, 1, 3, 4)
    return parts.reshape(PARTS, wider * rows, flat)


def join_parts(parts, nh):
    count = lax.axis_size("batch") * lax.axis_size("head")
    wider = count // PARTS
    _, rows, flat = parts.shape
    parts = parts.reshape(PARTS // nh, nh, wider, rows // wider, flat).transpose(0, 2, 1, 3, 4)
    return parts.reshape(count, rows // wider, flat)


def shards(
    block_input,
    cotangent,
    segment_lengths,
    thought_counts,
    packing_mask,
    attend_weight,
    output_weight,
    expand_weight,
    reduce_weight,
    vectors,
    first_attend,
    first_output,
    first_expand,
    first_reduce,
    first_vectors,
    second_attend,
    second_output,
    second_expand,
    second_reduce,
    second_vectors,
):
    nb, nh = lax.axis_size("batch"), lax.axis_size("head")
    count = nb * nh
    groups, kernel_groups = bit_groups(count), bit_groups(PARTS)
    same = count == PARTS
    place = (lax.axis_index("batch") * nh + lax.axis_index("head")).astype(jnp.int32)
    core = place % 2
    kernel_place = (place if same else jnp.zeros_like(place)).reshape(1)
    rows, length, model = block_input.shape
    tokens = rows * length
    hidden = expand_weight.shape[1]
    own_in, _, own_out = attend_weight.shape
    own = output_weight.shape[0]
    own_red = reduce_weight.shape[0]
    cols = vectors.shape[1]
    wide = hidden // model
    flat = 3 * own_out

    extra = jnp.pad(vectors.astype(BF16).T, ((0, -cols % 16), (0, flat - own)))
    piece = jnp.concatenate([attend_weight.astype(BF16).reshape(own_in, flat), extra], axis=0)
    attend_far = gather_far(piece, groups)

    blocks = expand_weight.astype(BF16).reshape(own, 2, wide // 2, model).transpose(1, 2, 0, 3)
    beside = swap(jnp.where(core == 0, blocks[1], blocks[0]), 1)
    mine = jnp.where(core == 0, blocks[0], blocks[1])
    piece = [
        jnp.concatenate(
            [jnp.where(core == 0, mine, beside), jnp.where(core == 0, beside, mine)], axis=1
        ).reshape(2 * own * (wide // 2), model),
        reduce_weight.astype(BF16),
        output_weight.astype(BF16),
    ]
    pad = -(own_red + own) % 16
    piece = jnp.concatenate(piece + [jnp.zeros((pad, model), BF16)], axis=0)
    late_all = lax.all_gather(piece, AXES, axis=0, tiled=False)
    attend_own = cross(attend_far, groups[1])
    attend_other = swap(attend_own, 1)
    if not same:
        masks = slot_masks(groups)
        attend = in_order([attend_own, attend_other], [masks, [m | 1 for m in masks]], place)
        vec = attend[:, own_in:, :own].transpose(1, 0, 2).reshape(-1, PARTS, model // PARTS)
        vec = jnp.pad(vec.transpose(1, 0, 2), ((0, 0), (0, 0), (0, flat - model // PARTS)))
        attend = join_heads(attend[:, :own_in].reshape(nb, nh, own_in, flat))
        attend_own, attend_other = halves(
            jnp.concatenate([attend, vec], axis=1), kernel_groups
        )

    own_lengths = lax.dynamic_slice_in_dim(
        segment_lengths, lax.axis_index("head") * rows, rows, 0
    )
    own_counts = lax.dynamic_slice_in_dim(thought_counts, lax.axis_index("head") * rows, rows, 0)
    start_of, weight_rows = row_facts(own_lengths, own_counts, packing_mask, length)
    start_of = start_of.reshape(rows, 1, length)
    weight_rows = weight_rows.reshape(tokens, 1)

    x = block_input.reshape(tokens, model)
    cot = cotangent.reshape(tokens, model)
    normed_low, qkv, attend_low, vec = project(
        kernel_place, x, attend_own, attend_other, nh, cols
    )
    context, probs = attend_forward(start_of, qkv, length)
    if not same:
        late = late_all
        both, per = 2 * own, 2 * model // PARTS
        expand_low = (
            late[:, : both * wide // 2]
            .reshape(count // 2, 2, wide // 2, both, model)
            .transpose(1, 2, 0, 3, 4)
            .reshape(2, wide // 2, PARTS // 2, per, model)
            .transpose(2, 0, 1, 3, 4)
            .reshape(PARTS, per * (wide // 2), model)
        )
        low = both * wide // 2
        rest = [
            expand_low,
            late[:, low : low + own_red].reshape(PARTS, hidden // PARTS, model),
            late[:, low + own_red : low + own_red + own].reshape(PARTS, per // 2, model),
            jnp.zeros((PARTS, 8, model), BF16),
        ]
        late_all = jnp.concatenate(rest, axis=1)
    late = (late_all,)
    hidden_states, middle, middle_low, activated, slope, branch = mlp_forward(
        late, context, x, cot, weight_rows, vec, hidden
    )

    def for_devices(keep, send, split):
        parts = [by_index(*both, kernel_groups, n == 1) for n, both in enumerate(zip(keep, send))]
        return by_slot(split(jnp.concatenate(parts, axis=1)), place, groups)

    def split_mid(parts):
        per = 2 * model // PARTS
        expand = (
            jnp.stack([parts[:, :per], parts[:, per + 32 :]], axis=1)
            .reshape(PARTS // 2, 2, 2, per, model)
            .transpose(1, 2, 0, 3, 4)
            .reshape(2, 2, count // 2, 2 * own, model)
            .transpose(2, 0, 1, 3, 4)
            .reshape(count, 4 * own, model)
        )
        output = parts[:, per : per + per // 2].reshape(count, own, model)
        return jnp.concatenate([expand, output], axis=1)

    red_keep, red_send = reduce_weight_grad(kernel_place, activated, branch)
    if same:
        cot, *red_send = ordered(cot, *red_send)
        red = Halves(red_keep, red_send, groups)
    grad_pre, grad_middle, grad_attn, grad_context, mid_sums = mlp_backward(
        late, cot, weight_rows, middle, slope, vec
    )
    if same:
        grad_pre, *terms = ordered(grad_pre, *red.flat())
        red.set(terms)
        grad_pre, *sends = ordered(grad_pre, *red.sends())
        red_received = red.receive(sends)

    mid_keep, mid_send = mid_weight_grad(
        kernel_place, middle_low, grad_pre, context, grad_attn
    )
    if same:
        grad_context, *terms = ordered(grad_context, *mid_send, *red_received)
        mid = Halves(mid_keep, terms[:2], groups)
        red.add(terms[2:])
        grad_context, *sends = ordered(grad_context, *red.sends())
        red_received = red.receive(sends)

    pairs = model // (2 * HEAD_DIM)
    operands = (qkv, context, grad_context, probs, length)
    d_qkv = attend_backward(*operands, 0, pairs // 2)
    if same:
        d_qkv, *terms = ordered(d_qkv, *mid.flat(), *red_received)
        mid.set(terms[:4])
        red.add(terms[4:])
        d_qkv, *sends = ordered(d_qkv, *mid.sends(), *red.last_sends())
        mid_received = mid.receive(sends[:2])
        red_received = red.last_receive(sends[2:])
    d_qkv = attend_backward(*operands, pairs // 2, rows * pairs, d_qkv)
    if same:
        d_qkv, *terms = ordered(d_qkv, *mid_received, *red_received)
        mid.add(terms[:2])
        red_received = terms[2:]
        d_qkv, *sends = ordered(d_qkv, *mid.sends())
        mid_received = mid.receive(sends)
    att_keep, att_send = attend_weight_grad(kernel_place, normed_low, d_qkv, nh)
    if same:
        att_send, *mid_received = ordered(att_send, *mid_received)
        att = Whole(att_keep, att_send, groups)
        mid.add(mid_received)
        d_qkv, *terms = ordered(d_qkv, *mid.last_sends(), *att.terms)
        att.terms = terms[-2:]
        mid_received = mid.last_receive(terms[:-2])
        d_qkv, *sends = ordered(d_qkv, *att.sends())
        att_received = att.receive(sends)
    grad_input, sums, sum_parts = input_grad(d_qkv, x, grad_middle, attend_low, vec, mid_sums)
    if same:
        sum_parts, *terms = ordered(sum_parts, *att_received, *mid_received)
        att.terms = att.terms + terms[:3]
        att_received = att.last_receive(att.last_sends())
        red_grad, found = red.finish(red_received), mid.finish(terms[3:])
        per = 2 * own
        mid = jnp.concatenate(
            [found[:per], found[per + 32 :], found[per : per + own]], axis=0
        )
    else:
        red_parts = for_devices(
            red_keep, red_send, lambda parts: parts.reshape(count, own_red, model)
        )
        mid_parts = for_devices(mid_keep, mid_send, split_mid)
        att_parts = for_devices(
            [att_keep], [att_send], lambda parts: join_parts(parts, nh).reshape(count, own_in, flat)
        )
        red_grad, mid = scatter(*red_parts, groups), scatter(*mid_parts, groups)
        att_grad = scatter(*att_parts, groups)
    out_grad = mid[4 * own : 5 * own]
    exp_both = mid[: 4 * own].reshape(2, 2, own, model)
    kept = jnp.where(core == 0, exp_both[:, 0], exp_both[:, 1])
    beside = swap(jnp.where(core == 0, exp_both[:, 1], exp_both[:, 0]), 1)
    exp_grad = jnp.stack(
        [jnp.where(core == 0, kept, beside), jnp.where(core == 0, beside, kept)]
    ).reshape(wide, own, model)
    exp_grad = exp_grad.transpose(1, 0, 2).reshape(own, hidden)


    if same:
        vector_grad = lax.all_to_all(sum_parts, AXES, 0, 0, tiled=True)
    else:
        vector_grad = lax.dynamic_slice_in_dim(all_sum(sums, groups), place * own, own, 1)
    late_weights = (output_weight, expand_weight, reduce_weight)
    late_states = [
        (grad, first, second, weight)
        for grad, first, second, weight in zip(
            (out_grad, exp_grad, red_grad),
            (first_output, first_expand, first_reduce),
            (second_output, second_expand, second_reduce),
            late_weights,
        )
    ]
    late_found, late_sums = adapt(late_states, [1, 2, 3])
    if same:
        late_sums, *att_received = ordered(late_sums, *att_received)
        att_grad = att.finish(att_received)

    def planes(state):
        return state.transpose(1, 0, 2)

    found, sums = adapt(
        [
            (att_grad, planes(first_attend), planes(second_attend), planes(attend_weight)),
            (vector_grad, first_vectors.T, second_vectors.T, vectors.T),
        ],
        [0, 4],
        late_sums,
        count if same else 0,
    )
    sums = lax.all_to_all(sums, AXES, 0, 0, tiled=True) if same else all_sum(sums, groups)
    adapted = [list(found[0]), *late_found, [a.T for a in found[1]]]
    *masters, trust_norms = master(
        sums,
        [found[0][2], *[a[2] for a in late_found], found[1][2]],
        [planes(attend_weight), *late_weights, vectors.T],
        4 + cols,
    )
    masters[4] = masters[4].T
    adapted[0] = [planes(a) for a in adapted[0]]
    masters[0] = planes(masters[0])
    return (
        hidden_states.reshape(rows, length, model),
        grad_input.reshape(rows, length, model),
        *[a[0] for a in adapted],
        *[a[1] for a in adapted],
        *masters,
        trust_norms,
    )


def solution(mesh):
    rows = P(AXES, None, None)
    state = [P("batch", None, "head")] + [P(AXES, None)] * 4
    return jax.shard_map(
        shards,
        mesh=mesh,
        in_specs=(rows, rows, P("batch", None), P("batch", None), P(AXES, None), *state * 3),
        out_specs=(rows, rows, *state * 3, P()),
        check_vma=False,
    )
```

```python
import jax
import jax.numpy as jnp
from jax import lax
from jax.experimental import pallas as pl
from jax.experimental.pallas import tpu as pltpu
from jax.sharding import PartitionSpec as P

HEAD_DIM = 64
THOUGHT_TOKENS = 8
STEP = 6
PARTS = 32
SPAN = 256
BLOCK = 128

NORM_EPS = 1e-05
NEGATIVE = -1e30
BETA = 0.5
RATE = 0.5
DECAY = 0.01
ADAM_EPS = 1e-06
AXES = ("batch", "head")
ROOT = 0.7978845608028654
CUBE = 0.044715
F32 = jnp.float32
BF16 = jnp.bfloat16
NT = (((1,), (1,)), ((), ()))
TN = (((0,), (0,)), ((), ()))


def dot(a, b, dims=(((1,), (0,)), ((), ()))):
    return lax.dot_general(a, b, dims, preferred_element_type=F32)


def params(grid=1, vmem=60):
    return pltpu.CompilerParams(
        dimension_semantics=("arbitrary",) * grid, vmem_limit_bytes=vmem * 1024 * 1024
    )


def cost(micros):
    return pl.CostEstimate(flops=int(micros * 0.29e9), bytes_accessed=1 << 18, transcendentals=0)


def whole(shape):
    return pl.BlockSpec(shape, lambda *_: (0,) * len(shape), pipeline_mode=pl.Buffered(1))


SCALARS = pl.BlockSpec(memory_space=pltpu.SMEM)


def row_facts(lengths, counts, mask, span):
    positions = jnp.arange(span, dtype=jnp.int32)
    ends = jnp.cumsum(lengths, axis=-1)
    starts = ends - lengths
    inside = (positions[None, :, None] >= starts[:, None, :]) & (
        positions[None, :, None] < ends[:, None, :]
    )
    start_of = jnp.sum(jnp.where(inside, starts[:, None, :], 0), axis=-1)
    passes = jnp.sum(jnp.where(inside, counts[:, None, :], 0), axis=-1)
    keep = (positions[None, :] - start_of >= THOUGHT_TOKENS * passes) & (mask > 0)
    return start_of, keep.astype(F32)


def windows(length):
    return [
        (low, max(0, low - SPAN), low + BLOCK - max(0, low - SPAN)) for low in range(0, length, BLOCK)
    ]


def fill_caps(start_ref, cap_ref, length):
    for number, (low, first, count) in enumerate(windows(length)):
        key = lax.broadcasted_iota(jnp.int32, (count, BLOCK), 0) + first
        query = lax.broadcasted_iota(jnp.int32, (count, BLOCK), 1) + low
        start = start_ref[0, :, low : low + BLOCK]
        allowed = (key <= query) & (key >= start)
        cap_ref[number, :count] = jnp.where(allowed, 3e38, NEGATIVE)


def cap_of(cap_ref, number, count):
    cap = cap_ref[number, :count]
    return jnp.concatenate([cap, cap], axis=1)


def for_heads(values):
    lane = lax.broadcasted_iota(jnp.int32, (1, 2 * HEAD_DIM), 1)
    return jnp.concatenate(
        [jnp.where(lane < HEAD_DIM, values, 0), jnp.where(lane >= HEAD_DIM, values, 0)], axis=0
    )


def of_heads(values):
    return jnp.concatenate([values[:HEAD_DIM, :BLOCK], values[HEAD_DIM:, BLOCK:]], axis=0)


def in_stages(units, ahead, behind, first, middle, last):
    started, worked = [first(unit) for unit in units[:ahead]], []
    for number, unit in enumerate(units):
        if number + ahead < len(units):
            started.append(first(units[number + ahead]))
        worked.append((unit, middle(unit, started.pop(0))))
        if len(worked) > behind:
            last(*worked.pop(0))
    for both in worked:
        last(*both)


def attend_forward_kernel(fresh, start_ref, q_ref, k_ref, v_ref, o_ref, p_ref, cap_ref):
    length = q_ref.shape[0]
    pl.when(fresh)(lambda: fill_caps(start_ref, cap_ref, length))
    value_t = v_ref[...].T

    def score(unit):
        _, (low, first, count) = unit
        query = for_heads(q_ref[low : low + BLOCK, :] * (HEAD_DIM**-0.5))
        return dot(k_ref[first : first + count, :], query, NT)

    def soften(unit, scores):
        number, (_, _, count) = unit
        scores = jnp.minimum(scores, cap_of(cap_ref, number, count))
        grown = jnp.exp(scores - jnp.max(scores, axis=0, keepdims=True))
        probs = (grown * (1.0 / total(grown))).astype(BF16)
        p_ref[0, 0, number, :count] = probs
        return probs

    def mix(unit, probs):
        _, (low, first, count) = unit
        result = dot(value_t[:, first : first + count], probs)
        o_ref[low : low + BLOCK, :] = of_heads(result).T.astype(BF16)

    in_stages(list(enumerate(windows(length))), 4, 1, score, soften, mix)


def attend_backward_kernel(q_ref, k_ref, v_ref, o_ref, do_ref, p_ref, *rest):
    d_ref = rest[-1]
    length = q_ref.shape[0]
    key_t = k_ref[...].T
    grad_key, grad_value = {}, {}

    def query_of(low):
        return for_heads(q_ref[low : low + BLOCK, :] * (HEAD_DIM**-0.5))

    def grad_of(low):
        return for_heads(do_ref[low : low + BLOCK, :])

    def score(unit):
        _, (low, first, count) = unit
        return dot(v_ref[first : first + count, :], grad_of(low), NT)

    def soften(unit, grad_probs):
        number, (low, _, count) = unit
        product = do_ref[low : low + BLOCK, :].astype(F32) * o_ref[low : low + BLOCK, :].astype(F32)
        product = product.T
        inner = jnp.concatenate([total(product[:HEAD_DIM]), total(product[HEAD_DIM:])], axis=1)
        probs = p_ref[0, 0, number, :count]
        return probs, (probs.astype(F32) * (grad_probs - inner)).astype(BF16)

    def mix(unit, found):
        _, (low, first, count) = unit
        probs, grad_scores = found
        terms = dot(probs, grad_of(low)), dot(grad_scores, query_of(low))
        grad_query = dot(key_t[:, first : first + count], grad_scores)
        d_ref[0, low : low + BLOCK, :] = (of_heads(grad_query).T * (HEAD_DIM**-0.5)).astype(BF16)
        for sums, term, place in ((grad_value, terms[0], 2), (grad_key, terms[1], 1)):
            for at in range(first, first + count, BLOCK):
                one = term[at - first : at - first + BLOCK]
                sums[at] = sums[at] + one if at in sums else one
            for at in list(sums):
                if at <= low - SPAN or low + BLOCK == length:
                    d_ref[place, at : at + BLOCK, :] = sums.pop(at).astype(BF16)

    in_stages(list(enumerate(windows(length))), 2, 0, score, soften, mix)


def attention_specs(length, pairs, low=0):
    pair = 2 * HEAD_DIM

    def at(i):
        return (i + low) // pairs, (i + low) % pairs

    def columns(n):
        return lambda i: (at(i)[0], n * pairs + at(i)[1])

    qkv = [pl.BlockSpec((length, pair), columns(n)) for n in range(3)]
    rows = pl.BlockSpec((length, pair), columns(0))
    probs = pl.BlockSpec((1, 1) + probs_shape(length), lambda i: (*at(i), 0, 0, 0))
    start = pl.BlockSpec((1, 1, length), lambda i: (at(i)[0], 0, 0))
    return start, qkv, rows, probs, lambda i: (0, *at(i))


def probs_shape(length):
    return (length // BLOCK, SPAN + BLOCK, 2 * BLOCK)


def attend_forward(start, qkv, length):
    tokens, model = qkv.shape[0], qkv.shape[1] // 3
    pairs = model // (2 * HEAD_DIM)
    rows = tokens // length
    start_spec, qkv_specs, row_spec, probs_spec, _ = attention_specs(length, pairs)

    def kernel(*refs):
        attend_forward_kernel(pl.program_id(0) % pairs == 0, *refs)

    return pl.pallas_call(
        kernel,
        grid=(rows * pairs,),
        in_specs=[start_spec] + qkv_specs,
        out_specs=[row_spec, probs_spec],
        out_shape=[
            jax.ShapeDtypeStruct((tokens, model), BF16),
            jax.ShapeDtypeStruct((rows, pairs) + probs_shape(length), BF16),
        ],
        scratch_shapes=[pltpu.VMEM((length // BLOCK, SPAN + BLOCK, BLOCK), F32)],
        compiler_params=params(),
        cost_estimate=cost(18),
        name="attend_forward",
    )(start, qkv, qkv, qkv)


def attend_backward(qkv, out, grad, probs, length, low, high, before=None):
    tokens, model = out.shape
    pairs = model // (2 * HEAD_DIM)
    _, qkv_specs, row_spec, probs_spec, at = attention_specs(length, pairs, low)
    operands = [qkv, qkv, qkv, out, grad, probs]
    in_specs = qkv_specs + [row_spec, row_spec, probs_spec]
    aliases = {}
    if before is not None:
        aliases = {len(operands): 0}
        operands.append(before)
        in_specs.append(pl.BlockSpec(memory_space=pl.ANY))
    return pl.pallas_call(
        attend_backward_kernel,
        grid=(high - low,),
        in_specs=in_specs,
        out_specs=pl.BlockSpec((3, length, 2 * HEAD_DIM), at),
        out_shape=jax.ShapeDtypeStruct((3, tokens, model), BF16),
        input_output_aliases=aliases,
        compiler_params=params(),
        cost_estimate=cost(2.0 * (high - low)),
        name="attend_backward",
    )(*operands)


def normalize(values):
    centre = values - jnp.mean(values, axis=-1, keepdims=True)
    factor = lax.rsqrt(jnp.mean(centre * centre, axis=-1, keepdims=True) + NORM_EPS)
    return centre * factor, factor


def norm_back(inner, normed, factor):
    return factor * (
        inner
        - jnp.mean(inner, axis=-1, keepdims=True)
        - normed * jnp.mean(inner * normed, axis=-1, keepdims=True)
    )


def total(values):
    return jnp.sum(values, axis=0, keepdims=True)


def project_kernel(place_ref, x_ref, own_ref, other_ref, nl_ref, qkv_ref, w_ref, vec_ref, *, heads):
    slots, rows, flat = own_ref.shape
    rows -= -(-vec_ref.shape[0] // 16) * 16
    part, model = flat // 3, x_ref.shape[1]
    groups = bit_groups(2 * slots)
    place = place_ref[0]

    @pl.when(pl.program_id(0) == 0)
    def _():
        for here in range(heads):

            @pl.when(place % heads == here)
            def _(here=here):
                for bit, ref in enumerate((own_ref, other_ref)):
                    for slot in range(slots):
                        mask = mask_of(slot, groups) | bit
                        head = here ^ (mask % heads)
                        row = pl.multiple_of(((place ^ mask) // heads) * rows, rows)
                        for j in range(3):
                            low = j * model + head * part
                            w_ref[pl.ds(row, rows), low : low + part] = ref[
                                slot, :rows, j * part : (j + 1) * part
                            ]

        count, each = vec_ref.shape[0], model // (2 * slots)
        lane = lax.broadcasted_iota(jnp.int32, (1, model), 1)
        found = jnp.zeros((count, model), F32)
        for bit, ref in enumerate((own_ref, other_ref)):
            for slot in range(slots):
                device = place ^ (mask_of(slot, groups) | bit)
                piece = ref[slot, rows:, :128].astype(F32)[:count]
                piece = jnp.concatenate([piece] * (model // 128), axis=1)
                piece = pltpu.roll(piece, (device * each) % 128, 1)
                inside = (lane >= device * each) & (lane < (device + 1) * each)
                found = jnp.where(inside, piece, found)
        vec_ref[...] = found

    normed, _ = normalize(x_ref[...].astype(F32))
    low = (normed * vec_ref[0:1, :] + vec_ref[1:2, :]).astype(BF16)
    nl_ref[...] = low
    for j in range(3):
        side = slice(j * model, (j + 1) * model)
        result = dot(low, w_ref[:, side])
        if j != 1:
            result = result + vec_ref[2 + j // 2 : 3 + j // 2, :]
        qkv_ref[:, side] = result.astype(BF16)


def project(place, x, own, other, heads, cols, tile=512):
    tokens, model = x.shape
    row = pl.BlockSpec((tile, model), lambda i: (i, 0))
    return pl.pallas_call(
        lambda *refs: project_kernel(*refs, heads=heads),
        grid=(tokens // tile,),
        in_specs=[SCALARS, row, whole(own.shape), whole(other.shape)],
        out_specs=[
            row,
            pl.BlockSpec((tile, 3 * model), lambda i: (i, 0)),
            pl.BlockSpec((model, 3 * model), lambda i: (0, 0)),
            pl.BlockSpec((cols, model), lambda i: (0, 0)),
        ],
        out_shape=[
            jax.ShapeDtypeStruct((tokens, model), BF16),
            jax.ShapeDtypeStruct((tokens, 3 * model), BF16),
            jax.ShapeDtypeStruct((model, 3 * model), BF16),
            jax.ShapeDtypeStruct((cols, model), F32),
        ],
        compiler_params=params(),
        cost_estimate=cost(14),
        name="project",
    )(place, x, own, other)


class Late:
    def __init__(self, refs, scratch):
        (self.parts,) = refs
        self.expand, self.reduce, self.output, self.stage, self.sem = scratch
        self.model = self.output.shape[1]
        self.chunks = self.expand.shape[0]

    def copies(self):
        per = self.model // self.stage.shape[1]
        red = self.reduce.shape[0] // (2 * self.stage.shape[1])
        end = 2 * per + red
        for device in range(self.parts.shape[0]):
            row, bit = (device // 2) * per, device % 2
            for n in range(2):
                yield (
                    self.parts.at[device, n * per : (n + 1) * per],
                    self.expand.at[2 * bit + n, row : row + per],
                )
            yield (
                self.parts.at[device, 2 * per : end],
                self.reduce.at[device * red : (device + 1) * red],
            )
            yield (
                self.parts.at[device, end : end + self.stage.shape[2]],
                self.stage.at[bit, device // 2],
            )

    def load(self):
        copies = [pltpu.make_async_copy(a, b, self.sem) for a, b in self.copies()]
        for copy in copies:
            copy.start()
        for copy in copies:
            copy.wait()
        slots = self.stage.shape[1]
        per = self.model // slots
        for n in range(slots):
            both = [self.stage[bit, n, : per // 2, :].astype(F32) for bit in range(2)]
            self.output[n * per : (n + 1) * per, :] = jnp.concatenate(both, axis=0).astype(BF16)

    def reduce_rows(self, c):
        return self.reduce[c * self.model : (c + 1) * self.model, :]

    @staticmethod
    def specs():
        return [pl.BlockSpec(memory_space=pl.ANY)]

    @staticmethod
    def scratch(late, hidden):
        slots, _, model = late[0].shape
        slots //= 2
        return [
            pltpu.VMEM((hidden // model, model, model), BF16),
            pltpu.VMEM((hidden, model), BF16),
            pltpu.VMEM((model, model), BF16),
            pltpu.VMEM((2, slots, 32, model), BF16),
            pltpu.SemaphoreType.DMA,
        ]


def mlp_forward_kernel(*refs):
    late = Late(refs[:-16], refs[-5:])
    ctx_ref, x_ref, cot_ref, wt_ref, vec_ref = refs[-16:-11]
    hid_ref, mid_ref, nm_ref, act_ref, dg_ref, gb_ref = refs[-11:-5]
    model = late.model
    pl.when(pl.program_id(0) == 0)(late.load)
    middle = x_ref[...].astype(F32) + dot(ctx_ref[...], late.output[...]) + vec_ref[4:5, :]
    mid_ref[...] = middle
    gb_ref[...] = (cot_ref[...].astype(F32) * wt_ref[...]).astype(BF16)
    normed, _ = normalize(middle)
    low = (normed * vec_ref[5:6, :] + vec_ref[6:7, :]).astype(BF16)
    nm_ref[...] = low
    result = middle + vec_ref[7:8, :]
    for c in range(late.chunks):
        side = slice(c * model, (c + 1) * model)
        pre = dot(low, late.expand[c]) + vec_ref[8 + c : 9 + c, :]
        square = pre * pre
        half = 0.5 + 0.5 * jnp.tanh(pre * (ROOT + (ROOT * CUBE) * square))
        act = pre * half
        dg = half + act * (1.0 - half) * (2.0 * ROOT + (6.0 * ROOT * CUBE) * square)
        dg_ref[:, side] = dg.astype(BF16)
        act = act.astype(BF16)
        act_ref[:, side] = act
        result = result + dot(act, late.reduce_rows(c))
    hid_ref[...] = result.astype(BF16)


def mlp_forward(late, ctx, x, cot, wt, vec, hidden, tile=256):
    tokens, model = x.shape
    row = pl.BlockSpec((tile, model), lambda i: (i, 0))
    wide = pl.BlockSpec((tile, hidden), lambda i: (i, 0))
    one = pl.BlockSpec((tile, 1), lambda i: (i, 0))

    def shape(width, kind=BF16):
        return jax.ShapeDtypeStruct((tokens, width), kind)

    return pl.pallas_call(
        mlp_forward_kernel,
        grid=(tokens // tile,),
        in_specs=Late.specs() + [row, row, row, one, whole(vec.shape)],
        out_specs=[row, row, row, wide, wide, row],
        out_shape=[
            shape(model), shape(model, F32), shape(model), shape(hidden), shape(hidden), shape(model),
        ],
        scratch_shapes=Late.scratch(late, hidden),
        compiler_params=params(),
        cost_estimate=cost(40),
        name="mlp_forward",
    )(*late, ctx, x, cot, wt, vec)


def mlp_backward_kernel(*refs):
    late = Late(refs[:-15], refs[-5:])
    cot_ref, wt_ref, mid_ref, dg_ref, vec_ref = refs[-15:-10]
    gpre_ref, gm_ref, ga_ref, gc_ref, sum_ref = refs[-10:-5]
    model = late.model

    @pl.when(pl.program_id(0) == 0)
    def _():
        late.load()
        sum_ref[...] = jnp.zeros_like(sum_ref)

    grad_out = cot_ref[...].astype(F32) * wt_ref[...]
    branch = grad_out.astype(BF16)
    sum_ref[3:4, :] += total(branch.astype(F32))
    back = None
    for c in range(late.chunks):
        side = slice(c * model, (c + 1) * model)
        grad = (dot(branch, late.reduce_rows(c), NT) * dg_ref[:, side].astype(F32)).astype(BF16)
        gpre_ref[:, side] = grad
        sum_ref[4 + c : 5 + c, :] += total(grad.astype(F32))
        term = dot(grad, late.expand[c], NT)
        back = term if back is None else back + term
    normed, factor = normalize(mid_ref[...])
    sum_ref[1:2, :] += total(back * normed)
    sum_ref[2:3, :] += total(back)
    grad_middle = grad_out + norm_back(back * vec_ref[5:6, :], normed, factor)
    gm_ref[...] = grad_middle
    low = grad_middle.astype(BF16)
    ga_ref[...] = low
    sum_ref[0:1, :] += total(low.astype(F32))
    gc_ref[...] = dot(low, late.output[...], NT).astype(BF16)


def mlp_backward(late, cot, wt, mid, dg, vec, tile=256):
    tokens, model = cot.shape
    hidden = dg.shape[1]
    row = pl.BlockSpec((tile, model), lambda i: (i, 0))
    wide = pl.BlockSpec((tile, hidden), lambda i: (i, 0))
    one = pl.BlockSpec((tile, 1), lambda i: (i, 0))

    def shape(width, kind=BF16):
        return jax.ShapeDtypeStruct((tokens, width), kind)

    return pl.pallas_call(
        mlp_backward_kernel,
        grid=(tokens // tile,),
        in_specs=Late.specs() + [row, one, row, wide, whole(vec.shape)],
        out_specs=[wide, row, row, row, pl.BlockSpec((8, model), lambda i: (0, 0))],
        out_shape=[
            shape(hidden), shape(model, F32), shape(model), shape(model),
            jax.ShapeDtypeStruct((8, model), F32),
        ],
        scratch_shapes=Late.scratch(late, hidden),
        compiler_params=params(),
        cost_estimate=cost(36),
        name="mlp_backward",
    )(*late, cot, wt, mid, dg, vec)


def put_parts(place, outs, pieces, turn=False):
    groups = bit_groups(2 * outs[0].shape[0])
    for bit in range(2):

        @pl.when(place % 2 == bit)
        def _(bit=bit):
            for device, index, value in pieces:
                mask = place ^ device
                slot = slot_of(turned(mask, groups) if turn else mask, groups)
                outs[(device % 2) ^ bit][(slot,) + index] = value


class Outbox:
    def __init__(self, place, outs, buffer, sems, turn):
        self.place, self.outs, self.buffer, self.sems, self.turn = place, outs, buffer, sems, turn

    def begin(self, step, rows, count):
        @pl.when(step >= 2)
        def _():
            self.wait(step, rows, count)

    def wait(self, step, rows, count):
        for n in range(count):
            part = self.buffer.at[step % 2, n * rows : (n + 1) * rows]
            pltpu.make_async_copy(part, part, self.sems.at[step % 2]).wait()

    def send(self, step, pieces):
        groups = bit_groups(2 * self.outs[0].shape[0])
        for bit in range(2):

            @pl.when(self.place % 2 == bit)
            def _(bit=bit):
                for low, rows, odd, device, kind, there in pieces:
                    mask = self.place ^ device
                    mask = turned(mask, groups) if self.turn[kind] else mask
                    out = self.outs[2 * (odd ^ bit) + kind].at[slot_of(mask, groups)]
                    pltpu.make_async_copy(
                        self.buffer.at[step % 2, low : low + rows],
                        out.at[there : there + rows],
                        self.sems.at[step % 2],
                    ).start()


def reduce_weight_grad_kernel(place_ref, a_ref, b_ref, *rest):
    *outs, buffer, sems = rest
    slots, rows, model = outs[0].shape
    step, last = pl.program_id(0), pl.num_programs(0) - 1
    count = model // rows
    box = Outbox(place_ref[0], outs, buffer, sems, (False, True))
    result = dot(a_ref[...], b_ref[...], TN).astype(BF16)
    box.begin(step, rows, count)
    buffer[step % 2] = result
    box.send(
        step,
        [(n * rows, rows, n // 2 % 2, step * (count // 2) + n // 2, n % 2, 0) for n in range(count)],
    )

    @pl.when(step == last)
    def _():
        box.wait(step + 1, rows, count)
        box.wait(step, rows, count)


def hbm_outs_of(*shapes):
    return dict(
        out_specs=[pl.BlockSpec(memory_space=pl.ANY)] * len(shapes),
        out_shape=[jax.ShapeDtypeStruct(shape, BF16) for shape in shapes],
    )


def outs_of(*shapes):
    return dict(
        out_specs=[pl.BlockSpec(shape, lambda *_: (0,) * len(shape)) for shape in shapes],
        out_shape=[jax.ShapeDtypeStruct(shape, BF16) for shape in shapes],
    )


def reduce_weight_grad(place, act, branch):
    tokens, model = branch.shape
    hidden = act.shape[1]
    shape = (PARTS // 2, hidden // PARTS // 2, model)
    found = pl.pallas_call(
        reduce_weight_grad_kernel,
        grid=(hidden // model,),
        in_specs=[SCALARS, pl.BlockSpec((tokens, model), lambda i: (0, i)), whole(branch.shape)],
        **hbm_outs_of(*[shape] * 4),
        scratch_shapes=[pltpu.VMEM((2, model, model), BF16), pltpu.SemaphoreType.DMA((2,))],
        compiler_params=params(),
        cost_estimate=cost(15),
        name="reduce_weight_grad",
    )(place, act, branch)
    return found[:2], found[2:]


def mid_weight_grad_kernel(place_ref, nm_ref, gpre_ref, ctx_hbm, ga_hbm, *rest):
    *outs, ctx_ref, ga_ref, buffer, sems, out_sems = rest
    copies = [
        pltpu.make_async_copy(ctx_hbm, ctx_ref, sems.at[0]),
        pltpu.make_async_copy(ga_hbm, ga_ref, sems.at[1]),
    ]
    slots, rows, model = outs[0].shape
    per = model // slots
    step = pl.program_id(0)
    last = pl.num_programs(0) - 1
    box = Outbox(place_ref[0], outs, buffer, out_sems, (False, True))

    @pl.when(step == 1)
    def _():
        for copy in copies:
            copy.start()

    for c in range(4):

        @pl.when(step == c)
        def _(c=c):
            result = dot(nm_ref[...], gpre_ref[...], TN).astype(BF16)
            if c >= 2:
                box.wait(c, per, slots)
            buffer[c % 2, :model] = result
            box.send(
                c, [(n * per, per, c // 2, 2 * n + c // 2, c % 2, 0) for n in range(slots)]
            )

    @pl.when(step == last)
    def _():
        for copy in copies:
            copy.wait()
        result = dot(ctx_ref[...], ga_ref[...], TN)
        half, tall = per // 2, rows - per
        empty = jnp.zeros((tall - half, model), F32)
        box.wait(4, per, slots)
        for n in range(2 * slots):
            both = jnp.concatenate([result[n * half : (n + 1) * half], empty], axis=0)
            buffer[0, n * tall : (n + 1) * tall] = both.astype(BF16)
        box.send(4, [(n * tall, tall, n % 2, n, 0, per) for n in range(2 * slots)])
        box.wait(3, per, slots)
        box.wait(4, tall, 2 * slots)


def mid_weight_grad(place, nm, gpre, ctx, ga):
    tokens, model = nm.shape
    hidden = gpre.shape[1]
    assert hidden == 4 * model
    slots, per = PARTS // 2, 2 * model // PARTS
    shapes = [(slots, per + 32, model), (slots, per, model)]
    found = pl.pallas_call(
        mid_weight_grad_kernel,
        grid=(5,),
        in_specs=[
            SCALARS,
            whole(nm.shape),
            pl.BlockSpec((tokens, model), lambda i: (0, jnp.minimum(i, 3))),
            pl.BlockSpec(memory_space=pl.ANY),
            pl.BlockSpec(memory_space=pl.ANY),
        ],
        **hbm_outs_of(*shapes * 2),
        scratch_shapes=[
            pltpu.VMEM(ctx.shape, BF16),
            pltpu.VMEM(ga.shape, BF16),
            pltpu.VMEM((2, 32 * PARTS, model), BF16),
            pltpu.SemaphoreType.DMA((2,)),
            pltpu.SemaphoreType.DMA((2,)),
        ],
        compiler_params=params(),
        cost_estimate=cost(19),
        name="mid_weight_grad",
    )(place, nm, gpre, ctx, ga)
    return found[:2], found[2:]


def attend_weight_grad_kernel(place_ref, a_ref, b_ref, keep_ref, send_ref, *, heads):
    slots, rows, flat = keep_ref.shape
    part = flat // 3
    result = dot(a_ref[...], b_ref[0], TN).astype(BF16)
    for j in range(3):

        @pl.when(pl.program_id(0) == j)
        def _(j=j):
            put_parts(
                place_ref[0],
                (keep_ref, send_ref),
                [
                    (
                        d,
                        (slice(None), slice(j * part, (j + 1) * part)),
                        result[
                            d // heads * rows : (d // heads + 1) * rows,
                            d % heads * part : (d % heads + 1) * part,
                        ],
                    )
                    for d in range(2 * slots)
                ],
            )


def attend_weight_grad(place, nl, d_qkv, heads):
    tokens, model = nl.shape
    return pl.pallas_call(
        lambda *refs: attend_weight_grad_kernel(*refs, heads=heads),
        grid=(3,),
        in_specs=[SCALARS, whole(nl.shape), pl.BlockSpec((1, tokens, model), lambda j: (j, 0, 0))],
        **outs_of(*[(PARTS // 2, model * heads // PARTS, 3 * model // heads)] * 2),
        compiler_params=params(),
        cost_estimate=cost(13),
        name="attend_weight_grad",
    )(place, nl, d_qkv)


def input_grad_kernel(d_ref, x_ref, gm_ref, w_ref, vec_ref, mid_ref, out_ref, sum_ref, part_ref):
    model = x_ref.shape[1]

    @pl.when(pl.program_id(0) == 0)
    def _():
        sum_ref[:4, :] = jnp.zeros((4, model), F32)
        sum_ref[4:, :] = mid_ref[...]

    back = None
    for j in range(3):
        term = dot(d_ref[j], w_ref[:, j * model : (j + 1) * model], NT)
        back = term if back is None else back + term
    normed, factor = normalize(x_ref[...].astype(F32))
    sum_ref[0:1, :] += total(back * normed)
    sum_ref[1:2, :] += total(back)
    sum_ref[2:3, :] += total(d_ref[0].astype(F32))
    sum_ref[3:4, :] += total(d_ref[2].astype(F32))
    out_ref[...] = (gm_ref[...] + norm_back(back * vec_ref[0:1, :], normed, factor)).astype(BF16)

    @pl.when(pl.program_id(0) == pl.num_programs(0) - 1)
    def _():
        count = part_ref.shape[0]
        each = model // count
        part_ref[...] = jnp.zeros_like(part_ref)
        for n in range(count):
            part_ref[n, : sum_ref.shape[0], :each] = sum_ref[:, n * each : (n + 1) * each]


def input_grad(d_qkv, x, gm, w, vec, mid_sums, tile=512):
    tokens, model = x.shape
    row = pl.BlockSpec((tile, model), lambda i: (i, 0))
    return pl.pallas_call(
        input_grad_kernel,
        grid=(tokens // tile,),
        in_specs=[
            pl.BlockSpec((3, tile, model), lambda i: (0, i, 0)), row, row,
            whole(w.shape), whole(vec.shape), whole(mid_sums.shape),
        ],
        out_specs=[
            row,
            pl.BlockSpec(vec.shape, lambda i: (0, 0)),
            pl.BlockSpec((PARTS, 16, 128), lambda i: (0, 0, 0)),
        ],
        out_shape=[
            jax.ShapeDtypeStruct((tokens, model), BF16),
            jax.ShapeDtypeStruct(vec.shape, F32),
            jax.ShapeDtypeStruct((PARTS, 16, 128), F32),
        ],
        compiler_params=params(),
        cost_estimate=cost(16),
        name="input_grad",
    )(d_qkv, x, gm, w, vec, mid_sums)


def bit_groups(count):
    bits = count.bit_length() - 1
    assert count == 1 << bits
    return [(0, 1)] + [(low, min(2, bits - low)) for low in range(1, bits, 2)]


def slot_of(mask, groups):
    slot = 0
    for low, width in groups[1:]:
        slot = slot * (1 << width) + ((mask >> low) & ((1 << width) - 1))
    return slot


def mask_of(slot, groups):
    mask = 0
    for low, width in groups[:0:-1]:
        mask |= (slot & ((1 << width) - 1)) << low
        slot >>= width
    return mask


def swap(value, mask):
    count = lax.axis_size("batch") * lax.axis_size("head")
    return lax.ppermute(value, AXES, [(i, i ^ mask) for i in range(count)])


def spread(piece, group):
    low, width = group
    return [piece] + [swap(piece, step << low) for step in range(1, 1 << width)]


def join(parts):
    return jnp.concatenate(parts, axis=0)


def gather_far(piece, groups):
    piece = piece[None]
    for group in groups[:1:-1]:
        piece = join(spread(piece, group))
    return piece


def cross(pieces, group):
    count, rows = pieces.shape[0], pieces.shape[1] // 2
    low, high = 1 << group[0], 2 << group[0]
    first, second = pieces[:, :rows], pieces[:, rows:]
    received = swap(first, high), swap(second, low)
    first, second = join([first, received[0]]), join([second, received[1]])
    others = swap(first, low), swap(second, high)
    first = join([first[:count], others[0][:count], first[count:], others[0][count:]])
    return jnp.concatenate([first, join([second, others[1]])], axis=1)


def ordered(*values):
    return lax.optimization_barrier(values)


class Halves:
    def __init__(self, keep, send, groups):
        self.groups = groups
        self.bits = [2 << groups[1][0], 1 << groups[1][0]]
        self.terms = [[kept, swap(sent, 1)] for kept, sent in zip(keep, send)]
        self.count = keep[0].shape[0]

    def flat(self):
        return [t for terms in self.terms for t in terms]

    def set(self, flat):
        count = len(self.terms[0])
        self.terms = [list(flat[:count]), list(flat[count:])]

    def sends(self):
        self.count //= 2
        here = slice(self.count, 2 * self.count)
        return [added([t[here] for t in terms]).astype(BF16) for terms in self.terms]

    def receive(self, sends):
        received = [swap(send, bit) for send, bit in zip(sends, self.bits)]
        self.bits = self.bits[::-1]
        return received

    def add(self, received):
        self.terms = [terms + [one] for terms, one in zip(self.terms, received)]

    def at(self, slot):
        return jnp.concatenate([added([t[slot] for t in terms]) for terms in self.terms], axis=0)

    def last_sends(self):
        return [self.at(slot).astype(BF16) for slot in range(1, self.count)]

    def last_receive(self, sends):
        return [swap(send, (n + 1) << self.groups[2][0]) for n, send in enumerate(sends)]

    def finish(self, received):
        return added([self.at(0), *received])


class Whole:
    def __init__(self, keep, send, groups):
        self.groups = groups
        self.terms = [keep, swap(send, 1)]
        self.count = keep.shape[0]

    def sends(self):
        self.count //= 4
        return [
            added([t[n * self.count : (n + 1) * self.count] for t in self.terms]).astype(BF16)
            for n in range(1, 4)
        ]

    def receive(self, sends):
        return [swap(send, (n + 1) << self.groups[1][0]) for n, send in enumerate(sends)]

    def last_sends(self):
        return [added([t[n] for t in self.terms]).astype(BF16) for n in range(1, self.count)]

    def last_receive(self, sends):
        return [swap(send, (n + 1) << self.groups[2][0]) for n, send in enumerate(sends)]

    def finish(self, received):
        return added([added([t[0] for t in self.terms]), *received])


def added(terms):
    return sum(term.astype(F32) for term in terms)


def scatter(keep, send, groups):
    terms = [keep, swap(send, 1)]
    for low, width in groups[1:]:
        count = 1 << width
        terms = [t.reshape((count, -1) + t.shape[1:]) for t in terms]
        sends = [added([t[step] for t in terms]).astype(BF16) for step in range(1, count)]
        terms = [added([t[0] for t in terms])]
        terms += [swap(send, (n + 1) << low) for n, send in enumerate(sends)]
    return added(terms)[0]


def all_sum(value, groups):
    for low, width in groups:
        value = sum([swap(value, s << low) for s in range(1, 1 << width)], value)
    return value


def turned(mask, groups):
    low = groups[1][0]
    both = (mask >> low) & 3
    return mask ^ ((both ^ (both >> 1) ^ ((both & 1) << 1)) << low)


def slot_masks(groups, turn=False):
    masks = [mask_of(slot, groups) for slot in range(1 << sum(width for _, width in groups[1:]))]
    return [turned(mask, groups) for mask in masks] if turn else masks


def in_order(parts, masks, place):
    found = [mask for part in masks for mask in part]
    slots = [0] * len(found)
    for slot, mask in enumerate(found):
        slots[mask] = slot
    devices = jnp.arange(len(found), dtype=jnp.int32)
    return jnp.take(join(parts), jnp.asarray(slots, jnp.int32)[place ^ devices], axis=0)


def by_slot(parts, place, groups):
    masks = jnp.asarray(slot_masks(groups), jnp.int32)
    return [jnp.take(parts, place ^ (masks | bit), axis=0) for bit in range(2)]


def adapt_kernel(rows, copies, *refs):
    count = len(rows)
    inputs, outputs = refs[: 4 * count + 1], refs[4 * count + 1 :]
    sum_ref = outputs[3 * count]
    sum_ref[...] = inputs[-1][...]
    half = sum_ref.shape[0] // 2
    correct = 1.0 - BETA**STEP
    for number, row in enumerate(rows):
        grad_ref, first_ref, second_ref, weight_ref = inputs[4 * number : 4 * number + 4]
        moment_ref, square_ref, update_ref = outputs[3 * number : 3 * number + 3]
        planes = weight_ref.shape[0] if len(weight_ref.shape) == 3 else 1
        width = weight_ref.shape[-1]
        norms = []
        for n in range(planes):
            at = n if len(weight_ref.shape) == 3 else Ellipsis
            if len(grad_ref.shape) == 3:
                grad = jnp.sum(grad_ref[...], axis=0)[: weight_ref.shape[0], :width]
            else:
                grad = grad_ref[:, n * width : (n + 1) * width]
            moment = BETA * first_ref[at] + (1.0 - BETA) * grad
            square = BETA * second_ref[at] + (1.0 - BETA) * grad * grad
            weight = weight_ref[at]
            update = moment / correct / (jnp.sqrt(square / correct) + ADAM_EPS) + DECAY * weight
            moment_ref[at] = moment
            square_ref[at] = square
            update_ref[at] = update
            norms.append([jnp.sum(v * v, axis=1, keepdims=True) for v in (weight, update)])
        for n in range(2):
            norm = sum(both[n] for both in norms)
            if row < 4:
                norm = total(norm)
            place = n * half + row
            sum_ref[place : place + norm.shape[0], :] = jnp.broadcast_to(norm, (norm.shape[0], 128))
    if copies:
        outputs[-1][...] = jnp.broadcast_to(diagonal(sum_ref[...]), outputs[-1].shape)


def diagonal(values):
    row = lax.broadcasted_iota(jnp.int32, values.shape, 0)
    lane = lax.broadcasted_iota(jnp.int32, values.shape, 1)
    return total(jnp.where(row == lane, values, 0.0))


def adapt(states, rows, sums=None, copies=0):
    if sums is None:
        sums = jnp.zeros((32, 128), F32)
    operands = [array for state in states for array in state] + [sums]
    shapes = [state[3].shape for state in states for _ in range(3)] + [sums.shape]
    if copies:
        shapes.append((copies, 8, 128))
    found = pl.pallas_call(
        lambda *refs: adapt_kernel(rows, copies, *refs),
        grid=(1,),
        in_specs=[whole(a.shape) for a in operands],
        out_specs=[pl.BlockSpec(s, lambda *_, n=len(s): (0,) * n) for s in shapes],
        out_shape=[jax.ShapeDtypeStruct(s, F32) for s in shapes],
        compiler_params=params(),
        cost_estimate=cost(4),
        name="adapt",
    )(*operands)
    return [found[3 * n : 3 * n + 3] for n in range(len(states))], found[-1]


def master_kernel(sum_ref, *refs):
    *refs, trust_ref = refs
    count = len(refs) // 3
    width = trust_ref.shape[1]
    if len(sum_ref.shape) == 3:
        line = jnp.sum(sum_ref[...], axis=0)[:1]
    else:
        line = diagonal(sum_ref[...])
    norms = [jnp.sqrt(line[:, n * width : (n + 1) * width]) for n in range(2)]
    ratio = norms[0] / (norms[1] + ADAM_EPS)
    for n, value in enumerate([*norms, ratio]):
        trust_ref[n : n + 1, :] = jnp.log(value)
    for n in range(count):
        update_ref, weight_ref, out_ref = refs[n], refs[count + n], refs[2 * count + n]
        if n < 4:
            scale = RATE * ratio[:, n : n + 1]
        else:
            shape = (weight_ref.shape[0], width)
            row = lax.broadcasted_iota(jnp.int32, shape, 0)
            lane = lax.broadcasted_iota(jnp.int32, shape, 1)
            picked = jnp.where(lane == row + 4, jnp.broadcast_to(ratio, shape), 0.0)
            scale = RATE * jnp.sum(picked, axis=1, keepdims=True)
        for at in range(weight_ref.shape[0]) if len(weight_ref.shape) == 3 else [Ellipsis]:
            out_ref[at] = weight_ref[at] - scale * update_ref[at]


def master(sums, updates, weights, width):
    arrays = [sums, *updates, *weights]
    shapes = [a.shape for a in weights] + [(3, width)]
    return pl.pallas_call(
        master_kernel,
        grid=(1,),
        in_specs=[whole(a.shape) for a in arrays],
        out_specs=[pl.BlockSpec(s, lambda *_, n=len(s): (0,) * n) for s in shapes],
        out_shape=[jax.ShapeDtypeStruct(s, F32) for s in shapes],
        compiler_params=params(),
        cost_estimate=cost(3),
        name="master",
    )(*arrays)


def halves(parts, groups):
    return by_slot(parts, jnp.int32(0), groups)


def by_index(keep, send, groups, turn=False):
    masks = slot_masks(groups, turn)
    return in_order([keep, send], [masks, [mask | 1 for mask in masks]], jnp.int32(0))


def join_heads(pieces):
    nb, nh, rows, flat = pieces.shape
    wider = nb * nh // PARTS
    parts = pieces.reshape(nb // wider, wider, nh, rows, flat).transpose(0, 2, 1, 3, 4)
    return parts.reshape(PARTS, wider * rows, flat)


def join_parts(parts, nh):
    count = lax.axis_size("batch") * lax.axis_size("head")
    wider = count // PARTS
    _, rows, flat = parts.shape
    parts = parts.reshape(PARTS // nh, nh, wider, rows // wider, flat).transpose(0, 2, 1, 3, 4)
    return parts.reshape(count, rows // wider, flat)


def shards(
    block_input,
    cotangent,
    segment_lengths,
    thought_counts,
    packing_mask,
    attend_weight,
    output_weight,
    expand_weight,
    reduce_weight,
    vectors,
    first_attend,
    first_output,
    first_expand,
    first_reduce,
    first_vectors,
    second_attend,
    second_output,
    second_expand,
    second_reduce,
    second_vectors,
):
    nb, nh = lax.axis_size("batch"), lax.axis_size("head")
    count = nb * nh
    groups, kernel_groups = bit_groups(count), bit_groups(PARTS)
    same = count == PARTS
    place = (lax.axis_index("batch") * nh + lax.axis_index("head")).astype(jnp.int32)
    core = place % 2
    kernel_place = (place if same else jnp.zeros_like(place)).reshape(1)
    rows, length, model = block_input.shape
    tokens = rows * length
    hidden = expand_weight.shape[1]
    own_in, _, own_out = attend_weight.shape
    own = output_weight.shape[0]
    own_red = reduce_weight.shape[0]
    cols = vectors.shape[1]
    wide = hidden // model
    flat = 3 * own_out

    extra = jnp.pad(vectors.astype(BF16).T, ((0, -cols % 16), (0, flat - own)))
    piece = jnp.concatenate([attend_weight.astype(BF16).reshape(own_in, flat), extra], axis=0)
    attend_far = gather_far(piece, groups)

    blocks = expand_weight.astype(BF16).reshape(own, 2, wide // 2, model).transpose(1, 2, 0, 3)
    beside = swap(jnp.where(core == 0, blocks[1], blocks[0]), 1)
    mine = jnp.where(core == 0, blocks[0], blocks[1])
    piece = [
        jnp.concatenate(
            [jnp.where(core == 0, mine, beside), jnp.where(core == 0, beside, mine)], axis=1
        ).reshape(2 * own * (wide // 2), model),
        reduce_weight.astype(BF16),
        output_weight.astype(BF16),
    ]
    pad = -(own_red + own) % 16
    piece = jnp.concatenate(piece + [jnp.zeros((pad, model), BF16)], axis=0)
    late_all = lax.all_gather(piece, AXES, axis=0, tiled=False)
    attend_own = cross(attend_far, groups[1])
    attend_other = swap(attend_own, 1)
    if not same:
        masks = slot_masks(groups)
        attend = in_order([attend_own, attend_other], [masks, [m | 1 for m in masks]], place)
        vec = attend[:, own_in:, :own].transpose(1, 0, 2).reshape(-1, PARTS, model // PARTS)
        vec = jnp.pad(vec.transpose(1, 0, 2), ((0, 0), (0, 0), (0, flat - model // PARTS)))
        attend = join_heads(attend[:, :own_in].reshape(nb, nh, own_in, flat))
        attend_own, attend_other = halves(
            jnp.concatenate([attend, vec], axis=1), kernel_groups
        )

    own_lengths = lax.dynamic_slice_in_dim(
        segment_lengths, lax.axis_index("head") * rows, rows, 0
    )
    own_counts = lax.dynamic_slice_in_dim(thought_counts, lax.axis_index("head") * rows, rows, 0)
    start_of, weight_rows = row_facts(own_lengths, own_counts, packing_mask, length)
    start_of = start_of.reshape(rows, 1, length)
    weight_rows = weight_rows.reshape(tokens, 1)

    x = block_input.reshape(tokens, model)
    cot = cotangent.reshape(tokens, model)
    normed_low, qkv, attend_low, vec = project(
        kernel_place, x, attend_own, attend_other, nh, cols
    )
    context, probs = attend_forward(start_of, qkv, length)
    if not same:
        late = late_all
        both, per = 2 * own, 2 * model // PARTS
        expand_low = (
            late[:, : both * wide // 2]
            .reshape(count // 2, 2, wide // 2, both, model)
            .transpose(1, 2, 0, 3, 4)
            .reshape(2, wide // 2, PARTS // 2, per, model)
            .transpose(2, 0, 1, 3, 4)
            .reshape(PARTS, per * (wide // 2), model)
        )
        low = both * wide // 2
        rest = [
            expand_low,
            late[:, low : low + own_red].reshape(PARTS, hidden // PARTS, model),
            late[:, low + own_red : low + own_red + own].reshape(PARTS, per // 2, model),
            jnp.zeros((PARTS, 8, model), BF16),
        ]
        late_all = jnp.concatenate(rest, axis=1)
    late = (late_all,)
    hidden_states, middle, middle_low, activated, slope, branch = mlp_forward(
        late, context, x, cot, weight_rows, vec, hidden
    )

    def for_devices(keep, send, split):
        parts = [by_index(*both, kernel_groups, n == 1) for n, both in enumerate(zip(keep, send))]
        return by_slot(split(jnp.concatenate(parts, axis=1)), place, groups)

    def split_mid(parts):
        per = 2 * model // PARTS
        expand = (
            jnp.stack([parts[:, :per], parts[:, per + 32 :]], axis=1)
            .reshape(PARTS // 2, 2, 2, per, model)
            .transpose(1, 2, 0, 3, 4)
            .reshape(2, 2, count // 2, 2 * own, model)
            .transpose(2, 0, 1, 3, 4)
            .reshape(count, 4 * own, model)
        )
        output = parts[:, per : per + per // 2].reshape(count, own, model)
        return jnp.concatenate([expand, output], axis=1)

    red_keep, red_send = reduce_weight_grad(kernel_place, activated, branch)
    if same:
        cot, *red_send = ordered(cot, *red_send)
        red = Halves(red_keep, red_send, groups)
    grad_pre, grad_middle, grad_attn, grad_context, mid_sums = mlp_backward(
        late, cot, weight_rows, middle, slope, vec
    )
    if same:
        grad_pre, *terms = ordered(grad_pre, *red.flat())
        red.set(terms)
        grad_pre, *sends = ordered(grad_pre, *red.sends())
        red_received = red.receive(sends)

    mid_keep, mid_send = mid_weight_grad(
        kernel_place, middle_low, grad_pre, context, grad_attn
    )
    if same:
        grad_context, *terms = ordered(grad_context, *mid_send, *red_received)
        mid = Halves(mid_keep, terms[:2], groups)
        red.add(terms[2:])
        grad_context, *sends = ordered(grad_context, *red.sends())
        red_received = red.receive(sends)

    pairs = model // (2 * HEAD_DIM)
    operands = (qkv, context, grad_context, probs, length)
    d_qkv = attend_backward(*operands, 0, pairs // 2)
    if same:
        d_qkv, *terms = ordered(d_qkv, *mid.flat(), *red_received)
        mid.set(terms[:4])
        red.add(terms[4:])
        d_qkv, *sends = ordered(d_qkv, *mid.sends(), *red.last_sends())
        mid_received = mid.receive(sends[:2])
        red_received = red.last_receive(sends[2:])
    d_qkv = attend_backward(*operands, pairs // 2, rows * pairs, d_qkv)
    if same:
        d_qkv, *terms = ordered(d_qkv, *mid_received, *red_received)
        mid.add(terms[:2])
        red_received = terms[2:]
        d_qkv, *sends = ordered(d_qkv, *mid.sends())
        mid_received = mid.receive(sends)
    att_keep, att_send = attend_weight_grad(kernel_place, normed_low, d_qkv, nh)
    if same:
        att_send, *mid_received = ordered(att_send, *mid_received)
        att = Whole(att_keep, att_send, groups)
        mid.add(mid_received)
        d_qkv, *terms = ordered(d_qkv, *mid.last_sends(), *att.terms)
        att.terms = terms[-2:]
        mid_nearest, *mid_sends = terms[:-2]
        mid_received = [
            swap(send, (n + 2) << groups[2][0]) for n, send in enumerate(mid_sends)
        ]
        d_qkv, *sends = ordered(d_qkv, *att.sends())
        att_received = att.receive(sends)
    grad_input, sums, sum_parts = input_grad(d_qkv, x, grad_middle, attend_low, vec, mid_sums)
    if same:
        sum_parts, mid_nearest, *terms = ordered(
            sum_parts, mid_nearest, *att_received, *mid_received, *red_received
        )
        att.terms = att.terms + terms[:3]
        att_received = att.last_receive(att.last_sends())
        mid_received = terms[3:5] + [swap(mid_nearest, 1 << groups[2][0])]
        red_grad, found = red.finish(terms[5:]), mid.finish(mid_received)
        per = 2 * own
        mid = jnp.concatenate(
            [found[:per], found[per + 32 :], found[per : per + own]], axis=0
        )
    else:
        red_parts = for_devices(
            red_keep, red_send, lambda parts: parts.reshape(count, own_red, model)
        )
        mid_parts = for_devices(mid_keep, mid_send, split_mid)
        att_parts = for_devices(
            [att_keep], [att_send], lambda parts: join_parts(parts, nh).reshape(count, own_in, flat)
        )
        red_grad, mid = scatter(*red_parts, groups), scatter(*mid_parts, groups)
        att_grad = scatter(*att_parts, groups)
    out_grad = mid[4 * own : 5 * own]
    exp_both = mid[: 4 * own].reshape(2, 2, own, model)
    kept = jnp.where(core == 0, exp_both[:, 0], exp_both[:, 1])
    beside = swap(jnp.where(core == 0, exp_both[:, 1], exp_both[:, 0]), 1)
    exp_grad = jnp.stack(
        [jnp.where(core == 0, kept, beside), jnp.where(core == 0, beside, kept)]
    ).reshape(wide, own, model)
    exp_grad = exp_grad.transpose(1, 0, 2).reshape(own, hidden)


    if same:
        vector_grad = lax.all_to_all(sum_parts, AXES, 0, 0, tiled=True)
    else:
        vector_grad = lax.dynamic_slice_in_dim(all_sum(sums, groups), place * own, own, 1)
    late_weights = (output_weight, expand_weight, reduce_weight)
    late_states = [
        (grad, first, second, weight)
        for grad, first, second, weight in zip(
            (out_grad, exp_grad, red_grad),
            (first_output, first_expand, first_reduce),
            (second_output, second_expand, second_reduce),
            late_weights,
        )
    ]
    late_found, late_sums = adapt(late_states, [1, 2, 3])
    if same:
        late_sums, *att_received = ordered(late_sums, *att_received)
        att_grad = att.finish(att_received)

    def planes(state):
        return state.transpose(1, 0, 2)

    found, sums = adapt(
        [
            (att_grad, planes(first_attend), planes(second_attend), planes(attend_weight)),
            (vector_grad, first_vectors.T, second_vectors.T, vectors.T),
        ],
        [0, 4],
        late_sums,
        count if same else 0,
    )
    sums = lax.all_to_all(sums, AXES, 0, 0, tiled=True) if same else all_sum(sums, groups)
    adapted = [list(found[0]), *late_found, [a.T for a in found[1]]]
    *masters, trust_norms = master(
        sums,
        [found[0][2], *[a[2] for a in late_found], found[1][2]],
        [planes(attend_weight), *late_weights, vectors.T],
        4 + cols,
    )
    masters[4] = masters[4].T
    adapted[0] = [planes(a) for a in adapted[0]]
    masters[0] = planes(masters[0])
    return (
        hidden_states.reshape(rows, length, model),
        grad_input.reshape(rows, length, model),
        *[a[0] for a in adapted],
        *[a[1] for a in adapted],
        *masters,
        trust_norms,
    )


def solution(mesh):
    rows = P(AXES, None, None)
    state = [P("batch", None, "head")] + [P(AXES, None)] * 4
    return jax.shard_map(
        shards,
        mesh=mesh,
        in_specs=(rows, rows, P("batch", None), P("batch", None), P(AXES, None), *state * 3),
        out_specs=(rows, rows, *state * 3, P()),
        check_vma=False,
    )
```

```python
import jax
import jax.numpy as jnp
from jax import lax
from jax.experimental import pallas as pl
from jax.experimental.pallas import tpu as pltpu
from jax.sharding import PartitionSpec as P

HEAD_DIM = 64
THOUGHT_TOKENS = 8
STEP = 6
PARTS = 32
SPAN = 256
BLOCK = 128

NORM_EPS = 1e-05
NEGATIVE = -1e30
BETA = 0.5
RATE = 0.5
DECAY = 0.01
ADAM_EPS = 1e-06
AXES = ("batch", "head")
ROOT = 0.7978845608028654
CUBE = 0.044715
F32 = jnp.float32
BF16 = jnp.bfloat16
NT = (((1,), (1,)), ((), ()))
TN = (((0,), (0,)), ((), ()))


def dot(a, b, dims=(((1,), (0,)), ((), ()))):
    return lax.dot_general(a, b, dims, preferred_element_type=F32)


def params(grid=1, vmem=60):
    return pltpu.CompilerParams(
        dimension_semantics=("arbitrary",) * grid, vmem_limit_bytes=vmem * 1024 * 1024
    )


def cost(micros):
    return pl.CostEstimate(flops=int(micros * 0.29e9), bytes_accessed=1 << 18, transcendentals=0)


def whole(shape):
    return pl.BlockSpec(shape, lambda *_: (0,) * len(shape), pipeline_mode=pl.Buffered(1))


SCALARS = pl.BlockSpec(memory_space=pltpu.SMEM)


def row_facts(lengths, counts, mask, span):
    positions = jnp.arange(span, dtype=jnp.int32)
    ends = jnp.cumsum(lengths, axis=-1)
    starts = ends - lengths
    inside = (positions[None, :, None] >= starts[:, None, :]) & (
        positions[None, :, None] < ends[:, None, :]
    )
    start_of = jnp.sum(jnp.where(inside, starts[:, None, :], 0), axis=-1)
    passes = jnp.sum(jnp.where(inside, counts[:, None, :], 0), axis=-1)
    keep = (positions[None, :] - start_of >= THOUGHT_TOKENS * passes) & (mask > 0)
    return start_of, keep.astype(F32)


def windows(length):
    return [
        (low, max(0, low - SPAN), low + BLOCK - max(0, low - SPAN)) for low in range(0, length, BLOCK)
    ]


def fill_caps(start_ref, cap_ref, length):
    for number, (low, first, count) in enumerate(windows(length)):
        key = lax.broadcasted_iota(jnp.int32, (count, BLOCK), 0) + first
        query = lax.broadcasted_iota(jnp.int32, (count, BLOCK), 1) + low
        start = start_ref[0, :, low : low + BLOCK]
        allowed = (key <= query) & (key >= start)
        cap_ref[number, :count] = jnp.where(allowed, 3e38, NEGATIVE)


def cap_of(cap_ref, number, count):
    cap = cap_ref[number, :count]
    return jnp.concatenate([cap, cap], axis=1)


def for_heads(values):
    lane = lax.broadcasted_iota(jnp.int32, (1, 2 * HEAD_DIM), 1)
    return jnp.concatenate(
        [jnp.where(lane < HEAD_DIM, values, 0), jnp.where(lane >= HEAD_DIM, values, 0)], axis=0
    )


def of_heads(values):
    return jnp.concatenate([values[:HEAD_DIM, :BLOCK], values[HEAD_DIM:, BLOCK:]], axis=0)


def in_stages(units, ahead, behind, first, middle, last):
    started, worked = [first(unit) for unit in units[:ahead]], []
    for number, unit in enumerate(units):
        if number + ahead < len(units):
            started.append(first(units[number + ahead]))
        worked.append((unit, middle(unit, started.pop(0))))
        if len(worked) > behind:
            last(*worked.pop(0))
    for both in worked:
        last(*both)


def attend_forward_kernel(fresh, start_ref, q_ref, k_ref, v_ref, o_ref, p_ref, cap_ref):
    length = q_ref.shape[0]
    pl.when(fresh)(lambda: fill_caps(start_ref, cap_ref, length))
    value_t = v_ref[...].T

    def score(unit):
        _, (low, first, count) = unit
        query = for_heads(q_ref[low : low + BLOCK, :] * (HEAD_DIM**-0.5))
        return dot(k_ref[first : first + count, :], query, NT)

    def soften(unit, scores):
        number, (_, _, count) = unit
        scores = jnp.minimum(scores, cap_of(cap_ref, number, count))
        grown = jnp.exp(scores - jnp.max(scores, axis=0, keepdims=True))
        probs = (grown * (1.0 / total(grown))).astype(BF16)
        p_ref[0, 0, number, :count] = probs
        return probs

    def mix(unit, probs):
        _, (low, first, count) = unit
        result = dot(value_t[:, first : first + count], probs)
        o_ref[low : low + BLOCK, :] = of_heads(result).T.astype(BF16)

    in_stages(list(enumerate(windows(length))), 4, 1, score, soften, mix)


def attend_backward_kernel(q_ref, k_ref, v_ref, o_ref, do_ref, p_ref, *rest):
    d_ref = rest[-1]
    length = q_ref.shape[0]
    key_t = k_ref[...].T
    grad_key, grad_value = {}, {}

    def query_of(low):
        return for_heads(q_ref[low : low + BLOCK, :] * (HEAD_DIM**-0.5))

    def grad_of(low):
        return for_heads(do_ref[low : low + BLOCK, :])

    def score(unit):
        _, (low, first, count) = unit
        return dot(v_ref[first : first + count, :], grad_of(low), NT)

    def soften(unit, grad_probs):
        number, (low, _, count) = unit
        product = do_ref[low : low + BLOCK, :].astype(F32) * o_ref[low : low + BLOCK, :].astype(F32)
        product = product.T
        inner = jnp.concatenate([total(product[:HEAD_DIM]), total(product[HEAD_DIM:])], axis=1)
        probs = p_ref[0, 0, number, :count]
        return probs, (probs.astype(F32) * (grad_probs - inner)).astype(BF16)

    def mix(unit, found):
        _, (low, first, count) = unit
        probs, grad_scores = found
        terms = dot(probs, grad_of(low)), dot(grad_scores, query_of(low))
        grad_query = dot(key_t[:, first : first + count], grad_scores)
        d_ref[0, low : low + BLOCK, :] = (of_heads(grad_query).T * (HEAD_DIM**-0.5)).astype(BF16)
        for sums, term, place in ((grad_value, terms[0], 2), (grad_key, terms[1], 1)):
            for at in range(first, first + count, BLOCK):
                one = term[at - first : at - first + BLOCK]
                sums[at] = sums[at] + one if at in sums else one
            for at in list(sums):
                if at <= low - SPAN or low + BLOCK == length:
                    d_ref[place, at : at + BLOCK, :] = sums.pop(at).astype(BF16)

    in_stages(list(enumerate(windows(length))), 2, 0, score, soften, mix)


def attention_specs(length, pairs, low=0):
    pair = 2 * HEAD_DIM

    def at(i):
        return (i + low) // pairs, (i + low) % pairs

    def columns(n):
        return lambda i: (at(i)[0], n * pairs + at(i)[1])

    qkv = [pl.BlockSpec((length, pair), columns(n)) for n in range(3)]
    rows = pl.BlockSpec((length, pair), columns(0))
    probs = pl.BlockSpec((1, 1) + probs_shape(length), lambda i: (*at(i), 0, 0, 0))
    start = pl.BlockSpec((1, 1, length), lambda i: (at(i)[0], 0, 0))
    return start, qkv, rows, probs, lambda i: (0, *at(i))


def probs_shape(length):
    return (length // BLOCK, SPAN + BLOCK, 2 * BLOCK)


def attend_forward(start, qkv, length):
    tokens, model = qkv.shape[0], qkv.shape[1] // 3
    pairs = model // (2 * HEAD_DIM)
    rows = tokens // length
    start_spec, qkv_specs, row_spec, probs_spec, _ = attention_specs(length, pairs)

    def kernel(*refs):
        attend_forward_kernel(pl.program_id(0) % pairs == 0, *refs)

    return pl.pallas_call(
        kernel,
        grid=(rows * pairs,),
        in_specs=[start_spec] + qkv_specs,
        out_specs=[row_spec, probs_spec],
        out_shape=[
            jax.ShapeDtypeStruct((tokens, model), BF16),
            jax.ShapeDtypeStruct((rows, pairs) + probs_shape(length), BF16),
        ],
        scratch_shapes=[pltpu.VMEM((length // BLOCK, SPAN + BLOCK, BLOCK), F32)],
        compiler_params=params(),
        cost_estimate=cost(18),
        name="attend_forward",
    )(start, qkv, qkv, qkv)


def attend_backward(qkv, out, grad, probs, length, low, high, before=None):
    tokens, model = out.shape
    pairs = model // (2 * HEAD_DIM)
    _, qkv_specs, row_spec, probs_spec, at = attention_specs(length, pairs, low)
    operands = [qkv, qkv, qkv, out, grad, probs]
    in_specs = qkv_specs + [row_spec, row_spec, probs_spec]
    aliases = {}
    if before is not None:
        aliases = {len(operands): 0}
        operands.append(before)
        in_specs.append(pl.BlockSpec(memory_space=pl.ANY))
    return pl.pallas_call(
        attend_backward_kernel,
        grid=(high - low,),
        in_specs=in_specs,
        out_specs=pl.BlockSpec((3, length, 2 * HEAD_DIM), at),
        out_shape=jax.ShapeDtypeStruct((3, tokens, model), BF16),
        input_output_aliases=aliases,
        compiler_params=params(),
        cost_estimate=cost(2.0 * (high - low)),
        name="attend_backward",
    )(*operands)


def normalize(values):
    centre = values - jnp.mean(values, axis=-1, keepdims=True)
    factor = lax.rsqrt(jnp.mean(centre * centre, axis=-1, keepdims=True) + NORM_EPS)
    return centre * factor, factor


def norm_back(inner, normed, factor):
    return factor * (
        inner
        - jnp.mean(inner, axis=-1, keepdims=True)
        - normed * jnp.mean(inner * normed, axis=-1, keepdims=True)
    )


def total(values):
    return jnp.sum(values, axis=0, keepdims=True)


def project_kernel(place_ref, x_ref, own_ref, other_ref, nl_ref, qkv_ref, w_ref, vec_ref, *, heads):
    slots, rows, flat = own_ref.shape
    rows -= -(-vec_ref.shape[0] // 16) * 16
    part, model = flat // 3, x_ref.shape[1]
    groups = bit_groups(2 * slots)
    place = place_ref[0]

    @pl.when(pl.program_id(0) == 0)
    def _():
        for here in range(heads):

            @pl.when(place % heads == here)
            def _(here=here):
                for bit, ref in enumerate((own_ref, other_ref)):
                    for slot in range(slots):
                        mask = mask_of(slot, groups) | bit
                        head = here ^ (mask % heads)
                        row = pl.multiple_of(((place ^ mask) // heads) * rows, rows)
                        for j in range(3):
                            low = j * model + head * part
                            w_ref[pl.ds(row, rows), low : low + part] = ref[
                                slot, :rows, j * part : (j + 1) * part
                            ]

        count, each = vec_ref.shape[0], model // (2 * slots)
        lane = lax.broadcasted_iota(jnp.int32, (1, model), 1)
        found = jnp.zeros((count, model), F32)
        for bit, ref in enumerate((own_ref, other_ref)):
            for slot in range(slots):
                device = place ^ (mask_of(slot, groups) | bit)
                piece = ref[slot, rows:, :128].astype(F32)[:count]
                piece = jnp.concatenate([piece] * (model // 128), axis=1)
                piece = pltpu.roll(piece, (device * each) % 128, 1)
                inside = (lane >= device * each) & (lane < (device + 1) * each)
                found = jnp.where(inside, piece, found)
        vec_ref[...] = found

    normed, _ = normalize(x_ref[...].astype(F32))
    low = (normed * vec_ref[0:1, :] + vec_ref[1:2, :]).astype(BF16)
    nl_ref[...] = low
    for j in range(3):
        side = slice(j * model, (j + 1) * model)
        result = dot(low, w_ref[:, side])
        if j != 1:
            result = result + vec_ref[2 + j // 2 : 3 + j // 2, :]
        qkv_ref[:, side] = result.astype(BF16)


def project(place, x, own, other, heads, cols, tile=512):
    tokens, model = x.shape
    row = pl.BlockSpec((tile, model), lambda i: (i, 0))
    return pl.pallas_call(
        lambda *refs: project_kernel(*refs, heads=heads),
        grid=(tokens // tile,),
        in_specs=[SCALARS, row, whole(own.shape), whole(other.shape)],
        out_specs=[
            row,
            pl.BlockSpec((tile, 3 * model), lambda i: (i, 0)),
            pl.BlockSpec((model, 3 * model), lambda i: (0, 0)),
            pl.BlockSpec((cols, model), lambda i: (0, 0)),
        ],
        out_shape=[
            jax.ShapeDtypeStruct((tokens, model), BF16),
            jax.ShapeDtypeStruct((tokens, 3 * model), BF16),
            jax.ShapeDtypeStruct((model, 3 * model), BF16),
            jax.ShapeDtypeStruct((cols, model), F32),
        ],
        compiler_params=params(),
        cost_estimate=cost(14),
        name="project",
    )(place, x, own, other)


class Late:
    def __init__(self, refs, scratch):
        (self.parts,) = refs
        self.expand, self.reduce, self.output, self.stage, self.sem = scratch
        self.model = self.output.shape[1]
        self.chunks = self.expand.shape[0]

    def copies(self):
        per = self.model // self.stage.shape[1]
        red = self.reduce.shape[0] // (2 * self.stage.shape[1])
        end = 2 * per + red
        for device in range(self.parts.shape[0]):
            row, bit = (device // 2) * per, device % 2
            for n in range(2):
                yield (
                    self.parts.at[device, n * per : (n + 1) * per],
                    self.expand.at[2 * bit + n, row : row + per],
                )
            yield (
                self.parts.at[device, 2 * per : end],
                self.reduce.at[device * red : (device + 1) * red],
            )
            yield (
                self.parts.at[device, end : end + self.stage.shape[2]],
                self.stage.at[bit, device // 2],
            )

    def load(self):
        copies = [pltpu.make_async_copy(a, b, self.sem) for a, b in self.copies()]
        for copy in copies:
            copy.start()
        for copy in copies:
            copy.wait()
        slots = self.stage.shape[1]
        per = self.model // slots
        for n in range(slots):
            both = [self.stage[bit, n, : per // 2, :].astype(F32) for bit in range(2)]
            self.output[n * per : (n + 1) * per, :] = jnp.concatenate(both, axis=0).astype(BF16)

    def reduce_rows(self, c):
        return self.reduce[c * self.model : (c + 1) * self.model, :]

    @staticmethod
    def specs():
        return [pl.BlockSpec(memory_space=pl.ANY)]

    @staticmethod
    def scratch(late, hidden):
        slots, _, model = late[0].shape
        slots //= 2
        return [
            pltpu.VMEM((hidden // model, model, model), BF16),
            pltpu.VMEM((hidden, model), BF16),
            pltpu.VMEM((model, model), BF16),
            pltpu.VMEM((2, slots, 32, model), BF16),
            pltpu.SemaphoreType.DMA,
        ]


def mlp_forward_kernel(*refs):
    late = Late(refs[:-16], refs[-5:])
    ctx_ref, x_ref, cot_ref, wt_ref, vec_ref = refs[-16:-11]
    hid_ref, mid_ref, nm_ref, act_ref, dg_ref, gb_ref = refs[-11:-5]
    model = late.model
    pl.when(pl.program_id(0) == 0)(late.load)
    middle = x_ref[...].astype(F32) + dot(ctx_ref[...], late.output[...]) + vec_ref[4:5, :]
    mid_ref[...] = middle
    gb_ref[...] = (cot_ref[...].astype(F32) * wt_ref[...]).astype(BF16)
    normed, _ = normalize(middle)
    low = (normed * vec_ref[5:6, :] + vec_ref[6:7, :]).astype(BF16)
    nm_ref[...] = low
    result = middle + vec_ref[7:8, :]
    for c in range(late.chunks):
        side = slice(c * model, (c + 1) * model)
        pre = dot(low, late.expand[c]) + vec_ref[8 + c : 9 + c, :]
        square = pre * pre
        half = 0.5 + 0.5 * jnp.tanh(pre * (ROOT + (ROOT * CUBE) * square))
        act = pre * half
        dg = half + act * (1.0 - half) * (2.0 * ROOT + (6.0 * ROOT * CUBE) * square)
        dg_ref[:, side] = dg.astype(BF16)
        act = act.astype(BF16)
        act_ref[:, side] = act
        result = result + dot(act, late.reduce_rows(c))
    hid_ref[...] = result.astype(BF16)


def mlp_forward(late, ctx, x, cot, wt, vec, hidden, tile=256):
    tokens, model = x.shape
    row = pl.BlockSpec((tile, model), lambda i: (i, 0))
    wide = pl.BlockSpec((tile, hidden), lambda i: (i, 0))
    one = pl.BlockSpec((tile, 1), lambda i: (i, 0))

    def shape(width, kind=BF16):
        return jax.ShapeDtypeStruct((tokens, width), kind)

    return pl.pallas_call(
        mlp_forward_kernel,
        grid=(tokens // tile,),
        in_specs=Late.specs() + [row, row, row, one, whole(vec.shape)],
        out_specs=[row, row, row, wide, wide, row],
        out_shape=[
            shape(model), shape(model, F32), shape(model), shape(hidden), shape(hidden), shape(model),
        ],
        scratch_shapes=Late.scratch(late, hidden),
        compiler_params=params(),
        cost_estimate=cost(40),
        name="mlp_forward",
    )(*late, ctx, x, cot, wt, vec)


def mlp_backward_kernel(*refs):
    late = Late(refs[:-15], refs[-5:])
    cot_ref, wt_ref, mid_ref, dg_ref, vec_ref = refs[-15:-10]
    gpre_ref, gm_ref, ga_ref, gc_ref, sum_ref = refs[-10:-5]
    model = late.model

    @pl.when(pl.program_id(0) == 0)
    def _():
        late.load()
        sum_ref[...] = jnp.zeros_like(sum_ref)

    grad_out = cot_ref[...].astype(F32) * wt_ref[...]
    branch = grad_out.astype(BF16)
    sum_ref[3:4, :] += total(branch.astype(F32))
    back = None
    for c in range(late.chunks):
        side = slice(c * model, (c + 1) * model)
        grad = (dot(branch, late.reduce_rows(c), NT) * dg_ref[:, side].astype(F32)).astype(BF16)
        gpre_ref[:, side] = grad
        sum_ref[4 + c : 5 + c, :] += total(grad.astype(F32))
        term = dot(grad, late.expand[c], NT)
        back = term if back is None else back + term
    normed, factor = normalize(mid_ref[...])
    sum_ref[1:2, :] += total(back * normed)
    sum_ref[2:3, :] += total(back)
    grad_middle = grad_out + norm_back(back * vec_ref[5:6, :], normed, factor)
    gm_ref[...] = grad_middle
    low = grad_middle.astype(BF16)
    ga_ref[...] = low
    sum_ref[0:1, :] += total(low.astype(F32))
    gc_ref[...] = dot(low, late.output[...], NT).astype(BF16)


def mlp_backward(late, cot, wt, mid, dg, vec, tile=256):
    tokens, model = cot.shape
    hidden = dg.shape[1]
    row = pl.BlockSpec((tile, model), lambda i: (i, 0))
    wide = pl.BlockSpec((tile, hidden), lambda i: (i, 0))
    one = pl.BlockSpec((tile, 1), lambda i: (i, 0))

    def shape(width, kind=BF16):
        return jax.ShapeDtypeStruct((tokens, width), kind)

    return pl.pallas_call(
        mlp_backward_kernel,
        grid=(tokens // tile,),
        in_specs=Late.specs() + [row, one, row, wide, whole(vec.shape)],
        out_specs=[wide, row, row, row, pl.BlockSpec((8, model), lambda i: (0, 0))],
        out_shape=[
            shape(hidden), shape(model, F32), shape(model), shape(model),
            jax.ShapeDtypeStruct((8, model), F32),
        ],
        scratch_shapes=Late.scratch(late, hidden),
        compiler_params=params(),
        cost_estimate=cost(36),
        name="mlp_backward",
    )(*late, cot, wt, mid, dg, vec)


def put_parts(place, outs, pieces, turn=False):
    groups = bit_groups(2 * outs[0].shape[0])
    for bit in range(2):

        @pl.when(place % 2 == bit)
        def _(bit=bit):
            for device, index, value in pieces:
                mask = place ^ device
                slot = slot_of(turned(mask, groups) if turn else mask, groups)
                outs[(device % 2) ^ bit][(slot,) + index] = value


class Outbox:
    def __init__(self, place, outs, buffer, sems, turn):
        self.place, self.outs, self.buffer, self.sems, self.turn = place, outs, buffer, sems, turn

    def begin(self, step, rows, count):
        @pl.when(step >= 2)
        def _():
            self.wait(step, rows, count)

    def wait(self, step, rows, count):
        for n in range(count):
            part = self.buffer.at[step % 2, n * rows : (n + 1) * rows]
            pltpu.make_async_copy(part, part, self.sems.at[step % 2]).wait()

    def send(self, step, pieces):
        groups = bit_groups(2 * self.outs[0].shape[0])
        for bit in range(2):

            @pl.when(self.place % 2 == bit)
            def _(bit=bit):
                for low, rows, odd, device, kind, there in pieces:
                    mask = self.place ^ device
                    mask = turned(mask, groups) if self.turn[kind] else mask
                    out = self.outs[2 * (odd ^ bit) + kind].at[slot_of(mask, groups)]
                    pltpu.make_async_copy(
                        self.buffer.at[step % 2, low : low + rows],
                        out.at[there : there + rows],
                        self.sems.at[step % 2],
                    ).start()


def reduce_weight_grad_kernel(place_ref, a_ref, b_ref, *rest):
    *outs, buffer, sems = rest
    slots, rows, model = outs[0].shape
    step, last = pl.program_id(0), pl.num_programs(0) - 1
    count = model // rows
    box = Outbox(place_ref[0], outs, buffer, sems, (False, True))
    result = dot(a_ref[...], b_ref[...], TN).astype(BF16)
    box.begin(step, rows, count)
    buffer[step % 2] = result
    box.send(
        step,
        [(n * rows, rows, n // 2 % 2, step * (count // 2) + n // 2, n % 2, 0) for n in range(count)],
    )

    @pl.when(step == last)
    def _():
        box.wait(step + 1, rows, count)
        box.wait(step, rows, count)


def hbm_outs_of(*shapes):
    return dict(
        out_specs=[pl.BlockSpec(memory_space=pl.ANY)] * len(shapes),
        out_shape=[jax.ShapeDtypeStruct(shape, BF16) for shape in shapes],
    )


def outs_of(*shapes):
    return dict(
        out_specs=[pl.BlockSpec(shape, lambda *_: (0,) * len(shape)) for shape in shapes],
        out_shape=[jax.ShapeDtypeStruct(shape, BF16) for shape in shapes],
    )


def reduce_weight_grad(place, act, branch):
    tokens, model = branch.shape
    hidden = act.shape[1]
    shape = (PARTS // 2, hidden // PARTS // 2, model)
    found = pl.pallas_call(
        reduce_weight_grad_kernel,
        grid=(hidden // model,),
        in_specs=[SCALARS, pl.BlockSpec((tokens, model), lambda i: (0, i)), whole(branch.shape)],
        **hbm_outs_of(*[shape] * 4),
        scratch_shapes=[pltpu.VMEM((2, model, model), BF16), pltpu.SemaphoreType.DMA((2,))],
        compiler_params=params(),
        cost_estimate=cost(15),
        name="reduce_weight_grad",
    )(place, act, branch)
    return found[:2], found[2:]


def mid_weight_grad_kernel(place_ref, nm_ref, gpre_ref, ctx_hbm, ga_hbm, *rest):
    *outs, ctx_ref, ga_ref, buffer, sems, out_sems = rest
    copies = [
        pltpu.make_async_copy(ctx_hbm, ctx_ref, sems.at[0]),
        pltpu.make_async_copy(ga_hbm, ga_ref, sems.at[1]),
    ]
    slots, rows, model = outs[0].shape
    per = model // slots
    step = pl.program_id(0)
    last = pl.num_programs(0) - 1
    box = Outbox(place_ref[0], outs, buffer, out_sems, (False, True))

    @pl.when(step == 1)
    def _():
        for copy in copies:
            copy.start()

    for c in range(4):

        @pl.when(step == c)
        def _(c=c):
            result = dot(nm_ref[...], gpre_ref[...], TN).astype(BF16)
            if c >= 2:
                box.wait(c, per, slots)
            buffer[c % 2, :model] = result
            box.send(
                c, [(n * per, per, c // 2, 2 * n + c // 2, c % 2, 0) for n in range(slots)]
            )

    @pl.when(step == last)
    def _():
        for copy in copies:
            copy.wait()
        result = dot(ctx_ref[...], ga_ref[...], TN)
        half, tall = per // 2, rows - per
        empty = jnp.zeros((tall - half, model), F32)
        box.wait(4, per, slots)
        for n in range(2 * slots):
            both = jnp.concatenate([result[n * half : (n + 1) * half], empty], axis=0)
            buffer[0, n * tall : (n + 1) * tall] = both.astype(BF16)
        box.send(4, [(n * tall, tall, n % 2, n, 0, per) for n in range(2 * slots)])
        box.wait(3, per, slots)
        box.wait(4, tall, 2 * slots)


def mid_weight_grad(place, nm, gpre, ctx, ga):
    tokens, model = nm.shape
    hidden = gpre.shape[1]
    assert hidden == 4 * model
    slots, per = PARTS // 2, 2 * model // PARTS
    shapes = [(slots, per + 32, model), (slots, per, model)]
    found = pl.pallas_call(
        mid_weight_grad_kernel,
        grid=(5,),
        in_specs=[
            SCALARS,
            whole(nm.shape),
            pl.BlockSpec((tokens, model), lambda i: (0, jnp.minimum(i, 3))),
            pl.BlockSpec(memory_space=pl.ANY),
            pl.BlockSpec(memory_space=pl.ANY),
        ],
        **hbm_outs_of(*shapes * 2),
        scratch_shapes=[
            pltpu.VMEM(ctx.shape, BF16),
            pltpu.VMEM(ga.shape, BF16),
            pltpu.VMEM((2, 32 * PARTS, model), BF16),
            pltpu.SemaphoreType.DMA((2,)),
            pltpu.SemaphoreType.DMA((2,)),
        ],
        compiler_params=params(),
        cost_estimate=cost(19),
        name="mid_weight_grad",
    )(place, nm, gpre, ctx, ga)
    return found[:2], found[2:]


def attend_weight_grad_kernel(place_ref, a_ref, b_ref, keep_ref, send_ref, *, heads):
    slots, rows, flat = keep_ref.shape
    part = flat // 3
    result = dot(a_ref[...], b_ref[0], TN).astype(BF16)
    for j in range(3):

        @pl.when(pl.program_id(0) == j)
        def _(j=j):
            put_parts(
                place_ref[0],
                (keep_ref, send_ref),
                [
                    (
                        d,
                        (slice(None), slice(j * part, (j + 1) * part)),
                        result[
                            d // heads * rows : (d // heads + 1) * rows,
                            d % heads * part : (d % heads + 1) * part,
                        ],
                    )
                    for d in range(2 * slots)
                ],
            )


def attend_weight_grad(place, nl, d_qkv, heads):
    tokens, model = nl.shape
    return pl.pallas_call(
        lambda *refs: attend_weight_grad_kernel(*refs, heads=heads),
        grid=(3,),
        in_specs=[SCALARS, whole(nl.shape), pl.BlockSpec((1, tokens, model), lambda j: (j, 0, 0))],
        **outs_of(*[(PARTS // 2, model * heads // PARTS, 3 * model // heads)] * 2),
        compiler_params=params(),
        cost_estimate=cost(13),
        name="attend_weight_grad",
    )(place, nl, d_qkv)


def input_grad_kernel(d_ref, x_ref, gm_ref, w_ref, vec_ref, mid_ref, out_ref, sum_ref, part_ref):
    model = x_ref.shape[1]

    @pl.when(pl.program_id(0) == 0)
    def _():
        sum_ref[:4, :] = jnp.zeros((4, model), F32)
        sum_ref[4:, :] = mid_ref[...]

    back = None
    for j in range(3):
        term = dot(d_ref[j], w_ref[:, j * model : (j + 1) * model], NT)
        back = term if back is None else back + term
    normed, factor = normalize(x_ref[...].astype(F32))
    sum_ref[0:1, :] += total(back * normed)
    sum_ref[1:2, :] += total(back)
    sum_ref[2:3, :] += total(d_ref[0].astype(F32))
    sum_ref[3:4, :] += total(d_ref[2].astype(F32))
    out_ref[...] = (gm_ref[...] + norm_back(back * vec_ref[0:1, :], normed, factor)).astype(BF16)

    @pl.when(pl.program_id(0) == pl.num_programs(0) - 1)
    def _():
        count = part_ref.shape[0]
        each = model // count
        part_ref[...] = jnp.zeros_like(part_ref)
        for n in range(count):
            part_ref[n, : sum_ref.shape[0], :each] = sum_ref[:, n * each : (n + 1) * each]


def input_grad(d_qkv, x, gm, w, vec, mid_sums, tile=512):
    tokens, model = x.shape
    row = pl.BlockSpec((tile, model), lambda i: (i, 0))
    return pl.pallas_call(
        input_grad_kernel,
        grid=(tokens // tile,),
        in_specs=[
            pl.BlockSpec((3, tile, model), lambda i: (0, i, 0)), row, row,
            whole(w.shape), whole(vec.shape), whole(mid_sums.shape),
        ],
        out_specs=[
            row,
            pl.BlockSpec(vec.shape, lambda i: (0, 0)),
            pl.BlockSpec((PARTS, 16, 128), lambda i: (0, 0, 0)),
        ],
        out_shape=[
            jax.ShapeDtypeStruct((tokens, model), BF16),
            jax.ShapeDtypeStruct(vec.shape, F32),
            jax.ShapeDtypeStruct((PARTS, 16, 128), F32),
        ],
        compiler_params=params(),
        cost_estimate=cost(16),
        name="input_grad",
    )(d_qkv, x, gm, w, vec, mid_sums)


def bit_groups(count):
    bits = count.bit_length() - 1
    assert count == 1 << bits
    return [(0, 1)] + [(low, min(2, bits - low)) for low in range(1, bits, 2)]


def slot_of(mask, groups):
    slot = 0
    for low, width in groups[1:]:
        slot = slot * (1 << width) + ((mask >> low) & ((1 << width) - 1))
    return slot


def mask_of(slot, groups):
    mask = 0
    for low, width in groups[:0:-1]:
        mask |= (slot & ((1 << width) - 1)) << low
        slot >>= width
    return mask


def swap(value, mask):
    count = lax.axis_size("batch") * lax.axis_size("head")
    return lax.ppermute(value, AXES, [(i, i ^ mask) for i in range(count)])


def spread(piece, group):
    low, width = group
    return [piece] + [swap(piece, step << low) for step in range(1, 1 << width)]


def join(parts):
    return jnp.concatenate(parts, axis=0)


def gather_far(piece, groups):
    piece = piece[None]
    for group in groups[:1:-1]:
        piece = join(spread(piece, group))
    return piece


def cross(pieces, group):
    count, rows = pieces.shape[0], pieces.shape[1] // 2
    low, high = 1 << group[0], 2 << group[0]
    first, second = pieces[:, :rows], pieces[:, rows:]
    received = swap(first, high), swap(second, low)
    first, second = join([first, received[0]]), join([second, received[1]])
    others = swap(first, low), swap(second, high)
    first = join([first[:count], others[0][:count], first[count:], others[0][count:]])
    return jnp.concatenate([first, join([second, others[1]])], axis=1)


def ordered(*values):
    return lax.optimization_barrier(values)


class Halves:
    def __init__(self, keep, send, groups):
        self.groups = groups
        self.bits = [2 << groups[1][0], 1 << groups[1][0]]
        self.terms = [[kept, swap(sent, 1)] for kept, sent in zip(keep, send)]
        self.count = keep[0].shape[0]

    def flat(self):
        return [t for terms in self.terms for t in terms]

    def set(self, flat):
        count = len(self.terms[0])
        self.terms = [list(flat[:count]), list(flat[count:])]

    def sends(self):
        self.count //= 2
        here = slice(self.count, 2 * self.count)
        return [added([t[here] for t in terms]).astype(BF16) for terms in self.terms]

    def receive(self, sends):
        received = [swap(send, bit) for send, bit in zip(sends, self.bits)]
        self.bits = self.bits[::-1]
        return received

    def add(self, received):
        self.terms = [terms + [one] for terms, one in zip(self.terms, received)]

    def at(self, slot):
        return jnp.concatenate([added([t[slot] for t in terms]) for terms in self.terms], axis=0)

    def last_sends(self):
        return [self.at(slot).astype(BF16) for slot in range(1, self.count)]

    def last_receive(self, sends):
        return [swap(send, (n + 1) << self.groups[2][0]) for n, send in enumerate(sends)]

    def finish(self, received):
        return added([self.at(0), *received])


class Whole:
    def __init__(self, keep, send, groups):
        self.groups = groups
        self.terms = [keep, swap(send, 1)]
        self.count = keep.shape[0]

    def sends(self):
        self.count //= 4
        return [
            added([t[n * self.count : (n + 1) * self.count] for t in self.terms]).astype(BF16)
            for n in range(1, 4)
        ]

    def receive(self, sends):
        return [swap(send, (n + 1) << self.groups[1][0]) for n, send in enumerate(sends)]

    def last_sends(self):
        return [added([t[n] for t in self.terms]).astype(BF16) for n in range(1, self.count)]

    def last_receive(self, sends):
        return [swap(send, (n + 1) << self.groups[2][0]) for n, send in enumerate(sends)]

    def finish(self, received):
        return added([added([t[0] for t in self.terms]), *received])


def added(terms):
    return sum(term.astype(F32) for term in terms)


def scatter(keep, send, groups):
    terms = [keep, swap(send, 1)]
    for low, width in groups[1:]:
        count = 1 << width
        terms = [t.reshape((count, -1) + t.shape[1:]) for t in terms]
        sends = [added([t[step] for t in terms]).astype(BF16) for step in range(1, count)]
        terms = [added([t[0] for t in terms])]
        terms += [swap(send, (n + 1) << low) for n, send in enumerate(sends)]
    return added(terms)[0]


def all_sum(value, groups):
    for low, width in groups:
        value = sum([swap(value, s << low) for s in range(1, 1 << width)], value)
    return value


def turned(mask, groups):
    low = groups[1][0]
    both = (mask >> low) & 3
    return mask ^ ((both ^ (both >> 1) ^ ((both & 1) << 1)) << low)


def slot_masks(groups, turn=False):
    masks = [mask_of(slot, groups) for slot in range(1 << sum(width for _, width in groups[1:]))]
    return [turned(mask, groups) for mask in masks] if turn else masks


def in_order(parts, masks, place):
    found = [mask for part in masks for mask in part]
    slots = [0] * len(found)
    for slot, mask in enumerate(found):
        slots[mask] = slot
    devices = jnp.arange(len(found), dtype=jnp.int32)
    return jnp.take(join(parts), jnp.asarray(slots, jnp.int32)[place ^ devices], axis=0)


def by_slot(parts, place, groups):
    masks = jnp.asarray(slot_masks(groups), jnp.int32)
    return [jnp.take(parts, place ^ (masks | bit), axis=0) for bit in range(2)]


def adapt_kernel(rows, copies, *refs):
    count = len(rows)
    inputs, outputs = refs[: 4 * count + 1], refs[4 * count + 1 :]
    sum_ref = outputs[3 * count]
    sum_ref[...] = inputs[-1][...]
    half = sum_ref.shape[0] // 2
    correct = 1.0 - BETA**STEP
    for number, row in enumerate(rows):
        grad_ref, first_ref, second_ref, weight_ref = inputs[4 * number : 4 * number + 4]
        moment_ref, square_ref, update_ref = outputs[3 * number : 3 * number + 3]
        planes = weight_ref.shape[0] if len(weight_ref.shape) == 3 else 1
        width = weight_ref.shape[-1]
        norms = []
        for n in range(planes):
            at = n if len(weight_ref.shape) == 3 else Ellipsis
            if len(grad_ref.shape) == 3:
                grad = jnp.sum(grad_ref[...], axis=0)[: weight_ref.shape[0], :width]
            else:
                grad = grad_ref[:, n * width : (n + 1) * width]
            moment = BETA * first_ref[at] + (1.0 - BETA) * grad
            square = BETA * second_ref[at] + (1.0 - BETA) * grad * grad
            weight = weight_ref[at]
            update = moment / correct / (jnp.sqrt(square / correct) + ADAM_EPS) + DECAY * weight
            moment_ref[at] = moment
            square_ref[at] = square
            update_ref[at] = update
            norms.append([jnp.sum(v * v, axis=1, keepdims=True) for v in (weight, update)])
        for n in range(2):
            norm = sum(both[n] for both in norms)
            if row < 4:
                norm = total(norm)
            place = n * half + row
            sum_ref[place : place + norm.shape[0], :] = jnp.broadcast_to(norm, (norm.shape[0], 128))
    if copies:
        outputs[-1][...] = jnp.broadcast_to(diagonal(sum_ref[...]), outputs[-1].shape)


def diagonal(values):
    row = lax.broadcasted_iota(jnp.int32, values.shape, 0)
    lane = lax.broadcasted_iota(jnp.int32, values.shape, 1)
    return total(jnp.where(row == lane, values, 0.0))


def adapt(states, rows, sums=None, copies=0):
    if sums is None:
        sums = jnp.zeros((32, 128), F32)
    operands = [array for state in states for array in state] + [sums]
    shapes = [state[3].shape for state in states for _ in range(3)] + [sums.shape]
    if copies:
        shapes.append((copies, 8, 128))
    found = pl.pallas_call(
        lambda *refs: adapt_kernel(rows, copies, *refs),
        grid=(1,),
        in_specs=[whole(a.shape) for a in operands],
        out_specs=[pl.BlockSpec(s, lambda *_, n=len(s): (0,) * n) for s in shapes],
        out_shape=[jax.ShapeDtypeStruct(s, F32) for s in shapes],
        compiler_params=params(),
        cost_estimate=cost(4),
        name="adapt",
    )(*operands)
    return [found[3 * n : 3 * n + 3] for n in range(len(states))], found[-1]


def master_kernel(sum_ref, *refs):
    *refs, trust_ref = refs
    count = len(refs) // 3
    width = trust_ref.shape[1]
    if len(sum_ref.shape) == 3:
        line = jnp.sum(sum_ref[...], axis=0)[:1]
    else:
        line = diagonal(sum_ref[...])
    norms = [jnp.sqrt(line[:, n * width : (n + 1) * width]) for n in range(2)]
    ratio = norms[0] / (norms[1] + ADAM_EPS)
    for n, value in enumerate([*norms, ratio]):
        trust_ref[n : n + 1, :] = jnp.log(value)
    for n in range(count):
        update_ref, weight_ref, out_ref = refs[n], refs[count + n], refs[2 * count + n]
        if n < 4:
            scale = RATE * ratio[:, n : n + 1]
        else:
            shape = (weight_ref.shape[0], width)
            row = lax.broadcasted_iota(jnp.int32, shape, 0)
            lane = lax.broadcasted_iota(jnp.int32, shape, 1)
            picked = jnp.where(lane == row + 4, jnp.broadcast_to(ratio, shape), 0.0)
            scale = RATE * jnp.sum(picked, axis=1, keepdims=True)
        for at in range(weight_ref.shape[0]) if len(weight_ref.shape) == 3 else [Ellipsis]:
            out_ref[at] = weight_ref[at] - scale * update_ref[at]


def master(sums, updates, weights, width):
    arrays = [sums, *updates, *weights]
    shapes = [a.shape for a in weights] + [(3, width)]
    return pl.pallas_call(
        master_kernel,
        grid=(1,),
        in_specs=[whole(a.shape) for a in arrays],
        out_specs=[pl.BlockSpec(s, lambda *_, n=len(s): (0,) * n) for s in shapes],
        out_shape=[jax.ShapeDtypeStruct(s, F32) for s in shapes],
        compiler_params=params(),
        cost_estimate=cost(3),
        name="master",
    )(*arrays)


def halves(parts, groups):
    return by_slot(parts, jnp.int32(0), groups)


def by_index(keep, send, groups, turn=False):
    masks = slot_masks(groups, turn)
    return in_order([keep, send], [masks, [mask | 1 for mask in masks]], jnp.int32(0))


def join_heads(pieces):
    nb, nh, rows, flat = pieces.shape
    wider = nb * nh // PARTS
    parts = pieces.reshape(nb // wider, wider, nh, rows, flat).transpose(0, 2, 1, 3, 4)
    return parts.reshape(PARTS, wider * rows, flat)


def join_parts(parts, nh):
    count = lax.axis_size("batch") * lax.axis_size("head")
    wider = count // PARTS
    _, rows, flat = parts.shape
    parts = parts.reshape(PARTS // nh, nh, wider, rows // wider, flat).transpose(0, 2, 1, 3, 4)
    return parts.reshape(count, rows // wider, flat)


def shards(
    block_input,
    cotangent,
    segment_lengths,
    thought_counts,
    packing_mask,
    attend_weight,
    output_weight,
    expand_weight,
    reduce_weight,
    vectors,
    first_attend,
    first_output,
    first_expand,
    first_reduce,
    first_vectors,
    second_attend,
    second_output,
    second_expand,
    second_reduce,
    second_vectors,
):
    nb, nh = lax.axis_size("batch"), lax.axis_size("head")
    count = nb * nh
    groups, kernel_groups = bit_groups(count), bit_groups(PARTS)
    same = count == PARTS
    place = (lax.axis_index("batch") * nh + lax.axis_index("head")).astype(jnp.int32)
    core = place % 2
    kernel_place = (place if same else jnp.zeros_like(place)).reshape(1)
    rows, length, model = block_input.shape
    tokens = rows * length
    hidden = expand_weight.shape[1]
    own_in, _, own_out = attend_weight.shape
    own = output_weight.shape[0]
    own_red = reduce_weight.shape[0]
    cols = vectors.shape[1]
    wide = hidden // model
    flat = 3 * own_out

    extra = jnp.pad(vectors.astype(BF16).T, ((0, -cols % 16), (0, flat - own)))
    piece = jnp.concatenate([attend_weight.astype(BF16).reshape(own_in, flat), extra], axis=0)
    attend_far = gather_far(piece, groups)

    blocks = expand_weight.astype(BF16).reshape(own, 2, wide // 2, model).transpose(1, 2, 0, 3)
    beside = swap(jnp.where(core == 0, blocks[1], blocks[0]), 1)
    mine = jnp.where(core == 0, blocks[0], blocks[1])
    piece = [
        jnp.concatenate(
            [jnp.where(core == 0, mine, beside), jnp.where(core == 0, beside, mine)], axis=1
        ).reshape(2 * own * (wide // 2), model),
        reduce_weight.astype(BF16),
        output_weight.astype(BF16),
    ]
    pad = -(own_red + own) % 16
    piece = jnp.concatenate(piece + [jnp.zeros((pad, model), BF16)], axis=0)
    late_all = lax.all_gather(piece, AXES, axis=0, tiled=False)
    attend_own = cross(attend_far, groups[1])
    attend_other = swap(attend_own, 1)
    if not same:
        masks = slot_masks(groups)
        attend = in_order([attend_own, attend_other], [masks, [m | 1 for m in masks]], place)
        vec = attend[:, own_in:, :own].transpose(1, 0, 2).reshape(-1, PARTS, model // PARTS)
        vec = jnp.pad(vec.transpose(1, 0, 2), ((0, 0), (0, 0), (0, flat - model // PARTS)))
        attend = join_heads(attend[:, :own_in].reshape(nb, nh, own_in, flat))
        attend_own, attend_other = halves(
            jnp.concatenate([attend, vec], axis=1), kernel_groups
        )

    own_lengths = lax.dynamic_slice_in_dim(
        segment_lengths, lax.axis_index("head") * rows, rows, 0
    )
    own_counts = lax.dynamic_slice_in_dim(thought_counts, lax.axis_index("head") * rows, rows, 0)
    start_of, weight_rows = row_facts(own_lengths, own_counts, packing_mask, length)
    start_of = start_of.reshape(rows, 1, length)
    weight_rows = weight_rows.reshape(tokens, 1)

    x = block_input.reshape(tokens, model)
    cot = cotangent.reshape(tokens, model)
    normed_low, qkv, attend_low, vec = project(
        kernel_place, x, attend_own, attend_other, nh, cols
    )
    context, probs = attend_forward(start_of, qkv, length)
    if not same:
        late = late_all
        both, per = 2 * own, 2 * model // PARTS
        expand_low = (
            late[:, : both * wide // 2]
            .reshape(count // 2, 2, wide // 2, both, model)
            .transpose(1, 2, 0, 3, 4)
            .reshape(2, wide // 2, PARTS // 2, per, model)
            .transpose(2, 0, 1, 3, 4)
            .reshape(PARTS, per * (wide // 2), model)
        )
        low = both * wide // 2
        rest = [
            expand_low,
            late[:, low : low + own_red].reshape(PARTS, hidden // PARTS, model),
            late[:, low + own_red : low + own_red + own].reshape(PARTS, per // 2, model),
            jnp.zeros((PARTS, 8, model), BF16),
        ]
        late_all = jnp.concatenate(rest, axis=1)
    late = (late_all,)
    hidden_states, middle, middle_low, activated, slope, branch = mlp_forward(
        late, context, x, cot, weight_rows, vec, hidden
    )

    def for_devices(keep, send, split):
        parts = [by_index(*both, kernel_groups, n == 1) for n, both in enumerate(zip(keep, send))]
        return by_slot(split(jnp.concatenate(parts, axis=1)), place, groups)

    def split_mid(parts):
        per = 2 * model // PARTS
        expand = (
            jnp.stack([parts[:, :per], parts[:, per + 32 :]], axis=1)
            .reshape(PARTS // 2, 2, 2, per, model)
            .transpose(1, 2, 0, 3, 4)
            .reshape(2, 2, count // 2, 2 * own, model)
            .transpose(2, 0, 1, 3, 4)
            .reshape(count, 4 * own, model)
        )
        output = parts[:, per : per + per // 2].reshape(count, own, model)
        return jnp.concatenate([expand, output], axis=1)

    red_keep, red_send = reduce_weight_grad(kernel_place, activated, branch)
    if same:
        cot, *red_send = ordered(cot, *red_send)
        red = Halves(red_keep, red_send, groups)
    grad_pre, grad_middle, grad_attn, grad_context, mid_sums = mlp_backward(
        late, cot, weight_rows, middle, slope, vec
    )
    if same:
        grad_pre, *terms = ordered(grad_pre, *red.flat())
        red.set(terms)
        grad_pre, *sends = ordered(grad_pre, *red.sends())
        red_received = red.receive(sends)

    mid_keep, mid_send = mid_weight_grad(
        kernel_place, middle_low, grad_pre, context, grad_attn
    )
    if same:
        grad_context, *terms = ordered(grad_context, *mid_send, *red_received)
        mid = Halves(mid_keep, terms[:2], groups)
        red.add(terms[2:])
        grad_context, *sends = ordered(grad_context, *red.sends())
        red_received = red.receive(sends)

    pairs = model // (2 * HEAD_DIM)
    operands = (qkv, context, grad_context, probs, length)
    d_qkv = attend_backward(*operands, 0, 2 * pairs // 3)
    if same:
        d_qkv, *terms = ordered(d_qkv, *mid.flat(), *red_received)
        mid.set(terms[:4])
        red.add(terms[4:])
        d_qkv, *sends = ordered(d_qkv, *mid.sends(), *red.last_sends())
        mid_received = mid.receive(sends[:2])
        red_received = red.last_receive(sends[2:])
    d_qkv = attend_backward(*operands, 2 * pairs // 3, rows * pairs, d_qkv)
    if same:
        d_qkv, *terms = ordered(d_qkv, *mid_received, *red_received)
        mid.add(terms[:2])
        red_received = terms[2:]
        d_qkv, *sends = ordered(d_qkv, *mid.sends())
        mid_received = mid.receive(sends)
    att_keep, att_send = attend_weight_grad(kernel_place, normed_low, d_qkv, nh)
    if same:
        att_send, *mid_received = ordered(att_send, *mid_received)
        att = Whole(att_keep, att_send, groups)
        mid.add(mid_received)
        d_qkv, *terms = ordered(d_qkv, *mid.last_sends(), *att.terms)
        att.terms = terms[-2:]
        mid_nearest, *mid_sends = terms[:-2]
        mid_received = [
            swap(send, (n + 2) << groups[2][0]) for n, send in enumerate(mid_sends)
        ]
        d_qkv, *sends = ordered(d_qkv, *att.sends())
        att_received = att.receive(sends)
    grad_input, sums, sum_parts = input_grad(d_qkv, x, grad_middle, attend_low, vec, mid_sums)
    if same:
        sum_parts, mid_nearest, *terms = ordered(
            sum_parts, mid_nearest, *att_received, *mid_received, *red_received
        )
        att.terms = att.terms + terms[:3]
        att_received = att.last_receive(att.last_sends())
        mid_received = terms[3:5] + [swap(mid_nearest, 1 << groups[2][0])]
        red_grad, found = red.finish(terms[5:]), mid.finish(mid_received)
        per = 2 * own
        mid = jnp.concatenate(
            [found[:per], found[per + 32 :], found[per : per + own]], axis=0
        )
    else:
        red_parts = for_devices(
            red_keep, red_send, lambda parts: parts.reshape(count, own_red, model)
        )
        mid_parts = for_devices(mid_keep, mid_send, split_mid)
        att_parts = for_devices(
            [att_keep], [att_send], lambda parts: join_parts(parts, nh).reshape(count, own_in, flat)
        )
        red_grad, mid = scatter(*red_parts, groups), scatter(*mid_parts, groups)
        att_grad = scatter(*att_parts, groups)
    out_grad = mid[4 * own : 5 * own]
    exp_both = mid[: 4 * own].reshape(2, 2, own, model)
    kept = jnp.where(core == 0, exp_both[:, 0], exp_both[:, 1])
    beside = swap(jnp.where(core == 0, exp_both[:, 1], exp_both[:, 0]), 1)
    exp_grad = jnp.stack(
        [jnp.where(core == 0, kept, beside), jnp.where(core == 0, beside, kept)]
    ).reshape(wide, own, model)
    exp_grad = exp_grad.transpose(1, 0, 2).reshape(own, hidden)


    if same:
        vector_grad = lax.all_to_all(sum_parts, AXES, 0, 0, tiled=True)
    else:
        vector_grad = lax.dynamic_slice_in_dim(all_sum(sums, groups), place * own, own, 1)
    late_weights = (output_weight, expand_weight, reduce_weight)
    late_states = [
        (grad, first, second, weight)
        for grad, first, second, weight in zip(
            (out_grad, exp_grad, red_grad),
            (first_output, first_expand, first_reduce),
            (second_output, second_expand, second_reduce),
            late_weights,
        )
    ]
    late_found, late_sums = adapt(late_states, [1, 2, 3])
    if same:
        late_sums, *att_received = ordered(late_sums, *att_received)
        att_grad = att.finish(att_received)

    def planes(state):
        return state.transpose(1, 0, 2)

    found, sums = adapt(
        [
            (att_grad, planes(first_attend), planes(second_attend), planes(attend_weight)),
            (vector_grad, first_vectors.T, second_vectors.T, vectors.T),
        ],
        [0, 4],
        late_sums,
        count if same else 0,
    )
    sums = lax.all_to_all(sums, AXES, 0, 0, tiled=True) if same else all_sum(sums, groups)
    adapted = [list(found[0]), *late_found, [a.T for a in found[1]]]
    *masters, trust_norms = master(
        sums,
        [found[0][2], *[a[2] for a in late_found], found[1][2]],
        [planes(attend_weight), *late_weights, vectors.T],
        4 + cols,
    )
    masters[4] = masters[4].T
    adapted[0] = [planes(a) for a in adapted[0]]
    masters[0] = planes(masters[0])
    return (
        hidden_states.reshape(rows, length, model),
        grad_input.reshape(rows, length, model),
        *[a[0] for a in adapted],
        *[a[1] for a in adapted],
        *masters,
        trust_norms,
    )


def solution(mesh):
    rows = P(AXES, None, None)
    state = [P("batch", None, "head")] + [P(AXES, None)] * 4
    return jax.shard_map(
        shards,
        mesh=mesh,
        in_specs=(rows, rows, P("batch", None), P("batch", None), P(AXES, None), *state * 3),
        out_specs=(rows, rows, *state * 3, P()),
        check_vma=False,
    )
```
